32 devices in a mesh: seq: 16 (over z, x, core), head: 2 (over y).
Axes of the slice: x: 2, y: 2, z: 4, core: 2. Of those that a mesh axis runs over, the one named last changes fastest.
Arguments:
- tokens: bfloat16 [4096, 768], P(('seq', 'head')), may hold values from -6 to 6
- cotangent: bfloat16 [4096, 768], P(('seq', 'head')), may hold values from -6 to 6
- w_query: bfloat16 [768, 768], P(('seq', 'head')), may hold values from -0.21875 to 0.21875
- w_key: bfloat16 [768, 768], P(('seq', 'head')), may hold values from -0.21875 to 0.21875
- w_value: bfloat16 [768, 768], P(('seq', 'head')), may hold values from -0.21875 to 0.21875
- w_output: bfloat16 [768, 768], P(('seq', 'head')), may hold values from -1.75 to 1.75
- w_inner: bfloat16 [768, 3072], P(('seq', 'head')), may hold values from -0.21875 to 0.21875
- w_outer: bfloat16 [3072, 768], P(('seq', 'head')), may hold values from -0.109375 to 0.109375
- gain_first: float32 [768], replicated, may hold values from 0.1 to 1.9
- shift_first: float32 [768], replicated, may hold values from -1.5 to 1.5
- gain_second: float32 [768], replicated, may hold values from 0.1 to 1.9
- shift_second: float32 [768], replicated, may hold values from -1.5 to 1.5
- attn_down: bfloat16 [8, 4, 16, 768], replicated, may hold values from -0.21875 to 0.21875
- attn_up: bfloat16 [8, 4, 16, 768], replicated, may hold values from -1 to 1
- inner_down: bfloat16 [8, 16, 768], replicated, may hold values from -0.21875 to 0.21875
- inner_up: bfloat16 [8, 16, 3072], replicated, may hold values from -1 to 1
- outer_down: bfloat16 [8, 16, 3072], replicated, may hold values from -0.109375 to 0.109375
- outer_up: bfloat16 [8, 16, 768], replicated, may hold values from -1 to 1
- lengths: int32 [1], replicated, may hold values from 1024 to 4096, as said below
- rand_blocks: int32 [64, 3], P('seq'), may hold values from 2 to 63, as said below
- adapter_pick: int32 [1], replicated, may hold values from 0 to 7
Outputs:
- output: bfloat16 [4096, 768], P(('seq', 'head'))
- grad_tokens: float32 [4096, 768], P(('seq', 'head'))
- grad_attn_down: float32 [8, 4, 16, 768], replicated
- grad_attn_up: float32 [8, 4, 16, 768], replicated
- grad_inner_down: float32 [8, 16, 768], replicated
- grad_inner_up: float32 [8, 16, 3072], replicated
- grad_outer_down: float32 [8, 16, 3072], replicated
- grad_outer_up: float32 [8, 16, 768], replicated
The draws below stay inside these ranges and needn't reach their ends.
Inputs may be any that keep to these rules, and one draw needn't show every extreme that they name: `lengths`: one sequence, drawn from the seed, has at least 3968 used slots. `rand_blocks`: row b names three different blocks of its own sequence, none of them 0, 1, b - 1, b or b + 1.
All inputs are finite; a program needn't handle non-finite values.
Results may differ from the reference program's by a relative error of at most 0.018.
The reference program's roundings to bfloat16 on the way count: a program that leaves them out, or rounds other values in their place, can miss the bound.
Values may be sent and summed in bfloat16 or wider, within the bound.
No kernel may reach another device: no remote copies, remote signals or barrier semaphores. Data moves between devices by JAX's collectives and lax.ppermute only.
A program may use at most 640 MiB of HBM per device.

```python
import jax
import jax.numpy as jnp
from jax import lax

D = 768
HEADS = 12
HDIM = 64
FF = 3072
BLOCK = 64
RANDOM = 3
RANK = 16
ADAPTERS = 8
ROWS_SEQ = 256
LENGTH = 4096
SEQS = 1
TOKENS = 4096


def draw_lengths(key, part):
    key = jax.random.fold_in(key, 11)
    seq_total = TOKENS // LENGTH
    first_key, second_key, third_key = jax.random.split(key, 3)
    ragged = jax.random.randint(first_key, (seq_total,), LENGTH // 4, LENGTH + 1)
    longest = jax.random.randint(second_key, (), LENGTH - ROWS_SEQ // 2, LENGTH + 1)
    chosen = jax.random.randint(third_key, (), 0, seq_total)
    return jnp.where(jnp.arange(seq_total) == chosen, longest, ragged).astype(jnp.int32)


def draw_rand_blocks(key, part):
    key = jax.random.fold_in(key, 7)
    total_blocks = TOKENS // BLOCK
    seq_blocks = LENGTH // BLOCK
    inseq = jnp.arange(total_blocks, dtype=jnp.int32) % seq_blocks
    candidates = seq_blocks - 5
    half_span = (candidates - 1) // 2
    first_key, second_key, third_key = jax.random.split(key, 3)
    anchor = jax.random.randint(first_key, (total_blocks,), 0, candidates)
    second_pick = (anchor + 1 + jax.random.randint(second_key, (total_blocks,), 0, half_span)) % candidates
    third_pick = (anchor + 1 + half_span + jax.random.randint(third_key, (total_blocks,), 0, half_span)) % candidates
    picks = jnp.stack([anchor, second_pick, third_pick], axis=1)
    return jnp.where(picks + 2 < inseq[:, None] - 1, picks + 2, picks + 5).astype(jnp.int32)


def levels(rng, dims, shards, least, largest):
    loudness = 1.0
    for axis_at, parts in shards:
        heights = jax.random.uniform(jax.random.fold_in(jax.random.fold_in(rng, 6), axis_at), (parts,), jnp.float32, least / len(shards), largest / len(shards))
        loudness = loudness * jnp.repeat(jnp.exp(heights), dims[axis_at] // parts).reshape((-1,) + (1,) * (len(dims) - 1 - axis_at))
    return loudness


def noise(stream_key, extent, width, limit, cuts=(), kind=jnp.bfloat16):
    drawn = jax.random.normal(stream_key, extent, jnp.float32) * width
    if len(cuts) > 0:
        drawn = levels(stream_key, extent, cuts, -0.22, 0.18) * drawn
    return jnp.clip(drawn, min=-limit, max=limit).astype(kind)


def setup_inputs(seed: int = 0) -> dict:
    arg_keys = jax.random.split(jax.random.key(seed), 22)
    tokens = noise(arg_keys[0], (TOKENS, D), 1.0, 6.0, ((0, 32),))
    cotangent = noise(arg_keys[1], (TOKENS, D), 1.0, 6.0, ((0, 32),))
    w_query = noise(arg_keys[2], (D, D), D ** -0.5, 0.21875, ((0, 32),))
    w_key = noise(arg_keys[3], (D, D), D ** -0.5, 0.21875, ((0, 32),))
    w_value = noise(arg_keys[4], (D, D), D ** -0.5, 0.21875, ((0, 32),))
    w_output = noise(arg_keys[5], (D, D), (D // 64) ** -0.5, 1.75, ((0, 32),))
    w_inner = noise(arg_keys[6], (D, FF), D ** -0.5, 0.21875, ((0, 32),))
    w_outer = noise(arg_keys[7], (FF, D), FF ** -0.5, 0.109375, ((0, 32),))
    gain_first = jnp.clip(1.0 + 0.18 * jax.random.normal(arg_keys[8], (D,), jnp.float32), 0.1, 1.9)
    shift_first = noise(arg_keys[9], (D,), 0.3, 1.5, (), jnp.float32)
    gain_second = jnp.clip(1.0 + 0.18 * jax.random.normal(arg_keys[10], (D,), jnp.float32), 0.1, 1.9)
    shift_second = noise(arg_keys[11], (D,), 0.3, 1.5, (), jnp.float32)
    attn_down = noise(arg_keys[12], (ADAPTERS, 4, RANK, D), D ** -0.5, 0.21875)
    attn_up = noise(arg_keys[13], (ADAPTERS, 4, RANK, D), (2 * RANK) ** -0.5, 1.0)
    inner_down = noise(arg_keys[14], (ADAPTERS, RANK, D), D ** -0.5, 0.21875)
    inner_up = noise(arg_keys[15], (ADAPTERS, RANK, FF), (2 * RANK) ** -0.5, 1.0)
    outer_down = noise(arg_keys[16], (ADAPTERS, RANK, FF), FF ** -0.5, 0.109375)
    outer_up = noise(arg_keys[17], (ADAPTERS, RANK, D), (2 * RANK) ** -0.5, 1.0)
    lengths = draw_lengths(jax.random.fold_in(arg_keys[21], 71), 0)
    rand_blocks = draw_rand_blocks(jax.random.fold_in(arg_keys[21], 71), 0)
    adapter_pick = jax.random.randint(arg_keys[20], (SEQS,), 0, ADAPTERS).astype(jnp.int32)
    return {"tokens": tokens, "cotangent": cotangent, "w_query": w_query, "w_key": w_key, "w_value": w_value, "w_output": w_output, "w_inner": w_inner, "w_outer": w_outer, "gain_first": gain_first, "shift_first": shift_first, "gain_second": gain_second, "shift_second": shift_second, "attn_down": attn_down, "attn_up": attn_up, "inner_down": inner_down, "inner_up": inner_up, "outer_down": outer_down, "outer_up": outer_up, "lengths": lengths, "rand_blocks": rand_blocks, "adapter_pick": adapter_pick}


floor_score = -1e+30
highest = lax.Precision.HIGHEST
norm_eps = 1e-12

@jax.custom_vjp
def low(v):
    return lax.optimization_barrier(v.astype(jnp.bfloat16)).astype(jnp.float32)

@jax.custom_vjp
def low_back(v):
    return v

def low_keep(v):
    return (low(v), None)

def low_pass(kept, grad):
    return (grad,)

def back_keep(v):
    return (v, None)

def back_low(kept, grad):
    return (low(grad),)
low.defvjp(low_keep, low_pass)
low_back.defvjp(back_keep, back_low)

def normalize(hidden, gain_vec, shift_vec):
    center = hidden - lax.optimization_barrier(jnp.mean(hidden, axis=-1, keepdims=True))
    spread = lax.optimization_barrier(jnp.mean(center * center, axis=-1, keepdims=True))
    return center * lax.rsqrt(spread + norm_eps) * gain_vec + shift_vec

def project(inputs, weight, down_map, up_map):
    reduced = low_back(low(jnp.dot(inputs, down_map.T, precision=highest)))
    return jnp.dot(inputs, weight, precision=highest) + jnp.dot(reduced, up_map, precision=highest)

def soft_rows(scores, allowed):
    masked = jnp.where(allowed, scores, floor_score)
    row_top = lax.optimization_barrier(jnp.max(masked, axis=-1, keepdims=True))
    exponent = jnp.where(allowed, jnp.exp(masked - row_top), 0.0)
    return exponent / lax.optimization_barrier(jnp.sum(exponent, axis=-1, keepdims=True))

def attend(queries, key_rows, value_rows, rand_index, length):
    seq_len = queries.shape[0]
    block_total = seq_len // BLOCK
    query_blocks = queries.reshape(block_total, BLOCK, HEADS, HDIM)
    key_blocks = key_rows.reshape(block_total, BLOCK, HEADS, HDIM)
    value_blocks = value_rows.reshape(block_total, BLOCK, HEADS, HDIM)
    block_ids = jnp.arange(block_total, dtype=jnp.int32)[:, None]
    chosen = jnp.concatenate([block_ids, block_ids - 1, block_ids + 1, jnp.zeros_like(block_ids), jnp.ones_like(block_ids), rand_index.astype(jnp.int32)], axis=1)
    sliding = jnp.arange(8, dtype=jnp.int32) < 3
    usable = (chosen >= 2) & (chosen < block_total) | jnp.logical_not(sliding)[None]
    key_valid = usable[:, :, None] & (chosen[:, :, None] * BLOCK + jnp.arange(BLOCK, dtype=jnp.int32)[None, None] < length)
    safe_ids = jnp.clip(chosen, 0, block_total - 1)

    def group_attend(group_index):
        first_row = group_index * 8
        group_ids = lax.dynamic_slice_in_dim(safe_ids, first_row, 8, 0)
        group_valid = lax.dynamic_slice_in_dim(key_valid, first_row, 8, 0).reshape(8, 1, 1, 8 * BLOCK)
        group_queries = lax.dynamic_slice_in_dim(query_blocks, first_row, 8, 0)
        key_sets = key_blocks[group_ids].reshape(8, 8 * BLOCK, HEADS, HDIM)
        value_sets = value_blocks[group_ids].reshape(8, 8 * BLOCK, HEADS, HDIM)
        scores = low_back(jnp.einsum('nqhd,nkhd->nhqk', group_queries, key_sets, precision=highest) * 0.125)
        soft_probs = soft_rows(scores, group_valid)
        return jnp.einsum('nhqk,nkhd->nqhd', low(soft_probs), value_sets, precision=highest)
    grouped = lax.map(jax.checkpoint(group_attend), jnp.arange(block_total // 8, dtype=jnp.int32))
    context = grouped.reshape(seq_len, HEADS, HDIM)
    lead_queries = queries[:2 * BLOCK].reshape(2 * BLOCK, HEADS, HDIM)
    lead_scores = low_back(jnp.einsum('qhd,khd->hqk', lead_queries, key_rows.reshape(seq_len, HEADS, HDIM), precision=highest) * 0.125)
    lead_probs = soft_rows(lead_scores, (jnp.arange(seq_len, dtype=jnp.int32) < length)[None, None])
    lead_context = jnp.einsum('hqk,khd->qhd', low(lead_probs), value_rows.reshape(seq_len, HEADS, HDIM), precision=highest)
    return jnp.concatenate([lead_context, context[2 * BLOCK:]], axis=0).reshape(seq_len, HEADS * HDIM)

def layer_forward(tokens, adapters, weights, rand_index, length, chosen_adapter):
    w_query, w_key, w_value, w_output, w_inner, w_outer, gain_first, shift_first, gain_second, shift_second = weights
    attn_down, attn_up, inner_down, inner_up, outer_down, outer_up = adapters
    down_sel = attn_down[chosen_adapter]
    up_sel = attn_up[chosen_adapter]
    queries = low_back(low(project(tokens, w_query, down_sel[0], up_sel[0])))
    key_rows = low_back(low(project(tokens, w_key, down_sel[1], up_sel[1])))
    value_rows = low_back(low(project(tokens, w_value, down_sel[2], up_sel[2])))
    context = low_back(low(attend(queries, key_rows, value_rows, rand_index, length)))
    attended = low_back(project(context, w_output, down_sel[3], up_sel[3]))
    first_norm = normalize(tokens + attended, gain_first, shift_first)
    inner_pre = low_back(project(low(first_norm), w_inner, inner_down[chosen_adapter], inner_up[chosen_adapter]))
    activated = low(jax.nn.gelu(inner_pre, approximate=False))
    outer_out = low_back(project(activated, w_outer, outer_down[chosen_adapter], outer_up[chosen_adapter]))
    valid = (jnp.arange(tokens.shape[0], dtype=jnp.int32) < length).astype(tokens.dtype)[:, None]
    return normalize(first_norm + outer_out, gain_second, shift_second) * valid

def reference(tokens, cotangent, w_query, w_key, w_value, w_output, w_inner, w_outer, gain_first, shift_first, gain_second, shift_second, attn_down, attn_up, inner_down, inner_up, outer_down, outer_up, lengths, rand_blocks, adapter_pick):
    weights = tuple((item.astype(jnp.float32) for item in (w_query, w_key, w_value, w_output, w_inner, w_outer, gain_first, shift_first, gain_second, shift_second)))
    adapters = tuple((item.astype(jnp.float32) for item in (attn_down, attn_up, inner_down, inner_up, outer_down, outer_up)))
    seq_total = lengths.shape[0]
    seq_len = tokens.shape[0] // seq_total
    inputs = tokens.astype(jnp.float32).reshape(seq_total, seq_len, D)
    cotangents = cotangent.astype(jnp.float32).reshape(seq_total, seq_len, D)
    randoms = rand_blocks.reshape(seq_total, seq_len // BLOCK, RANDOM)

    def per_sequence(totals, sequence_items):
        seq_tokens, seq_cot, seq_rand, seq_length, seq_adapter = sequence_items

        def forward(values, params):
            return layer_forward(values, params, weights, seq_rand, seq_length, seq_adapter)
        result, pullback = jax.vjp(forward, seq_tokens, adapters)
        grad_inputs, grad_params = pullback(seq_cot)
        return (tuple((total_one + grad_one for total_one, grad_one in zip(totals, grad_params))), (result, grad_inputs))
    zero_grads = tuple((jnp.zeros_like(item) for item in adapters))
    totals, (results, input_grads) = lax.scan(per_sequence, zero_grads, (inputs, cotangents, randoms, lengths, adapter_pick))
    return (results.reshape(-1, D).astype(jnp.bfloat16), input_grads.reshape(-1, D), totals[0], totals[1], totals[2], totals[3], totals[4], totals[5])
```

```python
import functools

import jax
import jax.numpy as jnp
from jax import lax
from jax.experimental import pallas as pl
from jax.experimental.pallas import tpu as pltpu
from jax.sharding import PartitionSpec as P

D = 768
HEADS = 12
HDIM = 64
BLOCK = 64
ADAPTERS = 8
RANK = 16
FF = 3072

PEERS = (0, 1, 4, 5)
GROUP_HEADS = HEADS // 4
SHARE = GROUP_HEADS * HDIM
WIDE = 256
LSE_LANE = SHARE
DEL_LANE = SHARE + 9
MASK_LANE = SHARE + 18
FLOOR = -1e30
STACK = GROUP_HEADS * BLOCK
AXES = ("seq", "head")
norm_eps = 1e-12
f32 = jnp.float32
bf16 = jnp.bfloat16
VMEM_LIMIT = 60 * 1024 * 1024


def dense_mul(left_op, right_op):
    return jnp.dot(left_op, right_op, preferred_element_type=f32)


def dense_right_t(left_op, right_op):
    return lax.dot_general(left_op, right_op, (((1,), (1,)), ((), ())), preferred_element_type=f32)


def dense_left_t(left_op, right_op):
    return lax.dot_general(left_op, right_op, (((0,), (0,)), ((), ())), preferred_element_type=f32)


def normalize(hidden, gain_vec, shift_vec):
    center = hidden - jnp.mean(hidden, axis=-1, keepdims=True)
    spread = jnp.mean(center * center, axis=-1, keepdims=True)
    return center * lax.rsqrt(spread + norm_eps) * gain_vec + shift_vec


def exact_gelu(hidden):
    return jax.nn.gelu(hidden, approximate=False)


def adapted(inputs, weight, down_map, up_map):
    reduced = dense_right_t(inputs, down_map).astype(bf16)
    return (dense_mul(inputs, weight) + dense_mul(reduced, up_map), reduced)


def adapted_back(inputs, reduced, grad_out, weight, down_map, up_map):
    grad_up = dense_left_t(reduced, grad_out)
    grad_reduced = dense_right_t(grad_out, up_map).astype(bf16)
    grad_down = dense_left_t(grad_reduced, inputs)
    grad_in = dense_right_t(grad_out, weight) + dense_mul(grad_reduced, down_map)
    return (grad_in, grad_down, grad_up)


def lanes(rows):
    return lax.broadcasted_iota(jnp.int32, (rows, WIDE), 1)


def head_lanes(lane, head):
    return (lane >= HDIM * head) & (lane < HDIM * (head + 1))


def part_lanes(lane, first, head):
    return (lane >= first + 3 * head) & (lane < first + 3 * head + 3)


def project_kernel(meta_ref, tok_ref, w_ref, u_ref, q_ref, k_ref, v_ref):
    rows = tok_ref.shape[0]
    raw = dense_mul(tok_ref[...], w_ref[...])
    lane = lanes(rows)
    data = lane < SHARE

    def part(j):
        piece = raw[:, WIDE * j : WIDE * (j + 1)]
        return (piece + dense_mul(piece[:, WIDE // 2 :].astype(bf16), u_ref[j])).astype(bf16).astype(f32)

    position = pl.program_id(0) * rows + lax.broadcasted_iota(jnp.int32, (rows, WIDE), 0)
    mask = jnp.where(position < meta_ref[1], 0.0, FLOOR)
    q_ref[...] = jnp.where(data, part(0) * 0.125, jnp.where(lane == MASK_LANE, 1.0, 0.0)).astype(bf16)
    k_ref[...] = jnp.where(
        data, part(1), jnp.where(lane < DEL_LANE, 1.0, jnp.where(lane == MASK_LANE, mask, 0.0))
    ).astype(bf16)
    v_ref[...] = jnp.where(data, part(2), jnp.where((lane >= DEL_LANE) & (lane < MASK_LANE), 1.0, 0.0)).astype(bf16)


def block_rows(ref, block, count=1):
    return ref[pl.ds(pl.multiple_of(block * BLOCK, BLOCK), count * BLOCK), :]


def merge_heads(stacked):
    lane = lanes(BLOCK)
    total = jnp.zeros((BLOCK, WIDE), f32)
    for head in range(GROUP_HEADS):
        total = jnp.where(head_lanes(lane, head), stacked[BLOCK * head : BLOCK * (head + 1)], total)
    return total


def key_set(ref, rand_ref, block, block_total, fill):
    own = block_rows(ref, block)
    left = block_rows(ref, jnp.maximum(block - 1, 0))
    right = block_rows(ref, jnp.minimum(block + 1, block_total - 1))
    if fill:
        blank = jnp.where(lanes(BLOCK) == MASK_LANE, FLOOR, 0.0).astype(bf16)
        left = jnp.where(block - 1 >= 2, left, blank)
        right = jnp.where(block + 1 < block_total, right, blank)
    rand = [block_rows(ref, rand_ref[block * 3 + r]) for r in range(3)]
    return jnp.concatenate([own, left, right, block_rows(ref, 0, 2)] + rand, axis=0)


def own_block(place, t):
    return 2 * (place ^ PEERS[t // 2]) + t % 2


def forward_kernel(meta_ref, rand_ref, q_ref, k_ref, v_ref, ctx_ref, aux_ref, s_ref):
    place = meta_ref[0]
    total_rows = q_ref.shape[0]
    block_total = total_rows // BLOCK
    chunk = 8 * BLOCK
    chunks = total_rows // chunk

    def queries(block):
        rows = block_rows(q_ref, block)
        lane = lanes(BLOCK)
        blank = jnp.zeros_like(rows)
        return jnp.concatenate(
            [
                jnp.where(head_lanes(lane, head) | (lane == MASK_LANE), rows, blank)
                for head in range(GROUP_HEADS)
            ],
            axis=0,
        )

    def finish(t, low, exact, top, total):
        lane = lanes(BLOCK)
        rows = pl.ds(t * BLOCK, BLOCK)
        ctx_ref[rows, :] = merge_heads(low).astype(bf16)
        aux = merge_heads(exact)
        lse = top + jnp.log(total)
        for head in range(GROUP_HEADS):
            aux = jnp.where(lane == LSE_LANE + head, lse[BLOCK * head : BLOCK * (head + 1)], aux)
        aux_ref[rows, :] = aux

    for t in range(8):
        block = own_block(place, t)

        @pl.when(block >= 2)
        def _(t=t, block=block):
            scores = dense_right_t(queries(block), key_set(k_ref, rand_ref, block, block_total, True))
            top = jnp.max(scores, axis=1, keepdims=True)
            weights = jnp.exp(scores - top)
            total = jnp.sum(weights, axis=1, keepdims=True)
            probs = weights / total
            low = probs.astype(bf16)
            rest = (probs - low.astype(f32)).astype(bf16)
            values = key_set(v_ref, rand_ref, block, block_total, False)
            context = dense_mul(low, values)
            finish(t, context, context + dense_mul(rest, values), top, total)

        if t < 2 or (t // 2) in (1, 2, 3):

            @pl.when(block < 2)
            def _(t=t, block=block):
                stack = queries(block)

                def score(c, top):
                    part = dense_right_t(stack, block_rows(k_ref, c * 8, 8))
                    s_ref[c] = part
                    return jnp.maximum(top, jnp.max(part, axis=1, keepdims=True))

                top = lax.fori_loop(0, chunks, score, jnp.full((STACK, 1), FLOOR, f32))

                def weigh(c, total):
                    part = jnp.exp(s_ref[c] - top)
                    s_ref[c] = part
                    return total + jnp.sum(part, axis=1, keepdims=True)

                total = lax.fori_loop(0, chunks, weigh, jnp.zeros((STACK, 1), f32))

                def mix(c, state):
                    context, rest_context = state
                    probs = s_ref[c] / total
                    low = probs.astype(bf16)
                    rest = (probs - low.astype(f32)).astype(bf16)
                    values = block_rows(v_ref, c * 8, 8)
                    return (context + dense_mul(low, values), rest_context + dense_mul(rest, values))

                zero = jnp.zeros((STACK, WIDE), f32)
                context, rest_context = lax.fori_loop(0, chunks, mix, (zero, zero))
                finish(t, context, context + rest_context, top, total)


def split_parts(value):
    high = value.astype(bf16).astype(f32)
    middle = (value - high).astype(bf16).astype(f32)
    return (high, middle, value - high - middle)


def delta_kernel(grad_ref, aux_ref, out_ref):
    rows = grad_ref.shape[0]
    lane = lanes(rows)
    grad = grad_ref[...].astype(f32)
    aux = aux_ref[...]
    result = jnp.where(lane < SHARE, grad, 0.0)
    product = grad * aux
    for head in range(GROUP_HEADS):
        delta = jnp.sum(jnp.where(head_lanes(lane, head), product, 0.0), axis=1, keepdims=True)
        lse = jnp.sum(jnp.where(lane == LSE_LANE + head, aux, 0.0), axis=1, keepdims=True)
        for p, value in enumerate(split_parts(lse)):
            result = jnp.where(lane == LSE_LANE + 3 * head + p, -value, result)
        for p, value in enumerate(split_parts(delta)):
            result = jnp.where(lane == DEL_LANE + 3 * head + p, -value, result)
    out_ref[...] = result.astype(bf16)


def backward_kernel(meta_ref, rand_ref, q_ref, k_ref, v_ref, g_ref, out_ref, dk_ref, dv_ref):
    place = meta_ref[0]
    total_rows = q_ref.shape[0]
    block_total = total_rows // BLOCK
    chunks = block_total // 8
    half = block_total // 16

    def grad_rows(block):
        other = (block // 2) ^ place
        piece = (other & 1) | ((other >> 1) & 2)
        slab = (other >> 3) + ((other >> 1) & 1) * half
        return block_rows(g_ref, slab * 8 + piece * 2 + (block & 1))

    def stacks(block):
        rows = block_rows(q_ref, block)
        grads = grad_rows(block)
        lane = lanes(BLOCK)
        blank = jnp.zeros_like(rows)
        queries = []
        outers = []
        for head in range(GROUP_HEADS):
            here = head_lanes(lane, head)
            queries.append(
                jnp.where(
                    here | (lane == MASK_LANE),
                    rows,
                    jnp.where(part_lanes(lane, LSE_LANE, head), grads, blank),
                )
            )
            outers.append(jnp.where(here | part_lanes(lane, DEL_LANE, head), grads, blank))
        return jnp.concatenate(queries, axis=0), jnp.concatenate(outers, axis=0)

    def query_side(stack, outer, keys, values):
        probs = jnp.exp(dense_right_t(stack, keys))
        scored = (probs * dense_right_t(outer, values)).astype(bf16)
        return dense_mul(scored, keys)

    def key_side(rows, keys, values, block, allowed):
        stack, outer = stacks(block)
        probs = jnp.exp(dense_right_t(keys, stack))
        if allowed is not None:
            probs = jnp.where(allowed, probs, 0.0)
        scored = (probs * dense_right_t(values, outer)).astype(bf16)
        dk_ref[rows, :] += dense_mul(scored, stack)
        dv_ref[rows, :] += dense_mul(probs.astype(bf16), outer)

    def put_query(t, stacked):
        out_ref[t // 2, pl.ds((t % 2) * BLOCK, BLOCK), :WIDE] = (merge_heads(stacked) * 0.125).astype(bf16)

    for t in range(8):
        block = own_block(place, t)

        @pl.when(block >= 2)
        def _(t=t, block=block):
            stack, outer = stacks(block)
            put_query(
                t,
                query_side(
                    stack,
                    outer,
                    key_set(k_ref, rand_ref, block, block_total, True),
                    key_set(v_ref, rand_ref, block, block_total, False),
                ),
            )

        @pl.when(block < 2)
        def _(t=t, block=block):
            stack, outer = stacks(block)

            def add(c, total):
                return total + query_side(stack, outer, block_rows(k_ref, c * 8, 8), block_rows(v_ref, c * 8, 8))

            put_query(t, lax.fori_loop(0, chunks, add, jnp.zeros((STACK, WIDE), f32)))

    dk_ref[...] = jnp.zeros_like(dk_ref)
    dv_ref[...] = jnp.zeros_like(dv_ref)
    for run in range(2):
        first = 2 * ((place ^ (4 * run)) & ~1)
        keys = block_rows(k_ref, first, 4)
        values = block_rows(v_ref, first, 4)
        rows = pl.ds(run * 4 * BLOCK, 4 * BLOCK)
        key_block = first + lax.broadcasted_iota(jnp.int32, (4 * BLOCK, STACK), 0) // BLOCK

        def band(step, carry, first=first, keys=keys, values=values, rows=rows, key_block=key_block):
            block = first - 1 + step

            @pl.when((block >= 2) & (block < block_total))
            def _():
                near = (key_block - block <= 1) & (block - key_block <= 1) & (key_block >= 2)
                key_side(rows, keys, values, block, near)

            return carry

        lax.fori_loop(0, 6, band, 0)
        key_side(rows, keys, values, 0, None)
        key_side(rows, keys, values, 1, None)

    def random_pairs(block, carry):
        for r in range(3):
            target = rand_ref[block * 3 + r]
            other = (target // 2) ^ place

            @pl.when((other & ~5) == 0)
            def _(target=target, other=other):
                start = pl.multiple_of(((other >> 2) & 1) * 4 * BLOCK + (target & 3) * BLOCK, BLOCK)
                key_side(
                    pl.ds(start, BLOCK), block_rows(k_ref, target), block_rows(v_ref, target), block, None
                )

        return carry

    lax.fori_loop(2, block_total, random_pairs, 0)

    @pl.when((place & ~5) == 0)
    def _():
        start = pl.multiple_of(((place >> 2) & 1) * 4 * BLOCK, BLOCK)
        keys = block_rows(k_ref, 0, 2)
        values = block_rows(v_ref, 0, 2)

        def every(block, carry):
            key_side(pl.ds(start, 2 * BLOCK), keys, values, block, None)
            return carry

        lax.fori_loop(2, block_total, every, 0)

    for piece in range(4):
        start = pl.multiple_of((piece // 2) * 4 * BLOCK + 2 * BLOCK * ((place ^ piece) & 1), BLOCK)
        out_ref[piece, :, WIDE : 2 * WIDE] = dk_ref[pl.ds(start, 2 * BLOCK), :].astype(bf16)
        out_ref[piece, :, 2 * WIDE :] = dv_ref[pl.ds(start, 2 * BLOCK), :].astype(bf16)


SMEM = pl.BlockSpec(memory_space=pltpu.SMEM)
VMEM = pl.BlockSpec(memory_space=pltpu.VMEM)


def shards(
    tokens,
    cotangent,
    w_query,
    w_key,
    w_value,
    w_output,
    w_inner,
    w_outer,
    gain_first,
    shift_first,
    gain_second,
    shift_second,
    attn_down,
    attn_up,
    inner_down,
    inner_up,
    outer_down,
    outer_up,
    lengths,
    rand_blocks,
    adapter_pick,
):
    device_total = lax.axis_size("seq") * lax.axis_size("head")
    local_rows = tokens.shape[0]
    seq_total = lengths.shape[0]
    members = device_total // seq_total
    rows_total = members * local_rows
    block_total = rows_total // BLOCK
    index = lax.axis_index("seq") * lax.axis_size("head") + lax.axis_index("head")
    place = index % members
    seq_number = index // members
    group = (place & 1) | ((place >> 1) & 2)
    seq_length = lengths[seq_number]
    chosen = adapter_pick[seq_number]

    def swap(value, mask):
        return lax.ppermute(value, AXES, [(j, j ^ mask) for j in range(device_total)])

    def select(table):
        return lax.dynamic_index_in_dim(table, chosen, 0, keepdims=False)

    down_sel, up_sel = select(attn_down), select(attn_up)
    inner_down_sel, inner_up_sel = select(inner_down), select(inner_up)
    outer_down_sel, outer_up_sel = select(outer_down), select(outer_up)

    def gather_all(value):
        return lax.all_gather(value, AXES, axis=0, tiled=False)

    early = gather_all(jnp.concatenate([tokens, w_query, w_key, w_value], axis=0))
    late = gather_all(
        jnp.concatenate(
            [w_output] + [w_inner[:, D * c : D * (c + 1)] for c in range(FF // D)] + [w_outer], axis=0
        )
    )
    slab = D // device_total
    tok_all = lax.dynamic_slice_in_dim(early, seq_number * members, members, 0)[:, :local_rows].reshape(rows_total, D)

    def early_weight(j):
        return early[:, local_rows + slab * j : local_rows + slab * (j + 1)].reshape(D, D)

    full_qkv = [early_weight(j) for j in range(3)]
    full_output = late[:, :slab].reshape(D, D)
    full_inner = jnp.concatenate(
        [late[:, slab * (1 + c) : slab * (2 + c)].reshape(D, D) for c in range(FF // D)], axis=1
    )
    full_outer = late[:, slab * (1 + FF // D) :].reshape(FF, D)

    rand_all = lax.all_gather(rand_blocks, "seq", axis=0, tiled=True)
    rand_flat = lax.dynamic_slice_in_dim(rand_all, seq_number * block_total, block_total, 0).reshape(-1)
    meta = jnp.stack([place, seq_length]).astype(jnp.int32)

    def share_columns(table):
        return lax.dynamic_slice_in_dim(table, group * SHARE, SHARE, 1)

    side_weight = jnp.concatenate(
        [
            piece
            for j in range(3)
            for piece in (
                share_columns(full_qkv[j]),
                down_sel[j].T,
                jnp.zeros((D, WIDE - SHARE - RANK), bf16),
            )
        ],
        axis=1,
    )
    side_up = jnp.stack(
        [
            jnp.pad(share_columns(up_sel[j]), ((WIDE // 4, WIDE // 4 - RANK), (0, WIDE - SHARE)))
            for j in range(3)
        ]
    )
    chunk = 8 * BLOCK
    wide_rows = jax.ShapeDtypeStruct((rows_total, WIDE), bf16)
    wide_block = pl.BlockSpec((chunk, WIDE), lambda c: (c, 0))
    query_all, key_all, value_all = pl.pallas_call(
        project_kernel,
        grid=(rows_total // chunk,),
        in_specs=[
            SMEM,
            pl.BlockSpec((chunk, D), lambda c: (c, 0)),
            pl.BlockSpec((D, 3 * WIDE), lambda c: (0, 0)),
            pl.BlockSpec((3, WIDE // 2, WIDE), lambda c: (0, 0, 0)),
        ],
        out_specs=[wide_block] * 3,
        out_shape=[wide_rows] * 3,
        compiler_params=pltpu.CompilerParams(vmem_limit_bytes=VMEM_LIMIT),
        name="project_all",
    )(meta, tok_all, side_weight, side_up)
    ctx, aux = pl.pallas_call(
        forward_kernel,
        in_specs=[SMEM, SMEM, VMEM, VMEM, VMEM],
        out_specs=[VMEM, VMEM],
        out_shape=[
            jax.ShapeDtypeStruct((chunk, WIDE), bf16),
            jax.ShapeDtypeStruct((chunk, WIDE), f32),
        ],
        scratch_shapes=[pltpu.VMEM((rows_total // chunk, STACK, chunk), f32)],
        compiler_params=pltpu.CompilerParams(vmem_limit_bytes=VMEM_LIMIT),
        name="attend_forward",
    )(meta, rand_flat, query_all, key_all, value_all)

    def exchange(pieces):
        return jnp.stack([pieces[0]] + [swap(pieces[a], PEERS[a]) for a in range(1, 4)])

    order = [g ^ group for g in range(4)]

    def natural(stack):
        return [lax.dynamic_index_in_dim(stack, source, 0, keepdims=False) for source in order]

    ctx_pieces = exchange(ctx.reshape(4, local_rows, WIDE)[:, :, :SHARE])
    context_tok = jnp.concatenate(natural(ctx_pieces), axis=1)

    token_pos = place * local_rows + jnp.arange(local_rows, dtype=jnp.int32)
    token_valid = (token_pos < seq_length).astype(f32)[:, None]
    attended, context_red = adapted(context_tok, full_output, down_sel[3], up_sel[3])
    first_sum = tokens.astype(f32) + attended
    first_norm, first_pull = jax.vjp(lambda hidden: normalize(hidden, gain_first, shift_first), first_sum)
    first_low = first_norm.astype(bf16)
    inner_pre, inner_red = adapted(first_low, full_inner, inner_down_sel, inner_up_sel)
    activated, gelu_pull = jax.vjp(exact_gelu, inner_pre)
    active_low = activated.astype(bf16)
    outer_out, outer_red = adapted(active_low, full_outer, outer_down_sel, outer_up_sel)
    second_norm, second_pull = jax.vjp(
        lambda hidden: normalize(hidden, gain_second, shift_second), first_norm + outer_out
    )
    output = (second_norm * token_valid).astype(bf16)
    (grad_second,) = second_pull(cotangent.astype(f32) * token_valid)
    grad_outer = grad_second.astype(bf16)
    grad_active, outer_down_grad, outer_up_grad = adapted_back(
        active_low, outer_red, grad_outer, full_outer, outer_down_sel, outer_up_sel
    )
    (grad_inner_pre,) = gelu_pull(grad_active)
    grad_inner = grad_inner_pre.astype(bf16)
    grad_first_in, inner_down_grad, inner_up_grad = adapted_back(
        first_low, inner_red, grad_inner, full_inner, inner_down_sel, inner_up_sel
    )
    (grad_attended,) = first_pull(grad_second + grad_first_in)
    grad_attended_low = grad_attended.astype(bf16)
    grad_context, context_down_grad, context_up_grad = adapted_back(
        context_tok, context_red, grad_attended_low, full_output, down_sel[3], up_sel[3]
    )
    grad_stack = grad_context.astype(bf16).reshape(local_rows, 4, SHARE).transpose(1, 0, 2)
    grad_pieces = exchange(jnp.stack(natural(grad_stack)))
    grad_own = jnp.pad(grad_pieces, ((0, 0), (0, 0), (0, WIDE - SHARE))).reshape(chunk, WIDE)
    grad_wide = pl.pallas_call(
        delta_kernel,
        in_specs=[VMEM, VMEM],
        out_specs=VMEM,
        out_shape=jax.ShapeDtypeStruct((chunk, WIDE), bf16),
        name="delta",
    )(grad_own, aux)
    slabs = jnp.concatenate([grad_wide] + [swap(grad_wide, 8 * r) for r in range(1, members // 8)], axis=0)
    grad_every = jnp.concatenate([slabs, swap(slabs, 2)], axis=0)
    grad_qkv = pl.pallas_call(
        backward_kernel,
        in_specs=[SMEM, SMEM, VMEM, VMEM, VMEM, VMEM],
        out_specs=VMEM,
        out_shape=jax.ShapeDtypeStruct((4, local_rows, 3 * WIDE), bf16),
        scratch_shapes=[pltpu.VMEM((chunk, WIDE), f32), pltpu.VMEM((chunk, WIDE), f32)],
        compiler_params=pltpu.CompilerParams(vmem_limit_bytes=VMEM_LIMIT),
        name="attend_backward",
    )(meta, rand_flat, query_all, key_all, value_all, grad_every)
    grad_parts = natural(exchange(grad_qkv))
    grad_tokens = grad_attended
    down_terms = []
    up_terms = []
    for j in range(3):
        grad_tok = jnp.concatenate([part[:, WIDE * j : WIDE * j + SHARE] for part in grad_parts], axis=1)
        reduced = dense_right_t(tokens, down_sel[j]).astype(bf16)
        grad_in, down_grad, up_grad = adapted_back(
            tokens, reduced, grad_tok, full_qkv[j], down_sel[j], up_sel[j]
        )
        grad_tokens = grad_tokens + grad_in
        down_terms.append(down_grad)
        up_terms.append(up_grad)

    def narrow(table):
        return [table[:, D * c : D * (c + 1)] for c in range(FF // D)]

    flat = jnp.concatenate(
        down_terms
        + [context_down_grad]
        + up_terms
        + [context_up_grad, inner_down_grad]
        + narrow(inner_up_grad)
        + narrow(outer_down_grad)
        + [outer_up_grad, jnp.zeros((32, D), f32)],
        axis=0,
    )
    for mask in (2, 1, 4):
        size = flat.shape[0] // 2
        upper = (place & mask) // mask
        keep = lax.dynamic_slice_in_dim(flat, upper * size, size, 0)
        give = lax.dynamic_slice_in_dim(flat, (1 - upper) * size, size, 0)
        flat = keep + swap(give, mask)
    sums = [flat] + [swap(flat, 8 * r) for r in range(1, members // 8)]
    while len(sums) > 1:
        sums = [sums[k] + sums[k + 1] for k in range(0, len(sums), 2)]
    flat = sums[0]
    for mask in (4, 1, 2):
        other = swap(flat, mask)
        upper = (place & mask) // mask
        flat = jnp.where(
            upper == 1,
            jnp.concatenate([other, flat], axis=0),
            jnp.concatenate([flat, other], axis=0),
        )
    held = [(flat, chosen)] + [
        (swap(flat, members * s), adapter_pick[seq_number ^ s]) for s in range(1, seq_total)
    ]

    def spread(first, count, width):
        def term(source, pick):
            rows = source[first * RANK : (first + count * (width // D)) * RANK]
            value = rows.reshape(count, width // D, RANK, D).transpose(0, 2, 1, 3).reshape(count, RANK, width)
            return (jnp.arange(ADAPTERS) == pick).astype(f32)[:, None, None, None] * value[None]

        total = functools.reduce(lambda x, y: x + y, [term(source, pick) for source, pick in held])
        return total if count > 1 else total[:, 0]

    wide = FF // D
    return (
        output,
        grad_tokens,
        spread(0, 4, D),
        spread(4, 4, D),
        spread(8, 1, D),
        spread(9, 1, FF),
        spread(9 + wide, 1, FF),
        spread(9 + 2 * wide, 1, D),
    )


def solution(mesh):
    rows = P(AXES, None)
    placed = (rows,) * 8 + (P(),) * 11 + (P("seq", None), P())
    return jax.shard_map(
        shards,
        mesh=mesh,
        in_specs=placed,
        out_specs=(rows, rows) + (P(),) * 6,
        check_vma=False,
    )
```

```python
import functools

import jax
import jax.numpy as jnp
from jax import lax
from jax.experimental import pallas as pl
from jax.experimental.pallas import tpu as pltpu
from jax.sharding import PartitionSpec as P

D = 768
HEADS = 12
HDIM = 64
BLOCK = 64
ADAPTERS = 8
RANK = 16
FF = 3072

PEERS = (0, 1, 4, 5)
GROUP_HEADS = HEADS // 4
SHARE = GROUP_HEADS * HDIM
WIDE = 256
LSE_LANE = SHARE
DEL_LANE = SHARE + 9
MASK_LANE = SHARE + 18
FLOOR = -1e30
STACK = GROUP_HEADS * BLOCK
AXES = ("seq", "head")
norm_eps = 1e-12
f32 = jnp.float32
bf16 = jnp.bfloat16
VMEM_LIMIT = 60 * 1024 * 1024


def dense_mul(left_op, right_op):
    return jnp.dot(left_op, right_op, preferred_element_type=f32)


def dense_right_t(left_op, right_op):
    return lax.dot_general(left_op, right_op, (((1,), (1,)), ((), ())), preferred_element_type=f32)


def dense_left_t(left_op, right_op):
    return lax.dot_general(left_op, right_op, (((0,), (0,)), ((), ())), preferred_element_type=f32)


def lanes(rows):
    return lax.broadcasted_iota(jnp.int32, (rows, WIDE), 1)


def head_lanes(lane, head):
    return (lane >= HDIM * head) & (lane < HDIM * (head + 1))


def part_lanes(lane, first, head):
    return (lane >= first + 3 * head) & (lane < first + 3 * head + 3)


def project_rows(raw, u_ref, position, seq_length):
    lane = lanes(raw.shape[0])
    data = lane < SHARE

    def part(j):
        piece = raw[:, WIDE * j : WIDE * (j + 1)]
        return (piece + dense_mul(piece[:, WIDE // 2 :].astype(bf16), u_ref[j])).astype(bf16).astype(f32)

    mask = jnp.where(position < seq_length, 0.0, FLOOR)
    query = jnp.where(data, part(0) * 0.125, jnp.where(lane == MASK_LANE, 1.0, 0.0)).astype(bf16)
    key = jnp.where(
        data, part(1), jnp.where(lane < DEL_LANE, 1.0, jnp.where(lane == MASK_LANE, mask, 0.0))
    ).astype(bf16)
    value = jnp.where(
        data, part(2), jnp.where((lane >= DEL_LANE) & (lane < MASK_LANE), 1.0, 0.0)
    ).astype(bf16)
    return query, key, value


def project_kernel(meta_ref, tok_ref, w_ref, u_ref, q_ref, k_ref, v_ref):
    rows = tok_ref.shape[0]
    position = pl.program_id(0) * rows + lax.broadcasted_iota(jnp.int32, (rows, WIDE), 0)
    q_ref[...], k_ref[...], v_ref[...] = project_rows(
        dense_mul(tok_ref[...], w_ref[...]), u_ref, position, meta_ref[1]
    )


def gathered_kernel(meta_ref, rand_ref, slice_ref, down_ref, u_ref, *refs):
    pieces = refs[: len(SLICE_ORDER)]
    q_ref, k_ref, v_ref, *ctx_refs, aux_ref, s_ref, tok_ref, wide_ref, w_ref = refs[len(SLICE_ORDER) :]
    place = meta_ref[0]
    slab = D // len(SLICE_ORDER)
    for s, offset in enumerate(SLICE_ORDER):
        start = pl.multiple_of((place ^ offset) * slab, 8)
        wide_ref[pl.ds(start, slab), :] = slice_ref[slab * s : slab * (s + 1), :]
    column = lax.broadcasted_iota(jnp.int32, (D, 3 * WIDE), 1) & (WIDE - 1)
    w_ref[...] = jnp.where(column < SHARE, wide_ref[...].astype(bf16), down_ref[...])
    rows = 2 * BLOCK
    first = 4 - 3 * ((place >> 1) & 1)
    arrival = [
        side ^ depth ^ step
        for side, near in ((0, first), (2, 5 - first))
        for depth in DEPTHS
        for step in (0, near, 5 - near, 5)
    ]
    for piece, offset in zip(pieces, arrival, strict=True):
        tok_ref[pl.ds(pl.multiple_of((place ^ offset) * rows, rows), rows), :] = piece[...]
    chunk = 8 * BLOCK

    def project(c, carry):
        here = pl.ds(pl.multiple_of(c * chunk, chunk), chunk)
        position = c * chunk + lax.broadcasted_iota(jnp.int32, (chunk, WIDE), 0)
        q_ref[here, :], k_ref[here, :], v_ref[here, :] = project_rows(
            dense_mul(tok_ref[here, :], w_ref[...]), u_ref, position, meta_ref[1]
        )
        return carry

    lax.fori_loop(0, tok_ref.shape[0] // chunk, project, 0)
    forward_kernel(meta_ref, rand_ref, q_ref, k_ref, v_ref, *ctx_refs, aux_ref, s_ref)


def block_rows(ref, block, count=1):
    return ref[pl.ds(pl.multiple_of(block * BLOCK, BLOCK), count * BLOCK), :]


def merge_heads(stacked):
    lane = lanes(BLOCK)
    total = jnp.zeros((BLOCK, WIDE), f32)
    for head in range(GROUP_HEADS):
        total = jnp.where(head_lanes(lane, head), stacked[BLOCK * head : BLOCK * (head + 1)], total)
    return total


def key_set(ref, rand_ref, block, block_total, fill):
    own = block_rows(ref, block)
    left = block_rows(ref, jnp.maximum(block - 1, 0))
    right = block_rows(ref, jnp.minimum(block + 1, block_total - 1))
    if fill:
        blank = jnp.where(lanes(BLOCK) == MASK_LANE, FLOOR, 0.0).astype(bf16)
        left = jnp.where(block - 1 >= 2, left, blank)
        right = jnp.where(block + 1 < block_total, right, blank)
    rand = [block_rows(ref, rand_ref[block * 3 + r]) for r in range(3)]
    return jnp.concatenate([own, left, right, block_rows(ref, 0, 2)] + rand, axis=0)


def own_block(place, t):
    return 2 * (place ^ PEERS[t // 2]) + t % 2


def forward_kernel(meta_ref, rand_ref, q_ref, k_ref, v_ref, *refs):
    ctx_refs, aux_ref, s_ref = refs[:4], refs[4], refs[5]
    place = meta_ref[0]
    total_rows = q_ref.shape[0]
    block_total = total_rows // BLOCK
    chunk = 8 * BLOCK
    chunks = total_rows // chunk

    def queries(block):
        rows = block_rows(q_ref, block)
        lane = lanes(BLOCK)
        blank = jnp.zeros_like(rows)
        return jnp.concatenate(
            [
                jnp.where(head_lanes(lane, head) | (lane == MASK_LANE), rows, blank)
                for head in range(GROUP_HEADS)
            ],
            axis=0,
        )

    def finish(t, low, exact, top, total):
        lane = lanes(BLOCK)
        rows = pl.ds(t * BLOCK, BLOCK)
        ctx_refs[t // 2][pl.ds((t % 2) * BLOCK, BLOCK), :] = merge_heads(low).astype(bf16)
        aux = merge_heads(exact)
        lse = top + jnp.log(total)
        for head in range(GROUP_HEADS):
            aux = jnp.where(lane == LSE_LANE + head, lse[BLOCK * head : BLOCK * (head + 1)], aux)
        aux_ref[rows, :] = aux

    for t in range(8):
        block = own_block(place, t)

        @pl.when(block >= 2)
        def _(t=t, block=block):
            scores = dense_right_t(queries(block), key_set(k_ref, rand_ref, block, block_total, True))
            top = jnp.max(scores, axis=1, keepdims=True)
            weights = jnp.exp(scores - top)
            total = jnp.sum(weights, axis=1, keepdims=True)
            probs = weights / total
            low = probs.astype(bf16)
            rest = (probs - low.astype(f32)).astype(bf16)
            values = key_set(v_ref, rand_ref, block, block_total, False)
            context = dense_mul(low, values)
            finish(t, context, context + dense_mul(rest, values), top, total)

        if t < 2 or (t // 2) in (1, 2, 3):

            @pl.when(block < 2)
            def _(t=t, block=block):
                stack = queries(block)

                def score(c, top):
                    part = dense_right_t(stack, block_rows(k_ref, c * 8, 8))
                    s_ref[c] = part
                    return jnp.maximum(top, jnp.max(part, axis=1, keepdims=True))

                top = lax.fori_loop(0, chunks, score, jnp.full((STACK, 1), FLOOR, f32))

                def weigh(c, total):
                    part = jnp.exp(s_ref[c] - top)
                    s_ref[c] = part
                    return total + jnp.sum(part, axis=1, keepdims=True)

                total = lax.fori_loop(0, chunks, weigh, jnp.zeros((STACK, 1), f32))

                def mix(c, state):
                    context, rest_context = state
                    probs = s_ref[c] / total
                    low = probs.astype(bf16)
                    rest = (probs - low.astype(f32)).astype(bf16)
                    values = block_rows(v_ref, c * 8, 8)
                    return (context + dense_mul(low, values), rest_context + dense_mul(rest, values))

                zero = jnp.zeros((STACK, WIDE), f32)
                context, rest_context = lax.fori_loop(0, chunks, mix, (zero, zero))
                finish(t, context, context + rest_context, top, total)


def split_parts(value):
    high = value.astype(bf16).astype(f32)
    middle = (value - high).astype(bf16).astype(f32)
    return (high, middle, value - high - middle)


def delta_kernel(*refs):
    grad_refs, aux_ref, out_ref = refs[:4], refs[4], refs[5]
    rows = 2 * BLOCK
    lane = lanes(rows)
    for a in range(4):
        here = pl.ds(a * rows, rows)
        grad = grad_refs[a][...].astype(f32)
        aux = aux_ref[here, :]
        result = jnp.where(lane < SHARE, grad, 0.0)
        product = grad * aux
        for head in range(GROUP_HEADS):
            delta = jnp.sum(jnp.where(head_lanes(lane, head), product, 0.0), axis=1, keepdims=True)
            lse = jnp.sum(jnp.where(lane == LSE_LANE + head, aux, 0.0), axis=1, keepdims=True)
            for p, value in enumerate(split_parts(lse)):
                result = jnp.where(lane == LSE_LANE + 3 * head + p, -value, result)
            for p, value in enumerate(split_parts(delta)):
                result = jnp.where(lane == DEL_LANE + 3 * head + p, -value, result)
        out_ref[here, :] = result.astype(bf16)


def backward_kernel(meta_ref, rand_ref, q_ref, k_ref, v_ref, *refs):
    slab_refs, out_refs, (g_ref, dk_ref, dv_ref) = refs[:-7], refs[-7:-3], refs[-3:]
    place = meta_ref[0]
    total_rows = q_ref.shape[0]
    for number, slab_ref in enumerate(slab_refs):
        g_ref[8 * BLOCK * number : 8 * BLOCK * (number + 1), :] = slab_ref[...]
    block_total = total_rows // BLOCK
    chunks = block_total // 8
    half = block_total // 16

    def grad_rows(block):
        other = (block // 2) ^ place
        piece = (other & 1) | ((other >> 1) & 2)
        slab = (other >> 3) + ((other >> 1) & 1) * half
        return block_rows(g_ref, slab * 8 + piece * 2 + (block & 1))

    def stacks(block):
        rows = block_rows(q_ref, block)
        grads = grad_rows(block)
        lane = lanes(BLOCK)
        blank = jnp.zeros_like(rows)
        queries = []
        outers = []
        for head in range(GROUP_HEADS):
            here = head_lanes(lane, head)
            queries.append(
                jnp.where(
                    here | (lane == MASK_LANE),
                    rows,
                    jnp.where(part_lanes(lane, LSE_LANE, head), grads, blank),
                )
            )
            outers.append(jnp.where(here | part_lanes(lane, DEL_LANE, head), grads, blank))
        return jnp.concatenate(queries, axis=0), jnp.concatenate(outers, axis=0)

    def query_side(stack, outer, keys, values):
        probs = jnp.exp(dense_right_t(stack, keys))
        scored = (probs * dense_right_t(outer, values)).astype(bf16)
        return dense_mul(scored, keys)

    def key_side(rows, keys, values, block, allowed):
        stack, outer = stacks(block)
        probs = jnp.exp(dense_right_t(keys, stack))
        if allowed is not None:
            probs = jnp.where(allowed, probs, 0.0)
        scored = (probs * dense_right_t(values, outer)).astype(bf16)
        dk_ref[rows, :] += dense_mul(scored, stack)
        dv_ref[rows, :] += dense_mul(probs.astype(bf16), outer)

    def put_query(t, stacked):
        out_refs[t // 2][pl.ds((t % 2) * BLOCK, BLOCK), :WIDE] = (merge_heads(stacked) * 0.125).astype(bf16)

    for t in range(8):
        block = own_block(place, t)

        @pl.when(block >= 2)
        def _(t=t, block=block):
            stack, outer = stacks(block)
            put_query(
                t,
                query_side(
                    stack,
                    outer,
                    key_set(k_ref, rand_ref, block, block_total, True),
                    key_set(v_ref, rand_ref, block, block_total, False),
                ),
            )

        @pl.when(block < 2)
        def _(t=t, block=block):
            stack, outer = stacks(block)

            def add(c, total):
                return total + query_side(stack, outer, block_rows(k_ref, c * 8, 8), block_rows(v_ref, c * 8, 8))

            put_query(t, lax.fori_loop(0, chunks, add, jnp.zeros((STACK, WIDE), f32)))

    dk_ref[...] = jnp.zeros_like(dk_ref)
    dv_ref[...] = jnp.zeros_like(dv_ref)
    for run in range(2):
        first = 2 * ((place ^ (4 * run)) & ~1)
        keys = block_rows(k_ref, first, 4)
        values = block_rows(v_ref, first, 4)
        rows = pl.ds(run * 4 * BLOCK, 4 * BLOCK)
        key_block = first + lax.broadcasted_iota(jnp.int32, (4 * BLOCK, STACK), 0) // BLOCK

        def band(step, carry, first=first, keys=keys, values=values, rows=rows, key_block=key_block):
            block = first - 1 + step

            @pl.when((block >= 2) & (block < block_total))
            def _():
                near = (key_block - block <= 1) & (block - key_block <= 1) & (key_block >= 2)
                key_side(rows, keys, values, block, near)

            return carry

        lax.fori_loop(0, 6, band, 0)
        key_side(rows, keys, values, 0, None)
        key_side(rows, keys, values, 1, None)

    def random_pairs(block, carry):
        for r in range(3):
            target = rand_ref[block * 3 + r]
            other = (target // 2) ^ place

            @pl.when((other & ~5) == 0)
            def _(target=target, other=other):
                start = pl.multiple_of(((other >> 2) & 1) * 4 * BLOCK + (target & 3) * BLOCK, BLOCK)
                key_side(
                    pl.ds(start, BLOCK), block_rows(k_ref, target), block_rows(v_ref, target), block, None
                )

        return carry

    lax.fori_loop(2, block_total, random_pairs, 0)

    @pl.when((place & ~5) == 0)
    def _():
        start = pl.multiple_of(((place >> 2) & 1) * 4 * BLOCK, BLOCK)
        keys = block_rows(k_ref, 0, 2)
        values = block_rows(v_ref, 0, 2)

        def every(block, carry):
            key_side(pl.ds(start, 2 * BLOCK), keys, values, block, None)
            return carry

        lax.fori_loop(2, block_total, every, 0)

    for piece in range(4):
        start = pl.multiple_of((piece // 2) * 4 * BLOCK + 2 * BLOCK * ((place ^ piece) & 1), BLOCK)
        out_refs[piece][:, WIDE : 2 * WIDE] = dk_ref[pl.ds(start, 2 * BLOCK), :].astype(bf16)
        out_refs[piece][:, 2 * WIDE :] = dv_ref[pl.ds(start, 2 * BLOCK), :].astype(bf16)


def normal(hidden):
    center = hidden - jnp.mean(hidden, axis=-1, keepdims=True)
    root = lax.rsqrt(jnp.mean(center * center, axis=-1, keepdims=True) + norm_eps)
    return center * root, root


def normal_back(grad, normed, root):
    mean = jnp.mean(grad, axis=-1, keepdims=True)
    return root * (grad - mean - normed * jnp.mean(grad * normed, axis=-1, keepdims=True))


def middle_kernel(
    fast,
    meta_ref,
    ctx_refs,
    tok_ref,
    cot_ref,
    late_ref,
    gain_ref,
    down_ref,
    up_ref,
    inner_down_ref,
    inner_up_ref,
    outer_down_ref,
    outer_up_ref,
    wide_ref,
    out_ref,
    grad_ref,
    piece_refs,
    terms_ref,
    hold_ref,
    pre_ref,
    act_ref,
    gin_ref,
):
    group = meta_ref[2]
    rows = tok_ref.shape[0]
    if fast:
        slab = 24
        for pair in range(D // (2 * slab)):
            block = late_ref[2 * slab * pair : 2 * slab * (pair + 1), D + FF :].astype(f32)
            cut = [
                block[slab * side : slab * (side + 1), D * c : D * (c + 1)]
                for side in range(2)
                for c in range(FF // D)
            ]
            wide_ref[8 * slab * pair : 8 * slab * (pair + 1), :] = jnp.concatenate(cut, axis=0).astype(bf16)
    for a in range(4):
        hold_ref[a] = ctx_refs[a][...]
    context = jnp.concatenate([hold_ref[group ^ g][:, :SHARE] for g in range(4)], axis=1)
    context_red = dense_right_t(context, down_ref[...]).astype(bf16)
    attended = dense_mul(context, late_ref[:, :D]) + dense_mul(context_red, up_ref[...])
    first, first_root = normal(tok_ref[...].astype(f32) + attended)
    first_norm = first * gain_ref[0:1, :] + gain_ref[1:2, :]
    first_low = first_norm.astype(bf16)
    inner_red = dense_right_t(first_low, inner_down_ref[...]).astype(bf16)
    outer_red = jnp.zeros((rows, RANK), f32)
    outer_out = jnp.zeros((rows, D), f32)
    for c in range(FF // D):
        here = slice(D * c, D * (c + 1))
        pre = dense_mul(first_low, late_ref[:, D * (c + 1) : D * (c + 2)]) + dense_mul(
            inner_red, inner_up_ref[:, here]
        )
        pre_ref[:, here] = pre
        active = (0.5 * pre * (1.0 + lax.erf(pre * 0.7071067811865476))).astype(bf16)
        act_ref[:, here] = active
        outer_red = outer_red + dense_right_t(active, outer_down_ref[:, here])
        outer_out = outer_out + dense_mul(active, wide_ref[here, :])
    outer_red = outer_red.astype(bf16)
    outer_out = outer_out + dense_mul(outer_red, outer_up_ref[...])
    second, second_root = normal(first_norm + outer_out)
    position = meta_ref[0] * rows + lax.broadcasted_iota(jnp.int32, (rows, D), 0)
    valid = (position < meta_ref[1]).astype(f32)
    out_ref[...] = ((second * gain_ref[2:3, :] + gain_ref[3:4, :]) * valid).astype(bf16)
    grad_second = normal_back(valid * cot_ref[...].astype(f32) * gain_ref[2:3, :], second, second_root)
    grad_outer = grad_second.astype(bf16)
    first_up = RANK * 3
    first_down = RANK * (3 + FF // D)
    terms_ref[first_down + RANK * (FF // D) :, :] = dense_left_t(outer_red, grad_outer)
    outer_grad_red = dense_right_t(grad_outer, outer_up_ref[...]).astype(bf16)
    inner_grad_red = jnp.zeros((rows, RANK), f32)
    grad_first = grad_second
    for c in range(FF // D):
        here = slice(D * c, D * (c + 1))
        grad_active = dense_right_t(grad_outer, wide_ref[here, :]) + dense_mul(
            outer_grad_red, outer_down_ref[:, here]
        )
        pre = pre_ref[:, here]
        slope = 0.5 * (1.0 + lax.erf(pre * 0.7071067811865476)) + pre * (
            0.3989422804014327 * jnp.exp(-0.5 * pre * pre)
        )
        grad_inner = (slope * grad_active).astype(bf16)
        terms_ref[first_up + RANK * c : first_up + RANK * (c + 1), :] = dense_left_t(inner_red, grad_inner)
        terms_ref[first_down + RANK * c : first_down + RANK * (c + 1), :] = dense_left_t(
            outer_grad_red, act_ref[:, here]
        )
        inner_grad_red = inner_grad_red + dense_right_t(grad_inner, inner_up_ref[:, here])
        grad_first = grad_first + dense_right_t(grad_inner, late_ref[:, D * (c + 1) : D * (c + 2)])
    inner_grad_red = inner_grad_red.astype(bf16)
    terms_ref[2 * RANK : 3 * RANK, :] = dense_left_t(inner_grad_red, first_low)
    grad_first = grad_first + dense_mul(inner_grad_red, inner_down_ref[...])
    grad_attended = normal_back(grad_first * gain_ref[0:1, :], first, first_root)
    grad_ref[...] = grad_attended
    grad_low = grad_attended.astype(bf16)
    context_grad_red = dense_right_t(grad_low, up_ref[...]).astype(bf16)
    terms_ref[:RANK, :] = dense_left_t(context_grad_red, context)
    terms_ref[RANK : 2 * RANK, :] = dense_left_t(context_red, grad_low)
    grad_context = (
        dense_right_t(grad_low, late_ref[:, :D]) + dense_mul(context_grad_red, down_ref[...])
    ).astype(bf16)
    blank = jnp.zeros((rows, WIDE - SHARE), bf16)
    for g in range(4):
        hold_ref[group ^ g] = jnp.concatenate([grad_context[:, SHARE * g : SHARE * (g + 1)], blank], axis=1)
    for a in range(4):
        piece_refs[a][...] = hold_ref[a]


def finish_kernel(fast, meta_ref, *refs):
    part_refs = refs[:4]
    tok_ref, w_ref, down_ref, up_ref, grad_ref, early_ref, out_ref, terms_ref, hold_ref, sum_ref = refs[4:]
    group = meta_ref[2]
    core = (meta_ref[0] >> 1) & 1
    for a in range(4):
        hold_ref[a] = part_refs[a][...]
    tokens = tok_ref[...]
    total = grad_ref[...]
    for j in range(3):
        grad = jnp.concatenate(
            [hold_ref[group ^ g][:, WIDE * j : WIDE * j + SHARE] for g in range(4)], axis=1
        )
        reduced = dense_right_t(tokens, down_ref[j]).astype(bf16)
        grad_reduced = dense_right_t(grad, up_ref[j]).astype(bf16)
        sum_ref[RANK * j : RANK * (j + 1), :] = dense_left_t(grad_reduced, tokens)
        sum_ref[RANK * (4 + j) : RANK * (5 + j), :] = dense_left_t(reduced, grad)
        total = total + dense_right_t(grad, w_ref[:, D * j : D * (j + 1)]) + dense_mul(grad_reduced, down_ref[j])
    out_ref[...] = total
    sum_ref[RANK * 3 : RANK * 4, :] = early_ref[:RANK, :]
    sum_ref[RANK * 7 : RANK * 8, :] = early_ref[RANK : 2 * RANK, :]
    sum_ref[RANK * 8 : KINDS * RANK, :] = early_ref[2 * RANK :, :]
    sum_ref[KINDS * RANK :, :] = jnp.zeros((SUM_ROWS - KINDS * RANK, D), f32)
    if fast:
        for part in range(8):
            terms_ref[(part // 4) ^ core, (part % 4) ^ group] = sum_ref[PART_ROWS * part : PART_ROWS * (part + 1), :]
    else:
        terms_ref[...] = sum_ref[...]


def spread_kernel(meta_ref, *refs):
    near_refs, far_refs = refs[:4], refs[4:8]
    outs = refs[14:20]
    sum_ref, sems = refs[20:]
    group = meta_ref[2]
    core = (meta_ref[0] >> 1) & 1
    chosen = meta_ref[3]
    for a in range(4):
        for side, ref in ((0, near_refs[a]), (1, far_refs[a])):
            start = pl.multiple_of(((core ^ side) * 4 + (group ^ a)) * PART_ROWS, 8)
            sum_ref[pl.ds(start, PART_ROWS), :] = ref[...]
    places = [outs[0].at[chosen, j] for j in range(4)] + [outs[1].at[chosen, j] for j in range(4)]
    places.append(outs[2].at[chosen])
    places += [outs[n].at[chosen, :, pl.ds(D * c, D)] for n in (3, 4) for c in range(FF // D)]
    places.append(outs[5].at[chosen])
    copies = [
        pltpu.make_async_copy(sum_ref.at[pl.ds(RANK * n, RANK), :], where, sems.at[n])
        for n, where in enumerate(places)
    ]
    for copy in copies:
        copy.start()
    for copy in copies:
        copy.wait()


KINDS = 18
SUM_ROWS = 320
PART_ROWS = SUM_ROWS // 8
ANY = pl.BlockSpec(memory_space=pl.ANY)
SMEM = pl.BlockSpec(memory_space=pltpu.SMEM)
VMEM = pl.BlockSpec(memory_space=pltpu.VMEM)
DEPTHS = (0, 8, 16, 24)
SLICE_ORDER = tuple(side ^ depth ^ peer for side in (0, 2) for depth in DEPTHS for peer in PEERS)


def gather_rows(value, device_total):
    def send(piece, even, odd):
        return lax.ppermute(
            piece, AXES, [(j, j ^ (odd if (j >> 1) & 1 else even)) for j in range(device_total)]
        )

    held = []
    for depth in DEPTHS:
        start = value if depth == 0 else send(value, depth, depth)
        across = send(start, 4, 1)
        held += [start, across, send(start, 1, 4), send(across, 1, 4)]
    return held + [send(piece, 2, 2) for piece in held]


def shards(
    tokens,
    cotangent,
    w_query,
    w_key,
    w_value,
    w_output,
    w_inner,
    w_outer,
    gain_first,
    shift_first,
    gain_second,
    shift_second,
    attn_down,
    attn_up,
    inner_down,
    inner_up,
    outer_down,
    outer_up,
    lengths,
    rand_blocks,
    adapter_pick,
):
    device_total = lax.axis_size("seq") * lax.axis_size("head")
    local_rows = tokens.shape[0]
    seq_total = lengths.shape[0]
    members = device_total // seq_total
    rows_total = members * local_rows
    block_total = rows_total // BLOCK
    index = lax.axis_index("seq") * lax.axis_size("head") + lax.axis_index("head")
    place = index % members
    seq_number = index // members
    group = (place & 1) | ((place >> 1) & 2)
    seq_length = lengths[seq_number]
    chosen = adapter_pick[seq_number]

    def swap(value, mask):
        return lax.ppermute(value, AXES, [(j, j ^ mask) for j in range(device_total)])

    def select(table):
        return lax.dynamic_index_in_dim(table, chosen, 0, keepdims=False)

    down_sel, up_sel = select(attn_down), select(attn_up)
    inner_down_sel, inner_up_sel = select(inner_down), select(inner_up)
    outer_down_sel, outer_up_sel = select(outer_down), select(outer_up)

    def gather_all(value):
        return lax.all_gather(value, AXES, axis=0, tiled=True)

    slab = D // device_total
    full_qkv = gather_all(jnp.concatenate([w_query, w_key, w_value], axis=1))
    late = gather_all(
        jnp.concatenate([w_output, w_inner] + [w_outer[slab * c : slab * (c + 1)] for c in range(FF // D)], axis=1)
    )
    meta = jnp.stack([place, seq_length, group, chosen]).astype(jnp.int32)
    fast = device_total == 32 and members == 32

    def share_columns(table, which=group):
        return lax.dynamic_slice_in_dim(table, which * SHARE, SHARE, table.ndim - 1)

    side_up = jnp.stack(
        [
            jnp.pad(share_columns(up_sel[j]), ((WIDE // 4, WIDE // 4 - RANK), (0, WIDE - SHARE)))
            for j in range(3)
        ]
    )
    side_down = jnp.concatenate(
        [jnp.pad(down_sel[j].T, ((0, 0), (SHARE, WIDE - SHARE - RANK))) for j in range(3)], axis=1
    )
    chunk = 8 * BLOCK
    wide_rows = jax.ShapeDtypeStruct((rows_total, WIDE), bf16)
    piece_shapes = [jax.ShapeDtypeStruct((local_rows, WIDE), bf16)] * 4
    ctx_shapes = piece_shapes + [jax.ShapeDtypeStruct((chunk, WIDE), f32)]
    score_scratch = pltpu.VMEM((rows_total // chunk, STACK, chunk), f32)
    if fast:
        columns = jnp.stack([w_query, w_key, w_value], axis=1)
        marks = jnp.pad(
            rand_blocks.reshape(1, 1, -1).astype(bf16), ((0, slab - 1), (0, 2), (0, WIDE - SHARE - rand_blocks.size))
        )

        def slices(peer):
            return jnp.concatenate([share_columns(columns, group ^ peer), marks], axis=2).reshape(slab, 3 * WIDE)

        pieces = gather_rows(tokens, device_total)
        mine = jnp.concatenate([slices(0)] + [swap(slices(p), PEERS[p]) for p in range(1, 4)], axis=0)
        mine, pieces[5] = lax.optimization_barrier((mine, pieces[5]))
        mine = jnp.concatenate([mine] + [swap(mine, depth) for depth in DEPTHS[1:]], axis=0)
        mine = jnp.concatenate([mine, swap(mine, 2)], axis=0)
        marks_all = mine.reshape(device_total, slab, 3 * WIDE)[:, 0, SHARE : SHARE + rand_blocks.size]
        source = jnp.argsort(jnp.array(SLICE_ORDER))[(2 * jnp.arange(device_total // 2)) ^ place]
        rand_flat = marks_all[source].astype(jnp.int32).reshape(-1)
        query_all, key_all, value_all, *ctx, aux = pl.pallas_call(
            gathered_kernel,
            in_specs=[SMEM, SMEM] + [VMEM] * (3 + len(pieces)),
            out_specs=[VMEM] * 8,
            out_shape=[wide_rows] * 3 + ctx_shapes,
            scratch_shapes=[
                score_scratch,
                pltpu.VMEM((rows_total, D), bf16),
                pltpu.VMEM((D, 3 * WIDE), f32),
                pltpu.VMEM((D, 3 * WIDE), bf16),
            ],
            compiler_params=pltpu.CompilerParams(vmem_limit_bytes=VMEM_LIMIT),
            name="project_attend",
        )(meta, rand_flat, mine.astype(f32), side_down, side_up, *pieces)
    else:
        tok_all = lax.dynamic_slice_in_dim(gather_all(tokens), seq_number * rows_total, rows_total, 0)
        rand_all = lax.all_gather(rand_blocks, "seq", axis=0, tiled=True)
        rand_flat = lax.dynamic_slice_in_dim(rand_all, seq_number * block_total, block_total, 0).reshape(-1)
        side_weight = (
            jnp.concatenate(
                [
                    jnp.pad(share_columns(full_qkv[:, D * j : D * (j + 1)]), ((0, 0), (0, WIDE - SHARE)))
                    for j in range(3)
                ],
                axis=1,
            )
            + side_down
        )
        wide_block = pl.BlockSpec((chunk, WIDE), lambda c: (c, 0))
        query_all, key_all, value_all = pl.pallas_call(
            project_kernel,
            grid=(rows_total // chunk,),
            in_specs=[
                SMEM,
                pl.BlockSpec((chunk, D), lambda c: (c, 0)),
                pl.BlockSpec((D, 3 * WIDE), lambda c: (0, 0)),
                pl.BlockSpec((3, WIDE // 2, WIDE), lambda c: (0, 0, 0)),
            ],
            out_specs=[wide_block] * 3,
            out_shape=[wide_rows] * 3,
            compiler_params=pltpu.CompilerParams(vmem_limit_bytes=VMEM_LIMIT),
            name="project_all",
        )(meta, tok_all, side_weight, side_up)
        *ctx, aux = pl.pallas_call(
            forward_kernel,
            in_specs=[SMEM, SMEM, VMEM, VMEM, VMEM],
            out_specs=[VMEM] * 5,
            out_shape=ctx_shapes,
            scratch_shapes=[score_scratch],
            compiler_params=pltpu.CompilerParams(vmem_limit_bytes=VMEM_LIMIT),
            name="attend_forward",
        )(meta, rand_flat, query_all, key_all, value_all)

    def exchange(pieces):
        return [pieces[0]] + [swap(pieces[a], PEERS[a]) for a in range(1, 4)]

    gains = jnp.stack([gain_first, shift_first, gain_second, shift_second])
    middle_in = [tokens, cotangent, late, gains, down_sel[3], up_sel[3]]
    middle_in += [inner_down_sel, inner_up_sel, outer_down_sel, outer_up_sel]
    wide_shape = [pltpu.VMEM((FF, D), bf16)]
    if not fast:
        middle_in.append(
            late[:, D + FF :].reshape(device_total, slab, FF // D, D).transpose(0, 2, 1, 3).reshape(FF, D)
        )
        wide_shape = []
    count = len(middle_in)

    def middle(meta_ref, *refs):
        ins, outs, scratch = refs[4 : 4 + count], refs[4 + count : 11 + count], refs[11 + count :]
        wide_ref = scratch[-1] if fast else ins[-1]
        middle_kernel(
            fast, meta_ref, refs[:4], *ins[:10], wide_ref, *outs[:2], outs[2:6], outs[6], *scratch[:4]
        )

    output, grad_attended, *grad_pieces, early_terms = pl.pallas_call(
        middle,
        in_specs=[SMEM] + [VMEM] * (4 + count),
        out_specs=[VMEM] * 7,
        out_shape=[
            jax.ShapeDtypeStruct((local_rows, D), bf16),
            jax.ShapeDtypeStruct((local_rows, D), f32),
        ]
        + piece_shapes
        + [jax.ShapeDtypeStruct(((KINDS - 6) * RANK, D), f32)],
        scratch_shapes=[
            pltpu.VMEM((4, local_rows, WIDE), bf16),
            pltpu.VMEM((local_rows, FF), f32),
            pltpu.VMEM((local_rows, FF), bf16),
            pltpu.VMEM((local_rows, FF), bf16),
        ]
        + wide_shape,
        compiler_params=pltpu.CompilerParams(vmem_limit_bytes=VMEM_LIMIT),
        name="middle",
    )(meta, *exchange(ctx), *middle_in)
    grad_wide = pl.pallas_call(
        delta_kernel,
        in_specs=[VMEM] * 5,
        out_specs=VMEM,
        out_shape=jax.ShapeDtypeStruct((chunk, WIDE), bf16),
        name="delta",
    )(*exchange(grad_pieces), aux)
    slabs = [grad_wide] + [swap(grad_wide, 8 * r) for r in range(1, members // 8)]
    slabs = slabs + [swap(slab_rows, 2) for slab_rows in slabs]
    grad_qkv = pl.pallas_call(
        backward_kernel,
        in_specs=[SMEM, SMEM] + [VMEM] * (3 + len(slabs)),
        out_specs=[VMEM] * 4,
        out_shape=[jax.ShapeDtypeStruct((local_rows, 3 * WIDE), bf16)] * 4,
        scratch_shapes=[
            pltpu.VMEM((rows_total, WIDE), bf16),
            pltpu.VMEM((chunk, WIDE), f32),
            pltpu.VMEM((chunk, WIDE), f32),
        ],
        compiler_params=pltpu.CompilerParams(vmem_limit_bytes=VMEM_LIMIT),
        name="attend_backward",
    )(meta, rand_flat, query_all, key_all, value_all, *slabs)
    grad_tokens, terms = pl.pallas_call(
        functools.partial(finish_kernel, fast),
        in_specs=[SMEM] + [VMEM] * 10,
        out_specs=[VMEM, VMEM],
        out_shape=[
            jax.ShapeDtypeStruct((local_rows, D), f32),
            jax.ShapeDtypeStruct((2, 4, PART_ROWS, D) if fast else (SUM_ROWS, D), f32),
        ],
        scratch_shapes=[pltpu.VMEM((4, local_rows, 3 * WIDE), bf16), pltpu.VMEM((SUM_ROWS, D), f32)],
        compiler_params=pltpu.CompilerParams(vmem_limit_bytes=VMEM_LIMIT),
        name="finish",
    )(meta, *exchange(grad_qkv), tokens, full_qkv, down_sel[:3], up_sel[:3], grad_attended, early_terms)

    out_shapes = [
        (ADAPTERS, 4, RANK, D),
        (ADAPTERS, 4, RANK, D),
        (ADAPTERS, RANK, D),
        (ADAPTERS, RANK, FF),
        (ADAPTERS, RANK, FF),
        (ADAPTERS, RANK, D),
    ]
    if fast:
        paired = terms[0] + swap(terms[1], 2)
        moved = [paired[0]] + [swap(paired[a], PEERS[a]) for a in range(1, 4)]
        part = (moved[0] + moved[1]) + (moved[2] + moved[3])
        moved = [part] + [swap(part, depth) for depth in DEPTHS[1:]]
        part = (moved[0] + moved[1]) + (moved[2] + moved[3])
        near = exchange([part] * 4)
        far = [swap(value, 2) for value in near]
        sums = pl.pallas_call(
            spread_kernel,
            in_specs=[SMEM] + [VMEM] * 8 + [ANY] * 6,
            out_specs=[ANY] * 6,
            out_shape=[jax.ShapeDtypeStruct(shape, f32) for shape in out_shapes],
            scratch_shapes=[pltpu.VMEM((SUM_ROWS, D), f32), pltpu.SemaphoreType.DMA((KINDS,))],
            input_output_aliases={9 + n: n for n in range(6)},
            name="spread",
        )(meta, *near, *far, *[jnp.zeros(shape, f32) for shape in out_shapes])
        return (output, grad_tokens, *sums)

    slots = (jnp.arange(seq_total) == seq_number).astype(f32)[:, None, None]
    every = lax.psum(slots * terms[None], AXES)

    def spread(first, count, width):
        def term(s):
            rows = every[s, first * RANK : (first + count * (width // D)) * RANK]
            value = rows.reshape(count, width // D, RANK, D).transpose(0, 2, 1, 3).reshape(count, RANK, width)
            return (jnp.arange(ADAPTERS) == adapter_pick[s]).astype(f32)[:, None, None, None] * value[None]

        return functools.reduce(lambda x, y: x + y, [term(s) for s in range(seq_total)])

    wide = FF // D
    sums = [
        spread(0, 4, D),
        spread(4, 4, D),
        spread(8, 1, D),
        spread(9, 1, FF),
        spread(9 + wide, 1, FF),
        spread(9 + 2 * wide, 1, D),
    ]
    return (output, grad_tokens, *[value.reshape(shape) for value, shape in zip(sums, out_shapes, strict=True)])


def solution(mesh):
    rows = P(AXES, None)
    placed = (rows,) * 8 + (P(),) * 11 + (P("seq", None), P())
    return jax.shard_map(
        shards,
        mesh=mesh,
        in_specs=placed,
        out_specs=(rows, rows) + (P(),) * 6,
        check_vma=False,
    )
```

```python
import functools

import jax
import jax.numpy as jnp
from jax import lax
from jax.experimental import pallas as pl
from jax.experimental.pallas import tpu as pltpu
from jax.sharding import PartitionSpec as P

D = 768
HEADS = 12
HDIM = 64
BLOCK = 64
ADAPTERS = 8
RANK = 16
FF = 3072

PEERS = (0, 8, 16, 24)
PLANE = (0, 1, 4, 5)
GROUP_HEADS = HEADS // 4
SHARE = GROUP_HEADS * HDIM
WIDE = 256
LSE_LANE = SHARE
DEL_LANE = SHARE + 9
MASK_LANE = SHARE + 18
FLOOR = -1e30
STACK = GROUP_HEADS * BLOCK
AXES = ("seq", "head")
norm_eps = 1e-12
f32 = jnp.float32
bf16 = jnp.bfloat16
VMEM_LIMIT = 60 * 1024 * 1024


def dense_mul(left_op, right_op):
    return jnp.dot(left_op, right_op, preferred_element_type=f32)


def dense_right_t(left_op, right_op):
    return lax.dot_general(left_op, right_op, (((1,), (1,)), ((), ())), preferred_element_type=f32)


def dense_left_t(left_op, right_op):
    return lax.dot_general(left_op, right_op, (((0,), (0,)), ((), ())), preferred_element_type=f32)


def lanes(rows):
    return lax.broadcasted_iota(jnp.int32, (rows, WIDE), 1)


def head_lanes(lane, head):
    return (lane >= HDIM * head) & (lane < HDIM * (head + 1))


def part_lanes(lane, first, head):
    return (lane >= first + 3 * head) & (lane < first + 3 * head + 3)


def project_rows(raw, u_ref):
    lane = lanes(raw.shape[0])
    data = lane < SHARE

    def part(j):
        piece = raw[:, WIDE * j : WIDE * (j + 1)]
        return (piece + dense_mul(piece[:, WIDE // 2 :].astype(bf16), u_ref[j])).astype(bf16).astype(f32)

    query = jnp.where(data, part(0) * 0.125, jnp.where(lane == MASK_LANE, 1.0, 0.0)).astype(bf16)
    return query, jnp.concatenate([part(1)[:, :SHARE], part(2)[:, :SHARE]], axis=1).astype(bf16)


def widen_pair(pair, position, seq_length):
    lane = lanes(pair.shape[0])
    data = lane < SHARE
    blank = jnp.zeros((pair.shape[0], WIDE - SHARE), bf16)
    key = jnp.concatenate([pair[:, :SHARE], blank], axis=1)
    value = jnp.concatenate([pair[:, SHARE:], blank], axis=1)
    mask = jnp.where(position < seq_length, 0.0, FLOOR)
    key_side = jnp.where(lane < DEL_LANE, 1.0, jnp.where(lane == MASK_LANE, mask, 0.0)).astype(bf16)
    value_side = jnp.where((lane >= DEL_LANE) & (lane < MASK_LANE), 1.0, 0.0).astype(bf16)
    return jnp.where(data, key, key_side), jnp.where(data, value, value_side)


def slab_offset(n, place, fast):
    if not fast:
        return (n & 7) | ((n >> 3) << 5)
    core = (place >> 1) & 1
    near = 4 - 3 * core if n < 4 else 1 + 3 * core
    return (0, near, 5 - near, 5)[n % 4] ^ (2 * (n // 4))


def slab_row(offset):
    return (offset & 7) | ((offset >> 5) << 3)


def plane_quarter(place):
    return (place & 1) | ((place >> 1) & 2)


def rand_at(fast, rand_ref, block, r):
    if not fast:
        return rand_ref[block * 3 + r]
    return rand_ref[(block // 4) * 2, WIDE // 4 + (block & 3) * 3 + r]


def pack_kernel(rand_ref, query_ref, key_ref, value_ref, output_ref, inner_ref, outer_ref, late_ref, *slice_refs):
    slab = query_ref.shape[0]
    group = ((lax.axis_index("seq") * lax.axis_size("head") + lax.axis_index("head")) >> 3) & 3
    late_ref[:, :D] = output_ref[...]
    late_ref[:, D : D + FF] = inner_ref[...]
    outer = outer_ref[...].astype(f32)
    for c in range(FF // D):
        late_ref[:, D + FF + D * c : D + FF + D * (c + 1)] = outer[slab * c : slab * (c + 1)].astype(bf16)
    spare = (slab, WIDE - SHARE)
    lane = lax.broadcasted_iota(jnp.int32, spare, 1)
    marks = jnp.zeros(spare, f32)
    for n in range(12):
        marks = jnp.where(lane == n, rand_ref[n // 3, n % 3].astype(f32), marks)
    marks = jnp.where(lax.broadcasted_iota(jnp.int32, spare, 0) == 0, marks, 0.0)
    sources = [ref[...].astype(f32) for ref in (query_ref, key_ref, value_ref)]
    for p in range(4):
        pieces = []
        for source in sources:
            mine = source[:, :SHARE]
            for g in range(1, 4):
                mine = jnp.where((group ^ p) == g, source[:, SHARE * g : SHARE * (g + 1)], mine)
            pieces += [mine, marks]
        slice_refs[p][...] = jnp.concatenate(pieces, axis=1).astype(bf16)


def put_tokens(fast, token_refs, tok_ref):
    rows = 2 * BLOCK
    if fast:
        own, far, near = token_refs
        parts = [own[...], near[:rows, :], far[...], near[rows:, :]]
    else:
        parts = [ref[...] for ref in token_refs]
    for a in range(4):
        tok_ref[rows * a : rows * (a + 1), :] = parts[a]


def project_kernel(fast, meta_ref, down_ref, up_ref, *refs):
    count = 3 if fast else 4
    tok_refs, refs = refs[:count], refs[count:]
    w_refs, (w_ref, u_ref, q_ref, pair_ref, rand_ref, tok_ref, wide_ref) = refs[:-7], refs[-7:]
    place = meta_ref[0]
    group = meta_ref[2]
    chosen = meta_ref[3]
    half = WIDE // 2
    lead = WIDE // 4
    rand_ref[...] = jnp.zeros_like(rand_ref)
    if fast:
        slab = D // 32
        for n, piece in enumerate(w_refs):
            rows = piece[...].astype(f32)
            for a in range(4):
                device = place ^ slab_offset(n, place, fast) ^ PEERS[a]
                wide_ref[pl.ds(pl.multiple_of(device * slab, 8), slab), :] = rows[slab * a : slab * (a + 1)]
                rand_ref[pl.ds(device, 1), :] = rows[slab * a : slab * a + 1, half:WIDE].astype(jnp.int32)
    else:
        wide_ref[...] = w_refs[0][...].astype(f32)
    own = lax.broadcasted_iota(jnp.int32, (D, half), 1) < lead
    above = jnp.zeros((lead, D), f32)
    below = jnp.zeros((half - lead - RANK, D), f32)
    side = jnp.zeros((RANK, WIDE - SHARE), f32)
    for j in range(3):
        low = slice(WIDE * j, WIDE * j + half)
        high = slice(WIDE * j + half, WIDE * (j + 1))
        turned = jnp.concatenate([above, down_ref[chosen, j].astype(f32), below], axis=0).T
        w_ref[:, low] = wide_ref[:, low].astype(bf16)
        w_ref[:, high] = jnp.where(own, wide_ref[:, high], turned).astype(bf16)
        up = up_ref[chosen, j].astype(f32)
        mine = jnp.zeros((RANK, SHARE), f32)
        for g in range(4):
            mine = mine + jnp.where(group == g, up[:, SHARE * g : SHARE * (g + 1)], 0.0)
        mine = jnp.concatenate([mine, side], axis=1)
        u_ref[j] = jnp.concatenate([above[:, :WIDE], mine, below[:, :WIDE]], axis=0).astype(bf16)
    put_tokens(fast, tok_refs, tok_ref)
    q_ref[...], pair_ref[...] = project_rows(dense_mul(tok_ref[...], w_ref[...]), u_ref)


def block_rows(ref, block, count=1):
    return ref[pl.ds(pl.multiple_of(block * BLOCK, BLOCK), count * BLOCK), :]


def merge_heads(stacked):
    lane = lanes(BLOCK)
    total = jnp.zeros((BLOCK, WIDE), f32)
    for head in range(GROUP_HEADS):
        total = jnp.where(head_lanes(lane, head), stacked[BLOCK * head : BLOCK * (head + 1)], total)
    return total


def key_set(ref, picks, block, block_total, fill):
    own = block_rows(ref, block)
    left = block_rows(ref, jnp.maximum(block - 1, 0))
    right = block_rows(ref, jnp.minimum(block + 1, block_total - 1))
    if fill:
        blank = jnp.where(lanes(BLOCK) == MASK_LANE, FLOOR, 0.0).astype(bf16)
        left = jnp.where(block - 1 >= 2, left, blank)
        right = jnp.where(block + 1 < block_total, right, blank)
    rand = [block_rows(ref, pick) for pick in picks]
    return jnp.concatenate([own, left, right, block_rows(ref, 0, 2)] + rand, axis=0)


def own_block(place, t):
    return 2 * (place ^ PEERS[t // 2]) + t % 2


def attend_kernel(fast, meta_ref, rand_ref, q_ref, *refs):
    slab_refs, (k_ref, v_ref, *ctx_refs, aux_ref, s_ref) = refs[:-8], refs[-8:]
    place = meta_ref[0]
    piece = 2 * BLOCK
    for n, slab_ref in enumerate(slab_refs):
        for a in range(4):
            device = place ^ slab_offset(n, place, fast) ^ PEERS[a]
            here = pl.ds(pl.multiple_of(device * piece, piece), piece)
            position = device * piece + lax.broadcasted_iota(jnp.int32, (piece, WIDE), 0)
            k_ref[here, :], v_ref[here, :] = widen_pair(
                slab_ref[piece * a : piece * (a + 1), :], position, meta_ref[1]
            )
    total_rows = k_ref.shape[0]
    block_total = total_rows // BLOCK
    chunks = total_rows // (8 * BLOCK)

    def queries(t):
        rows = q_ref[pl.ds(t * BLOCK, BLOCK), :]
        lane = lanes(BLOCK)
        blank = jnp.zeros_like(rows)
        return jnp.concatenate(
            [
                jnp.where(head_lanes(lane, head) | (lane == MASK_LANE), rows, blank)
                for head in range(GROUP_HEADS)
            ],
            axis=0,
        )

    def finish(t, low, exact, top, total):
        lane = lanes(BLOCK)
        rows = pl.ds(t * BLOCK, BLOCK)
        ctx_refs[t // 2][pl.ds((t % 2) * BLOCK, BLOCK), :] = merge_heads(low).astype(bf16)
        aux = merge_heads(exact)
        lse = top + jnp.log(total)
        for head in range(GROUP_HEADS):
            aux = jnp.where(lane == LSE_LANE + head, lse[BLOCK * head : BLOCK * (head + 1)], aux)
        aux_ref[rows, :] = aux

    def split(probs):
        low = probs.astype(bf16)
        return low, (probs - low.astype(f32)).astype(bf16)

    def sparse(t):
        block = own_block(place, t)
        picks = [rand_at(fast, rand_ref, block, r) for r in range(3)]
        scores = dense_right_t(queries(t), key_set(k_ref, picks, block, block_total, True))
        top = jnp.max(scores, axis=1, keepdims=True)
        weights = jnp.exp(scores - top)
        total = jnp.sum(weights, axis=1, keepdims=True)
        low, rest = split(weights * (1.0 / total))
        values = key_set(v_ref, picks, block, block_total, False)
        context = dense_mul(low, values)
        return context, context + dense_mul(rest, values), top, total

    for a in range(4):

        @pl.when((place ^ PEERS[a]) != 0)
        def _(a=a):
            results = [sparse(2 * a), sparse(2 * a + 1)]
            finish(2 * a, *results[0])
            finish(2 * a + 1, *results[1])

    at_once = s_ref.shape[1] // STACK

    def full(a, first):
        stack = jnp.concatenate([queries(2 * a + first + n) for n in range(at_once)], axis=0)
        height = at_once * STACK

        def score(c, state):
            top, total, tops = state
            part = dense_right_t(stack, block_rows(k_ref, c * 8, 8))
            here = jnp.max(part, axis=1, keepdims=True)
            weights = jnp.exp(part - here)
            s_ref[c] = weights
            later = jnp.maximum(top, here)
            total = total * jnp.exp(top - later) + jnp.sum(weights, axis=1, keepdims=True) * jnp.exp(here - later)
            return later, total, jnp.where(turn == c, here, tops)

        turn = lax.broadcasted_iota(jnp.int32, (height, 128), 1)
        top, total, tops = lax.fori_loop(
            0,
            chunks,
            score,
            (jnp.full((height, 1), FLOOR, f32), jnp.zeros((height, 1), f32), jnp.full((height, 128), FLOOR, f32)),
        )
        scales = jnp.exp(tops - top) * (1.0 / total)

        def mix(c, state):
            scale = jnp.sum(jnp.where(turn == c, scales, 0.0), axis=1, keepdims=True)
            low, rest = split(s_ref[c] * scale)
            values = block_rows(v_ref, c * 8, 8)
            return (state[0] + dense_mul(low, values), state[1] + dense_mul(rest, values))

        zero = jnp.zeros((height, WIDE), f32)
        context, rest = lax.fori_loop(0, chunks, mix, (zero, zero))
        for n in range(at_once):
            here = slice(STACK * n, STACK * (n + 1))
            finish(2 * a + first + n, context[here], (context + rest)[here], top[here], total[here])

    for a in range(4):

        @pl.when((place ^ PEERS[a]) == 0)
        def _(a=a):
            for first in range(0, 2, at_once):
                full(a, first)


def split_parts(value):
    high = value.astype(bf16).astype(f32)
    middle = (value - high).astype(bf16).astype(f32)
    return (high, middle, value - high - middle)


def delta_kernel(*refs):
    grad_refs, aux_ref, out_ref = refs[:4], refs[4], refs[5]
    rows = 2 * BLOCK
    lane = lanes(rows)
    for a in range(4):
        here = pl.ds(a * rows, rows)
        grad = grad_refs[a][...].astype(f32)
        aux = aux_ref[here, :]
        result = jnp.where(lane < SHARE, grad, 0.0)
        product = grad * aux
        for head in range(GROUP_HEADS):
            delta = jnp.sum(jnp.where(head_lanes(lane, head), product, 0.0), axis=1, keepdims=True)
            lse = jnp.sum(jnp.where(lane == LSE_LANE + head, aux, 0.0), axis=1, keepdims=True)
            for p, value in enumerate(split_parts(lse)):
                result = jnp.where(lane == LSE_LANE + 3 * head + p, -value, result)
            for p, value in enumerate(split_parts(delta)):
                result = jnp.where(lane == DEL_LANE + 3 * head + p, -value, result)
        out_ref[here, :] = result.astype(bf16)


def query_stacks(rows, grads):
    lane = lanes(BLOCK)
    blank = jnp.zeros_like(rows)
    queries = []
    outers = []
    for head in range(GROUP_HEADS):
        here = head_lanes(lane, head)
        queries.append(
            jnp.where(
                here | (lane == MASK_LANE), rows, jnp.where(part_lanes(lane, LSE_LANE, head), grads, blank)
            )
        )
        outers.append(jnp.where(here | part_lanes(lane, DEL_LANE, head), grads, blank))
    return jnp.concatenate(queries, axis=0), jnp.concatenate(outers, axis=0)


def near_kernel(fast, meta_ref, rand_ref, q_ref, k_ref, v_ref, g_ref, dq_ref, *refs):
    zero_outs, (blank_ref, sems) = refs[:-2], refs[-2:]
    place = meta_ref[0]
    block_total = k_ref.shape[0] // BLOCK
    copies = []
    if zero_outs:
        blank_ref[...] = jnp.zeros_like(blank_ref)
        for n, where in enumerate(zero_outs):
            shape = where.shape
            source = blank_ref if len(shape) == 4 else blank_ref.at[0 : shape[2] // D]
            for adapter in range(ADAPTERS):
                if len(shape) == 4:
                    copies.append((blank_ref, where.at[adapter], n))
                else:
                    for c in range(shape[2] // D):
                        copies.append((blank_ref.at[c], where.at[adapter, :, pl.ds(D * c, D)], n))
        copies = [pltpu.make_async_copy(source, where, sems.at[n]) for n, (source, where, _) in enumerate(copies)]
        for copy in copies:
            copy.start()

    def query_side(stack, outer, keys, values):
        probs = jnp.exp(dense_right_t(stack, keys))
        scored = (probs * dense_right_t(outer, values)).astype(bf16)
        return dense_mul(scored, keys)

    def put_query(t, stacked):
        dq_ref[pl.ds(t * BLOCK, BLOCK), :] = (merge_heads(stacked) * 0.125).astype(bf16)

    def stacks(t):
        here = slice(t * BLOCK, (t + 1) * BLOCK)
        return query_stacks(q_ref[here, :], g_ref[here, :])

    def sparse(t):
        block = own_block(place, t)
        picks = [rand_at(fast, rand_ref, block, r) for r in range(3)]
        return query_side(
            *stacks(t),
            key_set(k_ref, picks, block, block_total, True),
            key_set(v_ref, picks, block, block_total, False),
        )

    for a in range(4):

        @pl.when((place ^ PEERS[a]) != 0)
        def _(a=a):
            results = [sparse(2 * a), sparse(2 * a + 1)]
            put_query(2 * a, results[0])
            put_query(2 * a + 1, results[1])

        @pl.when((place ^ PEERS[a]) == 0)
        def _(a=a):
            pairs = [stacks(2 * a), stacks(2 * a + 1)]
            stack = jnp.concatenate([pair[0] for pair in pairs], axis=0)
            outer = jnp.concatenate([pair[1] for pair in pairs], axis=0)

            def add(c, total):
                return total + query_side(stack, outer, block_rows(k_ref, c * 8, 8), block_rows(v_ref, c * 8, 8))

            total = lax.fori_loop(0, block_total // 8, add, jnp.zeros((2 * STACK, WIDE), f32))
            put_query(2 * a, total[:STACK])
            put_query(2 * a + 1, total[STACK:])

    for copy in copies:
        copy.wait()


def far_kernel(fast, meta_ref, rand_ref, k_ref, v_ref, dq_ref, w_ref, u_ref, early_ref, *refs):
    count = 3 if fast else 4
    tok_refs, refs = refs[:count], refs[count:]
    slab_refs, refs = refs[:-14], refs[-14:]
    part_refs, near_ref, away_ref, refs = refs[:4], refs[4], refs[5], refs[6:]
    q_ref, g_ref, dk_ref, dv_ref, grad_ref, tok_ref, terms_ref, pair_ref = refs
    place = meta_ref[0]
    group = meta_ref[2]
    block_total = k_ref.shape[0] // BLOCK
    count = len(slab_refs) // 2
    rows = 2 * BLOCK
    for n in range(count):
        here = pl.ds(pl.multiple_of(slab_row(slab_offset(n, place, fast)) * 4 * rows, rows), 4 * rows)
        q_ref[here, :] = slab_refs[n][...]
        g_ref[here, :] = slab_refs[count + n][...]

    def stacks(blocks):
        pairs = []
        for block in blocks:
            other = (block // 2) ^ place
            where = slab_row(other) * 8 + ((other >> 3) & 3) * 2 + (block & 1)
            pairs.append(query_stacks(block_rows(q_ref, where), block_rows(g_ref, where)))
        return (
            jnp.concatenate([pair[0] for pair in pairs], axis=0),
            jnp.concatenate([pair[1] for pair in pairs], axis=0),
        )

    def key_side(keys, values, blocks, allowed):
        stack, outer = stacks(blocks)
        probs = jnp.exp(dense_right_t(keys, stack))
        if allowed is not None:
            probs = jnp.where(allowed, probs, 0.0)
        scored = (probs * dense_right_t(values, outer)).astype(bf16)
        return dense_mul(scored, stack), dense_mul(probs.astype(bf16), outer)

    def put(here, grads):
        dk_ref[here, :] += grads[0]
        dv_ref[here, :] += grads[1]

    key_local = lax.broadcasted_iota(jnp.int32, (rows, 6 * STACK), 0) // BLOCK
    turn = lax.broadcasted_iota(jnp.int32, (rows, 6 * STACK), 1) // STACK
    for a in range(4):
        first = 2 * (place ^ PEERS[a])
        here = slice(rows * a, rows * (a + 1))
        blocks = [0, 1, jnp.maximum(first - 1, 0), first, first + 1, jnp.minimum(first + 2, block_total - 1)]
        key_block = first + key_local
        block = first - 3 + turn
        near = (key_block - block <= 1) & (block - key_block <= 1) & (block >= 2) & (block < block_total)
        allowed = ((turn < 2) | near) & (key_block >= 2)
        keys = block_rows(k_ref, first, 2)
        values = block_rows(v_ref, first, 2)
        dk_ref[here, :], dv_ref[here, :] = key_side(keys, values, blocks, allowed)

    def collect(block, count):
        for r in range(3):
            target = rand_at(fast, rand_ref, block, r)
            mine = (((target // 2) ^ place) & ~24) == 0

            @pl.when(mine)
            def _(target=target, count=count):
                pair_ref[count] = target * 65536 + block

            count = count + mine.astype(jnp.int32)
        return count

    pair_total = lax.fori_loop(2, block_total, collect, jnp.int32(0))

    def random_pairs(step, carry):
        grads = []
        for k in range(4):
            number = 4 * step + k
            live = number < pair_total
            code = pair_ref[jnp.minimum(number, pair_total - 1)]
            target = code // 65536
            block = code - target * 65536
            start = ((((target // 2) ^ place) >> 3) & 3) * rows + (target & 1) * BLOCK
            grads.append(
                (
                    pl.ds(pl.multiple_of(start, BLOCK), BLOCK),
                    key_side(block_rows(k_ref, target), block_rows(v_ref, target), (block,), live),
                )
            )
        for here, parts in grads:
            put(here, parts)
        return carry

    lax.fori_loop(0, (pair_total + 3) // 4, random_pairs, 0)

    @pl.when((place & ~24) == 0)
    def _():
        here = pl.ds(pl.multiple_of(group * rows, rows), rows)
        keys = block_rows(k_ref, 0, 2)
        values = block_rows(v_ref, 0, 2)

        def every(step, carry):
            put(here, key_side(keys, values, [4 * step + k for k in range(4)], None))
            return carry

        lax.fori_loop(0, block_total // 4, every, 0)

    data = lanes(rows) < SHARE
    for a in range(4):
        here = slice(rows * a, rows * (a + 1))
        grad_ref[here, :WIDE] = dq_ref[here, :]
        grad_ref[here, WIDE : 2 * WIDE] = jnp.where(data, dk_ref[here, :], 0.0).astype(bf16)
        grad_ref[here, 2 * WIDE :] = jnp.where(data, dv_ref[here, :], 0.0).astype(bf16)
    put_tokens(fast, tok_refs, tok_ref)
    tokens = tok_ref[...]
    lead = WIDE // 4
    terms = []
    ups = []
    for j in range(3):
        high = slice(WIDE * j + WIDE // 2, WIDE * (j + 1))
        grad = grad_ref[:, WIDE * j : WIDE * (j + 1)]
        reduced = dense_mul(tokens, w_ref[:, high]).astype(bf16)
        grad_reduced = dense_right_t(grad, u_ref[j]).astype(bf16)
        terms.append(dense_left_t(grad_reduced, tokens)[lead : lead + RANK])
        up = dense_left_t(reduced, grad)[lead : lead + RANK, :SHARE]
        ups.append(jnp.concatenate([jnp.where(group == g, up, 0.0) for g in range(4)], axis=1))
        grad_ref[:, high] = grad_ref[:, high] + grad_reduced
    terms += ups + [jnp.zeros((RANK, D), f32)] * 2
    core = (place >> 1) & 1
    quarter = plane_quarter(place)
    for part, value in enumerate(terms):
        early = early_ref[EARLY_PART * part : EARLY_PART * (part + 1), :]
        where = (((part // 4) ^ core) * 4 + ((part % 4) ^ quarter)) if fast else part
        terms_ref[where, :RANK] = value
        terms_ref[where, RANK:] = early
    near_ref[...] = terms_ref[:4]
    away_ref[...] = terms_ref[4:].astype(away_ref.dtype)
    for a in range(4):
        part_refs[a][...] = dense_right_t(grad_ref[rows * a : rows * (a + 1), :], w_ref[...]).astype(bf16)


def normal(hidden):
    center = hidden - jnp.mean(hidden, axis=-1, keepdims=True)
    root = lax.rsqrt(jnp.mean(center * center, axis=-1, keepdims=True) + norm_eps)
    return center * root, root


def normal_back(grad, normed, root):
    mean = jnp.mean(grad, axis=-1, keepdims=True)
    return root * (grad - mean - normed * jnp.mean(grad * normed, axis=-1, keepdims=True))


def middle_kernel(
    fast,
    meta_ref,
    ctx_refs,
    tok_ref,
    cot_ref,
    late_hbm,
    gain_ref,
    down_table,
    up_table,
    inner_down_table,
    inner_up_table,
    outer_down_table,
    outer_up_table,
    wide_ref,
    out_ref,
    grad_ref,
    piece_refs,
    terms_ref,
    hold_ref,
    pre_ref,
    act_ref,
    late_ref,
    sems,
):
    group = meta_ref[2]
    chosen = meta_ref[3]
    rows = tok_ref.shape[0]
    down_ref = down_table.at[chosen, 3]
    up_ref = up_table.at[chosen, 3]
    inner_down_ref = inner_down_table.at[chosen]
    inner_up_ref = inner_up_table.at[chosen]
    outer_down_ref = outer_down_table.at[chosen]
    outer_up_ref = outer_up_table.at[chosen]
    share = D // (FF // D)
    places = [(slice(None), slice(D * c, D * (c + 1))) for c in range(1 + FF // D)]
    if fast:
        places += [(slice(share * c, share * (c + 1)), slice(D + FF, D + 2 * FF)) for c in range(FF // D)]
    copies = [
        pltpu.make_async_copy(late_hbm.at[place], late_ref.at[place], sems.at[n]) for n, place in enumerate(places)
    ]
    order = [0] + [n for c in range(FF // D) for n in (1 + c, 1 + FF // D + c) if n < len(copies)]
    for n in order:
        copies[n].start()

    def build(c):
        copies[1 + FF // D + c].wait()
        slab = 24
        for pair in range(share // (2 * slab)):
            first = share * c + 2 * slab * pair
            block = late_ref[first : first + 2 * slab, D + FF :].astype(f32)
            cut = [
                block[slab * side : slab * (side + 1), D * n : D * (n + 1)]
                for side in range(2)
                for n in range(FF // D)
            ]
            wide_ref[4 * first : 4 * first + 8 * slab, :] = jnp.concatenate(cut, axis=0).astype(bf16)

    for a in range(4):
        hold_ref[a] = ctx_refs[a][...]
    context = jnp.concatenate([hold_ref[group ^ g][:, :SHARE] for g in range(4)], axis=1)
    context_red = dense_right_t(context, down_ref[...]).astype(bf16)
    copies[0].wait()
    attended = dense_mul(context, late_ref[:, :D]) + dense_mul(context_red, up_ref[...])
    first, first_root = normal(tok_ref[...].astype(f32) + attended)
    first_norm = first * gain_ref[0:1, :] + gain_ref[1:2, :]
    first_low = first_norm.astype(bf16)
    inner_red = dense_right_t(first_low, inner_down_ref[...]).astype(bf16)
    outer_red = jnp.zeros((rows, RANK), f32)
    outer_out = jnp.zeros((rows, D), f32)
    for c in range(FF // D):
        here = slice(D * c, D * (c + 1))
        copies[1 + c].wait()
        if fast:
            build(c)
        pre = dense_mul(first_low, late_ref[:, D * (c + 1) : D * (c + 2)]) + dense_mul(
            inner_red, inner_up_ref[:, here]
        )
        pre_ref[:, here] = pre
        active = (0.5 * pre * (1.0 + lax.erf(pre * 0.7071067811865476))).astype(bf16)
        act_ref[:, here] = active
        outer_red = outer_red + dense_right_t(active, outer_down_ref[:, here])
        outer_out = outer_out + dense_mul(active, wide_ref[here, :])
    outer_red = outer_red.astype(bf16)
    outer_out = outer_out + dense_mul(outer_red, outer_up_ref[...])
    second, second_root = normal(first_norm + outer_out)
    position = meta_ref[0] * rows + lax.broadcasted_iota(jnp.int32, (rows, D), 0)
    valid = (position < meta_ref[1]).astype(f32)
    out_ref[...] = ((second * gain_ref[2:3, :] + gain_ref[3:4, :]) * valid).astype(bf16)
    grad_second = normal_back(valid * cot_ref[...].astype(f32) * gain_ref[2:3, :], second, second_root)
    grad_outer = grad_second.astype(bf16)
    first_up = RANK * 3
    first_down = RANK * (3 + FF // D)
    terms_ref[first_down + RANK * (FF // D) :, :] = dense_left_t(outer_red, grad_outer)
    outer_grad_red = dense_right_t(grad_outer, outer_up_ref[...]).astype(bf16)
    inner_grad_red = jnp.zeros((rows, RANK), f32)
    grad_first = grad_second
    for c in range(FF // D):
        here = slice(D * c, D * (c + 1))
        grad_active = dense_right_t(grad_outer, wide_ref[here, :]) + dense_mul(
            outer_grad_red, outer_down_ref[:, here]
        )
        pre = pre_ref[:, here]
        slope = 0.5 * (1.0 + lax.erf(pre * 0.7071067811865476)) + pre * (
            0.3989422804014327 * jnp.exp(-0.5 * pre * pre)
        )
        grad_inner = (slope * grad_active).astype(bf16)
        terms_ref[first_up + RANK * c : first_up + RANK * (c + 1), :] = dense_left_t(inner_red, grad_inner)
        terms_ref[first_down + RANK * c : first_down + RANK * (c + 1), :] = dense_left_t(
            outer_grad_red, act_ref[:, here]
        )
        inner_grad_red = inner_grad_red + dense_right_t(grad_inner, inner_up_ref[:, here])
        grad_first = grad_first + dense_right_t(grad_inner, late_ref[:, D * (c + 1) : D * (c + 2)])
    inner_grad_red = inner_grad_red.astype(bf16)
    terms_ref[2 * RANK : 3 * RANK, :] = dense_left_t(inner_grad_red, first_low)
    grad_first = grad_first + dense_mul(inner_grad_red, inner_down_ref[...])
    grad_attended = normal_back(grad_first * gain_ref[0:1, :], first, first_root)
    grad_ref[...] = grad_attended
    grad_low = grad_attended.astype(bf16)
    context_grad_red = dense_right_t(grad_low, up_ref[...]).astype(bf16)
    terms_ref[:RANK, :] = dense_left_t(context_grad_red, context)
    terms_ref[RANK : 2 * RANK, :] = dense_left_t(context_red, grad_low)
    grad_context = (
        dense_right_t(grad_low, late_ref[:, :D]) + dense_mul(context_grad_red, down_ref[...])
    ).astype(bf16)
    blank = jnp.zeros((rows, WIDE - SHARE), bf16)
    for g in range(4):
        hold_ref[group ^ g] = jnp.concatenate([grad_context[:, SHARE * g : SHARE * (g + 1)], blank], axis=1)
    for a in range(4):
        piece_refs[a][...] = hold_ref[a]


def spread_kernel(meta_ref, *refs):
    part_refs = refs[:8]
    outs = refs[14:20]
    sum_ref, sems = refs[20:]
    quarter = plane_quarter(meta_ref[0])
    core = (meta_ref[0] >> 1) & 1
    chosen = meta_ref[3]
    for n in range(8):
        part = (core ^ (n // 4)) * 4 + (quarter ^ (n % 4))
        sum_ref[pl.ds(pl.multiple_of(part * RANK, RANK), RANK), :] = part_refs[n][:RANK, :].astype(f32)
        sum_ref[pl.ds(pl.multiple_of(LATE_ROWS + part * EARLY_PART, 8), EARLY_PART), :] = part_refs[n][RANK:, :].astype(f32)
    places = [outs[0].at[chosen, j] for j in range(3)] + [outs[1].at[chosen, j] for j in range(3)]
    places += [None, None, outs[0].at[chosen, 3], outs[1].at[chosen, 3], outs[2].at[chosen]]
    places += [outs[n].at[chosen, :, pl.ds(D * c, D)] for n in (3, 4) for c in range(FF // D)]
    places.append(outs[5].at[chosen])
    copies = [
        pltpu.make_async_copy(sum_ref.at[pl.ds(RANK * n, RANK), :], where, sems.at[n])
        for n, where in enumerate(places)
        if where is not None
    ]
    for copy in copies:
        copy.start()
    for copy in copies:
        copy.wait()


LATE_ROWS = 8 * RANK
EARLY_KINDS = 12
EARLY_PART = EARLY_KINDS * RANK // 8
ANY = pl.BlockSpec(memory_space=pl.ANY)
SMEM = pl.BlockSpec(memory_space=pltpu.SMEM)
VMEM = pl.BlockSpec(memory_space=pltpu.VMEM)


def shards(
    tokens,
    cotangent,
    w_query,
    w_key,
    w_value,
    w_output,
    w_inner,
    w_outer,
    gain_first,
    shift_first,
    gain_second,
    shift_second,
    attn_down,
    attn_up,
    inner_down,
    inner_up,
    outer_down,
    outer_up,
    lengths,
    rand_blocks,
    adapter_pick,
):
    device_total = lax.axis_size("seq") * lax.axis_size("head")
    local_rows = tokens.shape[0]
    seq_total = lengths.shape[0]
    members = device_total // seq_total
    rows_total = members * local_rows
    block_total = rows_total // BLOCK
    chunk = 4 * local_rows
    index = lax.axis_index("seq") * lax.axis_size("head") + lax.axis_index("head")
    place = index % members
    seq_number = index // members
    group = (place >> 3) & 3
    seq_length = lengths[seq_number]
    chosen = adapter_pick[seq_number]
    fast = device_total == 32 and members == 32
    together = lax.optimization_barrier

    def send(value, even, odd):
        return lax.ppermute(
            value, AXES, [(j, j ^ (odd if (j >> 1) & 1 else even)) for j in range(device_total)]
        )

    def swap(value, mask):
        return send(value, mask, mask)

    def one(value):
        return send(value, 4, 1)

    def two(value):
        return send(value, 1, 4)

    def exchange(pieces, masks=PEERS):
        return [pieces[0]] + [swap(pieces[a], masks[a]) for a in range(1, 4)]

    def gather_start(value):
        if not fast:
            masks = [slab_offset(n, place, False) for n in range(members // 4)]
            return [value] + [swap(value, mask) for mask in masks[1:]]
        return [value, one(value), two(value)]

    def gather_end(slabs):
        if not fast:
            return slabs
        slabs = slabs + [two(slabs[1])]
        return slabs + [swap(slab, 2) for slab in slabs]

    def gather_group(value):
        return gather_end(gather_start(value))

    def gather_all(value):
        return lax.all_gather(value, AXES, axis=0, tiled=True)

    def share_columns(table, which=group):
        return lax.dynamic_slice_in_dim(table, which * SHARE, SHARE, table.ndim - 1)

    slab = D // device_total
    meta = jnp.stack([place, seq_length, group, chosen]).astype(jnp.int32)
    if fast:
        late_local, *slices = pl.pallas_call(
            pack_kernel,
            in_specs=[SMEM] + [VMEM] * 6,
            out_specs=[VMEM] * 5,
            out_shape=[jax.ShapeDtypeStruct((slab, D + 2 * FF), bf16)]
            + [jax.ShapeDtypeStruct((slab, 3 * WIDE), bf16)] * 4,
            name="pack",
        )(rand_blocks, w_query, w_key, w_value, w_output, w_inner, w_outer)
        late = gather_all(late_local)
        mine = exchange(slices)
        far_tokens = swap(tokens, PEERS[2])
        near_tokens = swap(jnp.concatenate([tokens, far_tokens], axis=0), PEERS[1])
        token_refs = [tokens, far_tokens, near_tokens]
        w_slabs = gather_group(jnp.concatenate(mine, axis=0))
    else:
        late = gather_all(
            jnp.concatenate([w_output, w_inner] + [w_outer[slab * c : slab * (c + 1)] for c in range(FF // D)], axis=1)
        )
        full_qkv = gather_all(jnp.concatenate([w_query, w_key, w_value], axis=1))
        rand_all = lax.all_gather(rand_blocks, "seq", axis=0, tiled=True)
        rand_flat = lax.dynamic_slice_in_dim(rand_all, seq_number * block_total, block_total, 0).reshape(-1)
        token_refs = exchange([tokens] * 4)
        w_slabs = [
            jnp.concatenate(
                [
                    jnp.pad(share_columns(full_qkv[:, D * j : D * (j + 1)]), ((0, 0), (0, WIDE - SHARE)))
                    for j in range(3)
                ],
                axis=1,
            )
        ]

    wide_rows = jax.ShapeDtypeStruct((rows_total, WIDE), bf16)
    piece_shapes = [jax.ShapeDtypeStruct((local_rows, WIDE), bf16)] * 4
    side_weight, side_up, query_own, pair_own, rand_table = pl.pallas_call(
        functools.partial(project_kernel, fast),
        in_specs=[SMEM] + [VMEM] * (2 + len(token_refs) + len(w_slabs)),
        out_specs=[VMEM] * 5,
        out_shape=[
            jax.ShapeDtypeStruct((D, 3 * WIDE), bf16),
            jax.ShapeDtypeStruct((3, WIDE // 2, WIDE), bf16),
            jax.ShapeDtypeStruct((chunk, WIDE), bf16),
            jax.ShapeDtypeStruct((chunk, 2 * SHARE), bf16),
            jax.ShapeDtypeStruct((32, WIDE // 2), jnp.int32),
        ],
        scratch_shapes=[pltpu.VMEM((chunk, D), bf16), pltpu.VMEM((D, 3 * WIDE), f32)],
        compiler_params=pltpu.CompilerParams(vmem_limit_bytes=VMEM_LIMIT),
        name="project",
    )(meta, attn_down, attn_up, *token_refs, *w_slabs)
    if fast:
        rand_flat = rand_table
    pair_slabs = gather_group(pair_own)
    key_all, value_all, *ctx, aux = pl.pallas_call(
        functools.partial(attend_kernel, fast),
        in_specs=[SMEM, SMEM] + [VMEM] * (1 + len(pair_slabs)),
        out_specs=[VMEM] * 7,
        out_shape=[wide_rows] * 2 + piece_shapes + [jax.ShapeDtypeStruct((chunk, WIDE), f32)],
        scratch_shapes=[pltpu.VMEM((rows_total // chunk, (2 if fast else 1) * STACK, chunk), f32)],
        compiler_params=pltpu.CompilerParams(vmem_limit_bytes=VMEM_LIMIT),
        name="attend",
    )(meta, rand_flat, query_own, *pair_slabs)
    ctx_pieces = exchange(ctx)
    query_send, ctx_pieces[1] = together((query_own, ctx_pieces[1]))
    query_slabs = gather_group(query_send)

    gains = jnp.stack([gain_first, shift_first, gain_second, shift_second])
    middle_in = [tokens, cotangent, late, gains, attn_down, attn_up, inner_down, inner_up, outer_down, outer_up]
    wide_shape = [pltpu.VMEM((FF, D), bf16)]
    if not fast:
        middle_in.append(
            late[:, D + FF :].reshape(device_total, slab, FF // D, D).transpose(0, 2, 1, 3).reshape(FF, D)
        )
        wide_shape = []
    count = len(middle_in)

    def middle(meta_ref, *refs):
        ins, outs, scratch = refs[4 : 4 + count], refs[4 + count : 11 + count], refs[11 + count :]
        wide_ref = scratch[-1] if fast else ins[-1]
        middle_kernel(
            fast, meta_ref, refs[:4], *ins[:10], wide_ref, *outs[:2], outs[2:6], outs[6], *scratch[:5]
        )


    output, grad_attended, *grad_pieces, early_terms = pl.pallas_call(
        middle,
        in_specs=[SMEM] + [VMEM] * 6 + [ANY] + [VMEM] * (count - 3),
        out_specs=[VMEM] * 7,
        out_shape=[
            jax.ShapeDtypeStruct((local_rows, D), bf16),
            jax.ShapeDtypeStruct((local_rows, D), f32),
        ]
        + piece_shapes
        + [jax.ShapeDtypeStruct((EARLY_KINDS * RANK, D), f32)],
        scratch_shapes=[
            pltpu.VMEM((4, local_rows, WIDE), bf16),
            pltpu.VMEM((local_rows, FF), f32),
            pltpu.VMEM((local_rows, FF), bf16),
            pltpu.VMEM(late.shape, bf16),
            pltpu.SemaphoreType.DMA((1 + 2 * (FF // D),)),
        ]
        + wide_shape,
        compiler_params=pltpu.CompilerParams(vmem_limit_bytes=VMEM_LIMIT),
        name="middle",
    )(meta, *ctx_pieces, *middle_in)
    grad_wide = pl.pallas_call(
        delta_kernel,
        in_specs=[VMEM] * 5,
        out_specs=VMEM,
        out_shape=jax.ShapeDtypeStruct((chunk, WIDE), bf16),
        name="delta",
    )(*exchange(grad_pieces), aux)
    def reduced(terms):
        paired = terms[0] + swap(terms[1], 2)
        moved = exchange([paired[a] for a in range(4)])
        part = (moved[0] + moved[1]) + (moved[2] + moved[3])
        moved = [part] + [swap(part, depth) for depth in DEPTHS[1:]]
        return (moved[0] + moved[1]) + (moved[2] + moved[3])

    grad_slabs = gather_start(grad_wide)
    out_shapes = [
        jax.ShapeDtypeStruct(shape, f32)
        for shape in (
            (ADAPTERS, 4, RANK, D),
            (ADAPTERS, 4, RANK, D),
            (ADAPTERS, RANK, D),
            (ADAPTERS, RANK, FF),
            (ADAPTERS, RANK, FF),
            (ADAPTERS, RANK, D),
        )
    ]
    zero_shapes = out_shapes if fast else []
    query_grad, *zeros = pl.pallas_call(
        functools.partial(near_kernel, fast),
        in_specs=[SMEM, SMEM] + [VMEM] * 4,
        out_specs=[VMEM] + [ANY] * len(zero_shapes),
        out_shape=[jax.ShapeDtypeStruct((chunk, WIDE), bf16)] + zero_shapes,
        scratch_shapes=[pltpu.VMEM((4, RANK, D), f32), pltpu.SemaphoreType.DMA((ADAPTERS * 12,))],
        compiler_params=pltpu.CompilerParams(vmem_limit_bytes=VMEM_LIMIT),
        cost_estimate=pl.CostEstimate(flops=4000000000, bytes_accessed=8000000, transcendentals=1000000),
        name="near",
    )(meta, rand_flat, query_own, key_all, value_all, grad_wide)
    query_grad, *grad_slabs = together((query_grad, *grad_slabs))
    grad_slabs = gather_end(grad_slabs)
    *parts, near_terms, away_terms = pl.pallas_call(
        functools.partial(far_kernel, fast),
        in_specs=[SMEM, SMEM] + [VMEM] * (6 + len(token_refs) + 2 * len(grad_slabs)),
        out_specs=[VMEM] * 6,
        out_shape=[jax.ShapeDtypeStruct((local_rows, D), bf16)] * 4
        + [jax.ShapeDtypeStruct((4, RANK + EARLY_PART, D), kind) for kind in (f32, bf16 if fast else f32)],
        scratch_shapes=[
            pltpu.VMEM((rows_total, WIDE), bf16),
            pltpu.VMEM((rows_total, WIDE), bf16),
            pltpu.VMEM((chunk, WIDE), f32),
            pltpu.VMEM((chunk, WIDE), f32),
            pltpu.VMEM((chunk, 3 * WIDE), bf16),
            pltpu.VMEM((chunk, D), bf16),
            pltpu.VMEM((8, RANK + EARLY_PART, D), f32),
            pltpu.SMEM((3 * block_total + 8,), jnp.int32),
        ],
        compiler_params=pltpu.CompilerParams(vmem_limit_bytes=VMEM_LIMIT),
        name="far",
    )(
        meta,
        rand_flat,
        key_all,
        value_all,
        query_grad,
        side_weight,
        side_up,
        early_terms,
        *token_refs,
        *query_slabs,
        *grad_slabs,
    )
    def token_sum(pieces):
        pieces = [piece.astype(f32) for piece in pieces]
        return grad_attended + ((pieces[0] + pieces[1]) + (pieces[2] + pieces[3]))

    arrived = [parts[0], swap(parts[1], PEERS[1])]
    if fast:
        paired = near_terms + swap(away_terms, 2).astype(f32)
        moved = [paired[0]] + [swap(paired[a].astype(bf16), PLANE[a]).astype(f32) for a in range(1, 4)]
        part = ((moved[0] + moved[1]) + (moved[2] + moved[3])).astype(bf16)
        moved = [piece.astype(f32) for piece in exchange([part] * 4)]
        part = ((moved[0] + moved[1]) + (moved[2] + moved[3])).astype(bf16)
        part, parts[2], parts[3] = together((part, parts[2], parts[3]))
    arrived += [swap(parts[a], PEERS[a]) for a in (2, 3)]
    if fast:
        part_list = exchange([part] * 4, PLANE)
        part_list = part_list + [swap(value, 2) for value in part_list]
        sums = pl.pallas_call(
            spread_kernel,
            in_specs=[SMEM] + [VMEM] * 8 + [ANY] * 6,
            out_specs=[ANY] * 6,
            out_shape=out_shapes,
            scratch_shapes=[
                pltpu.VMEM((LATE_ROWS + EARLY_KINDS * RANK, D), f32),
                pltpu.SemaphoreType.DMA((8 + EARLY_KINDS,)),
            ],
            input_output_aliases={9 + n: n for n in range(6)},
            name="spread",
        )(meta, *part_list, *zeros)
        return (output, token_sum(arrived), *sums)

    terms = jnp.concatenate([near_terms, away_terms], axis=0)
    terms = jnp.concatenate([terms[:, :RANK].reshape(-1, D), terms[:, RANK:].reshape(-1, D)], axis=0)
    slots = (jnp.arange(seq_total) == seq_number).astype(f32)[:, None, None]
    every = lax.psum(slots * terms[None], AXES)

    def spread(kinds, width):
        def term(s):
            rows = jnp.concatenate([every[s, kind * RANK : (kind + width // D) * RANK] for kind in kinds], axis=0)
            value = rows.reshape(len(kinds), width // D, RANK, D).transpose(0, 2, 1, 3)
            value = value.reshape(len(kinds), RANK, width)
            return (jnp.arange(ADAPTERS) == adapter_pick[s]).astype(f32)[:, None, None, None] * value[None]

        return functools.reduce(lambda x, y: x + y, [term(s) for s in range(seq_total)])

    wide = FF // D
    sums = [
        spread((0, 1, 2, 8), D),
        spread((3, 4, 5, 9), D),
        spread((10,), D),
        spread((11,), FF),
        spread((11 + wide,), FF),
        spread((11 + 2 * wide,), D),
    ]
    return (
        output,
        token_sum(arrived),
        *[value.reshape(leaf.shape) for value, leaf in zip(sums, out_shapes, strict=True)],
    )


def solution(mesh):
    rows = P(AXES, None)
    placed = (rows,) * 8 + (P(),) * 11 + (P("seq", None), P())
    return jax.shard_map(
        shards,
        mesh=mesh,
        in_specs=placed,
        out_specs=(rows, rows) + (P(),) * 6,
        check_vma=False,
    )
```

```python
import functools

import jax
import jax.numpy as jnp
from jax import lax
from jax.experimental import pallas as pl
from jax.experimental.pallas import tpu as pltpu
from jax.sharding import PartitionSpec as P

D = 768
HEADS = 12
HDIM = 64
BLOCK = 64
ADAPTERS = 8
RANK = 16
FF = 3072

PEERS = (0, 8, 16, 24)
PLANE = (0, 1, 4, 5)
GROUP_HEADS = HEADS // 4
SHARE = GROUP_HEADS * HDIM
WIDE = 256
LSE_LANE = SHARE
DEL_LANE = SHARE + 9
MASK_LANE = SHARE + 18
FLOOR = -1e30
STACK = GROUP_HEADS * BLOCK
AXES = ("seq", "head")
norm_eps = 1e-12
f32 = jnp.float32
bf16 = jnp.bfloat16
VMEM_LIMIT = 60 * 1024 * 1024


def dense_mul(left_op, right_op):
    return jnp.dot(left_op, right_op, preferred_element_type=f32)


def dense_right_t(left_op, right_op):
    return lax.dot_general(left_op, right_op, (((1,), (1,)), ((), ())), preferred_element_type=f32)


def dense_left_t(left_op, right_op):
    return lax.dot_general(left_op, right_op, (((0,), (0,)), ((), ())), preferred_element_type=f32)


def lanes(rows):
    return lax.broadcasted_iota(jnp.int32, (rows, WIDE), 1)


def head_lanes(lane, head):
    return (lane >= HDIM * head) & (lane < HDIM * (head + 1))


def part_lanes(lane, first, head):
    return (lane >= first + 3 * head) & (lane < first + 3 * head + 3)


def project_rows(raw, u_ref):
    lane = lanes(raw.shape[0])
    data = lane < SHARE

    def part(j):
        piece = raw[:, WIDE * j : WIDE * (j + 1)]
        return (piece + dense_mul(piece[:, WIDE // 2 :].astype(bf16), u_ref[j])).astype(bf16).astype(f32)

    query = jnp.where(data, part(0) * 0.125, jnp.where(lane == MASK_LANE, 1.0, 0.0)).astype(bf16)
    return query, jnp.concatenate([part(1)[:, :SHARE], part(2)[:, :SHARE]], axis=1).astype(bf16)


def widen_pair(pair, position, seq_length):
    lane = lanes(pair.shape[0])
    data = lane < SHARE
    blank = jnp.zeros((pair.shape[0], WIDE - SHARE), bf16)
    key = jnp.concatenate([pair[:, :SHARE], blank], axis=1)
    value = jnp.concatenate([pair[:, SHARE:], blank], axis=1)
    mask = jnp.where(position < seq_length, 0.0, FLOOR)
    key_side = jnp.where(lane < DEL_LANE, 1.0, jnp.where(lane == MASK_LANE, mask, 0.0)).astype(bf16)
    value_side = jnp.where((lane >= DEL_LANE) & (lane < MASK_LANE), 1.0, 0.0).astype(bf16)
    return jnp.where(data, key, key_side), jnp.where(data, value, value_side)


def slab_offset(n, place, fast):
    if not fast:
        return (n & 7) | ((n >> 3) << 5)
    core = (place >> 1) & 1
    near = 4 - 3 * core if n < 4 else 1 + 3 * core
    return (0, near, 5 - near, 5)[n % 4] ^ (2 * (n // 4))


def slab_row(offset):
    return (offset & 7) | ((offset >> 5) << 3)


def plane_quarter(place):
    return (place & 1) | ((place >> 1) & 2)


def rand_at(fast, rand_ref, block, r):
    if not fast:
        return rand_ref[block * 3 + r]
    return rand_ref[(block // 4) * 2, WIDE // 4 + (block & 3) * 3 + r]


def pack_kernel(rand_ref, query_ref, key_ref, value_ref, output_ref, inner_ref, outer_ref, late_ref, *slice_refs):
    slab = query_ref.shape[0]
    group = ((lax.axis_index("seq") * lax.axis_size("head") + lax.axis_index("head")) >> 3) & 3
    late_ref[:, :D] = output_ref[...]
    late_ref[:, D : D + FF] = inner_ref[...]
    outer = outer_ref[...].astype(f32)
    for c in range(FF // D):
        late_ref[:, D + FF + D * c : D + FF + D * (c + 1)] = outer[slab * c : slab * (c + 1)].astype(bf16)
    spare = (slab, WIDE - SHARE)
    lane = lax.broadcasted_iota(jnp.int32, spare, 1)
    marks = jnp.zeros(spare, f32)
    for n in range(12):
        marks = jnp.where(lane == n, rand_ref[n // 3, n % 3].astype(f32), marks)
    marks = jnp.where(lax.broadcasted_iota(jnp.int32, spare, 0) == 0, marks, 0.0)
    sources = [ref[...].astype(f32) for ref in (query_ref, key_ref, value_ref)]
    for p in range(4):
        pieces = []
        for source in sources:
            mine = source[:, :SHARE]
            for g in range(1, 4):
                mine = jnp.where((group ^ p) == g, source[:, SHARE * g : SHARE * (g + 1)], mine)
            pieces += [mine, marks]
        slice_refs[p][...] = jnp.concatenate(pieces, axis=1).astype(bf16)


def put_tokens(fast, token_refs, tok_ref):
    rows = 2 * BLOCK
    if fast:
        own, far, near = token_refs
        parts = [own[...], near[:rows, :], far[...], near[rows:, :]]
    else:
        parts = [ref[...] for ref in token_refs]
    for a in range(4):
        tok_ref[rows * a : rows * (a + 1), :] = parts[a]


def project_kernel(fast, meta_ref, down_ref, up_ref, *refs):
    count = 3 if fast else 4
    tok_refs, refs = refs[:count], refs[count:]
    w_refs, (w_ref, u_ref, q_ref, pair_ref, rand_ref, tok_ref, wide_ref) = refs[:-7], refs[-7:]
    place = meta_ref[0]
    group = meta_ref[2]
    chosen = meta_ref[3]
    half = WIDE // 2
    lead = WIDE // 4
    rand_ref[...] = jnp.zeros_like(rand_ref)
    if fast:
        slab = D // 32
        for n, piece in enumerate(w_refs):
            rows = piece[...].astype(f32)
            for a in range(4):
                device = place ^ slab_offset(n, place, fast) ^ PEERS[a]
                wide_ref[pl.ds(pl.multiple_of(device * slab, 8), slab), :] = rows[slab * a : slab * (a + 1)]
                rand_ref[pl.ds(device, 1), :] = rows[slab * a : slab * a + 1, half:WIDE].astype(jnp.int32)
    else:
        wide_ref[...] = w_refs[0][...].astype(f32)
    own = lax.broadcasted_iota(jnp.int32, (D, half), 1) < lead
    above = jnp.zeros((lead, D), f32)
    below = jnp.zeros((half - lead - RANK, D), f32)
    side = jnp.zeros((RANK, WIDE - SHARE), f32)
    for j in range(3):
        low = slice(WIDE * j, WIDE * j + half)
        high = slice(WIDE * j + half, WIDE * (j + 1))
        turned = jnp.concatenate([above, down_ref[chosen, j].astype(f32), below], axis=0).T
        w_ref[:, low] = wide_ref[:, low].astype(bf16)
        w_ref[:, high] = jnp.where(own, wide_ref[:, high], turned).astype(bf16)
        up = up_ref[chosen, j].astype(f32)
        mine = jnp.zeros((RANK, SHARE), f32)
        for g in range(4):
            mine = mine + jnp.where(group == g, up[:, SHARE * g : SHARE * (g + 1)], 0.0)
        mine = jnp.concatenate([mine, side], axis=1)
        u_ref[j] = jnp.concatenate([above[:, :WIDE], mine, below[:, :WIDE]], axis=0).astype(bf16)
    put_tokens(fast, tok_refs, tok_ref)
    q_ref[...], pair_ref[...] = project_rows(dense_mul(tok_ref[...], w_ref[...]), u_ref)


def block_rows(ref, block, count=1):
    return ref[pl.ds(pl.multiple_of(block * BLOCK, BLOCK), count * BLOCK), :]


def merge_heads(stacked):
    lane = lanes(BLOCK)
    total = jnp.zeros((BLOCK, WIDE), f32)
    for head in range(GROUP_HEADS):
        total = jnp.where(head_lanes(lane, head), stacked[BLOCK * head : BLOCK * (head + 1)], total)
    return total


def key_set(ref, picks, block, block_total, fill):
    own = block_rows(ref, block)
    left = block_rows(ref, jnp.maximum(block - 1, 0))
    right = block_rows(ref, jnp.minimum(block + 1, block_total - 1))
    if fill:
        blank = jnp.where(lanes(BLOCK) == MASK_LANE, FLOOR, 0.0).astype(bf16)
        left = jnp.where(block - 1 >= 2, left, blank)
        right = jnp.where(block + 1 < block_total, right, blank)
    rand = [block_rows(ref, pick) for pick in picks]
    return jnp.concatenate([own, left, right, block_rows(ref, 0, 2)] + rand, axis=0)


def own_block(place, t):
    return 2 * (place ^ PEERS[t // 2]) + t % 2


def attend_kernel(fast, meta_ref, rand_ref, q_ref, *refs):
    slab_refs, (k_ref, v_ref, *ctx_refs, aux_ref, s_ref) = refs[:-8], refs[-8:]
    place = meta_ref[0]
    piece = 2 * BLOCK
    for n, slab_ref in enumerate(slab_refs):
        for a in range(4):
            device = place ^ slab_offset(n, place, fast) ^ PEERS[a]
            here = pl.ds(pl.multiple_of(device * piece, piece), piece)
            position = device * piece + lax.broadcasted_iota(jnp.int32, (piece, WIDE), 0)
            k_ref[here, :], v_ref[here, :] = widen_pair(
                slab_ref[piece * a : piece * (a + 1), :], position, meta_ref[1]
            )
    total_rows = k_ref.shape[0]
    block_total = total_rows // BLOCK
    chunks = total_rows // (8 * BLOCK)

    def queries(t):
        rows = q_ref[pl.ds(t * BLOCK, BLOCK), :]
        lane = lanes(BLOCK)
        blank = jnp.zeros_like(rows)
        return jnp.concatenate(
            [
                jnp.where(head_lanes(lane, head) | (lane == MASK_LANE), rows, blank)
                for head in range(GROUP_HEADS)
            ],
            axis=0,
        )

    def finish(t, low, exact, top, total):
        lane = lanes(BLOCK)
        rows = pl.ds(t * BLOCK, BLOCK)
        ctx_refs[t // 2][pl.ds((t % 2) * BLOCK, BLOCK), :] = merge_heads(low).astype(bf16)
        aux = merge_heads(exact)
        lse = top + jnp.log(total)
        for head in range(GROUP_HEADS):
            aux = jnp.where(lane == LSE_LANE + head, lse[BLOCK * head : BLOCK * (head + 1)], aux)
        aux_ref[rows, :] = aux

    def split(probs):
        low = probs.astype(bf16)
        return low, (probs - low.astype(f32)).astype(bf16)

    def sparse(t):
        block = own_block(place, t)
        picks = [rand_at(fast, rand_ref, block, r) for r in range(3)]
        scores = dense_right_t(queries(t), key_set(k_ref, picks, block, block_total, True))
        top = jnp.max(scores, axis=1, keepdims=True)
        weights = jnp.exp(scores - top)
        total = jnp.sum(weights, axis=1, keepdims=True)
        low, rest = split(weights * (1.0 / total))
        values = key_set(v_ref, picks, block, block_total, False)
        context = dense_mul(low, values)
        return context, context + dense_mul(rest, values), top, total

    for a in range(4):

        @pl.when((place ^ PEERS[a]) != 0)
        def _(a=a):
            results = [sparse(2 * a), sparse(2 * a + 1)]
            finish(2 * a, *results[0])
            finish(2 * a + 1, *results[1])

    at_once = s_ref.shape[1] // STACK

    def full(a, first):
        stack = jnp.concatenate([queries(2 * a + first + n) for n in range(at_once)], axis=0)
        height = at_once * STACK

        def score(c, state):
            top, total, tops = state
            part = dense_right_t(stack, block_rows(k_ref, c * 8, 8))
            here = jnp.max(part, axis=1, keepdims=True)
            weights = jnp.exp(part - here)
            s_ref[c] = weights
            later = jnp.maximum(top, here)
            total = total * jnp.exp(top - later) + jnp.sum(weights, axis=1, keepdims=True) * jnp.exp(here - later)
            return later, total, jnp.where(turn == c, here, tops)

        turn = lax.broadcasted_iota(jnp.int32, (height, 128), 1)
        top, total, tops = lax.fori_loop(
            0,
            chunks,
            score,
            (jnp.full((height, 1), FLOOR, f32), jnp.zeros((height, 1), f32), jnp.full((height, 128), FLOOR, f32)),
        )
        scales = jnp.exp(tops - top) * (1.0 / total)

        def mix(c, state):
            scale = jnp.sum(jnp.where(turn == c, scales, 0.0), axis=1, keepdims=True)
            low, rest = split(s_ref[c] * scale)
            values = block_rows(v_ref, c * 8, 8)
            return (state[0] + dense_mul(low, values), state[1] + dense_mul(rest, values))

        zero = jnp.zeros((height, WIDE), f32)
        context, rest = lax.fori_loop(0, chunks, mix, (zero, zero), unroll=2)
        for n in range(at_once):
            here = slice(STACK * n, STACK * (n + 1))
            finish(2 * a + first + n, context[here], (context + rest)[here], top[here], total[here])

    for a in range(4):

        @pl.when((place ^ PEERS[a]) == 0)
        def _(a=a):
            for first in range(0, 2, at_once):
                full(a, first)


def split_parts(value):
    high = value.astype(bf16).astype(f32)
    middle = (value - high).astype(bf16).astype(f32)
    return (high, middle, value - high - middle)


def delta_kernel(*refs):
    grad_refs, aux_ref, out_ref = refs[:4], refs[4], refs[5]
    rows = 2 * BLOCK
    lane = lanes(rows)
    for a in range(4):
        here = pl.ds(a * rows, rows)
        grad = grad_refs[a][...].astype(f32)
        aux = aux_ref[here, :]
        result = jnp.where(lane < SHARE, grad, 0.0)
        product = grad * aux
        for head in range(GROUP_HEADS):
            delta = jnp.sum(jnp.where(head_lanes(lane, head), product, 0.0), axis=1, keepdims=True)
            lse = jnp.sum(jnp.where(lane == LSE_LANE + head, aux, 0.0), axis=1, keepdims=True)
            for p, value in enumerate(split_parts(lse)):
                result = jnp.where(lane == LSE_LANE + 3 * head + p, -value, result)
            for p, value in enumerate(split_parts(delta)):
                result = jnp.where(lane == DEL_LANE + 3 * head + p, -value, result)
        out_ref[here, :] = result.astype(bf16)


def query_stacks(rows, grads):
    lane = lanes(BLOCK)
    blank = jnp.zeros_like(rows)
    queries = []
    outers = []
    for head in range(GROUP_HEADS):
        here = head_lanes(lane, head)
        queries.append(
            jnp.where(
                here | (lane == MASK_LANE), rows, jnp.where(part_lanes(lane, LSE_LANE, head), grads, blank)
            )
        )
        outers.append(jnp.where(here | part_lanes(lane, DEL_LANE, head), grads, blank))
    return jnp.concatenate(queries, axis=0), jnp.concatenate(outers, axis=0)


def near_kernel(fast, meta_ref, rand_ref, q_ref, k_ref, v_ref, g_ref, dq_ref, *refs):
    zero_outs, (blank_ref, sems) = refs[:-2], refs[-2:]
    place = meta_ref[0]
    block_total = k_ref.shape[0] // BLOCK
    copies = []
    if zero_outs:
        blank_ref[...] = jnp.zeros_like(blank_ref)
        for n, where in enumerate(zero_outs):
            shape = where.shape
            source = blank_ref if len(shape) == 4 else blank_ref.at[0 : shape[2] // D]
            for adapter in range(ADAPTERS):
                if len(shape) == 4:
                    copies.append((blank_ref, where.at[adapter], n))
                else:
                    for c in range(shape[2] // D):
                        copies.append((blank_ref.at[c], where.at[adapter, :, pl.ds(D * c, D)], n))
        copies = [pltpu.make_async_copy(source, where, sems.at[n]) for n, (source, where, _) in enumerate(copies)]
        for copy in copies:
            copy.start()

    def query_side(stack, outer, keys, values):
        probs = jnp.exp(dense_right_t(stack, keys))
        scored = (probs * dense_right_t(outer, values)).astype(bf16)
        return dense_mul(scored, keys)

    def put_query(t, stacked):
        dq_ref[pl.ds(t * BLOCK, BLOCK), :] = (merge_heads(stacked) * 0.125).astype(bf16)

    def stacks(t):
        here = slice(t * BLOCK, (t + 1) * BLOCK)
        return query_stacks(q_ref[here, :], g_ref[here, :])

    def sparse(t):
        block = own_block(place, t)
        picks = [rand_at(fast, rand_ref, block, r) for r in range(3)]
        return query_side(
            *stacks(t),
            key_set(k_ref, picks, block, block_total, True),
            key_set(v_ref, picks, block, block_total, False),
        )

    for a in range(4):

        @pl.when((place ^ PEERS[a]) != 0)
        def _(a=a):
            results = [sparse(2 * a), sparse(2 * a + 1)]
            put_query(2 * a, results[0])
            put_query(2 * a + 1, results[1])

        @pl.when((place ^ PEERS[a]) == 0)
        def _(a=a):
            pairs = [stacks(2 * a), stacks(2 * a + 1)]
            stack = jnp.concatenate([pair[0] for pair in pairs], axis=0)
            outer = jnp.concatenate([pair[1] for pair in pairs], axis=0)

            def add(c, total):
                return total + query_side(stack, outer, block_rows(k_ref, c * 8, 8), block_rows(v_ref, c * 8, 8))

            total = lax.fori_loop(0, block_total // 8, add, jnp.zeros((2 * STACK, WIDE), f32), unroll=2)
            put_query(2 * a, total[:STACK])
            put_query(2 * a + 1, total[STACK:])

    for copy in copies:
        copy.wait()


def collect_kernel(fast, block_total, meta_ref, rand_ref, pair_ref):
    place = meta_ref[0]

    def collect(block, count):
        for r in range(3):
            target = rand_at(fast, rand_ref, block, r)
            mine = (((target // 2) ^ place) & ~24) == 0

            @pl.when(mine)
            def _(target=target, count=count):
                pair_ref[count + 1] = target * 65536 + block

            count = count + mine.astype(jnp.int32)
        return count

    pair_ref[0] = lax.fori_loop(2, block_total, collect, jnp.int32(0))


def far_kernel(fast, meta_ref, pair_ref, k_ref, v_ref, dq_ref, w_ref, u_ref, early_ref, *refs):
    count = 3 if fast else 4
    tok_refs, refs = refs[:count], refs[count:]
    slab_refs, refs = refs[:-11], refs[-11:]
    part_refs, near_ref, away_ref, refs = refs[:2], refs[2], refs[3], refs[4:]
    q_ref, g_ref, dk_ref, dv_ref, grad_ref, tok_ref, terms_ref = refs
    place = meta_ref[0]
    group = meta_ref[2]
    block_total = k_ref.shape[0] // BLOCK
    count = len(slab_refs) // 2
    rows = 2 * BLOCK
    for n in range(count):
        here = pl.ds(pl.multiple_of(slab_row(slab_offset(n, place, fast)) * 4 * rows, rows), 4 * rows)
        q_ref[here, :] = slab_refs[n][...]
        g_ref[here, :] = slab_refs[count + n][...]

    def stacks(blocks):
        pairs = []
        for block in blocks:
            other = (block // 2) ^ place
            where = slab_row(other) * 8 + ((other >> 3) & 3) * 2 + (block & 1)
            pairs.append(query_stacks(block_rows(q_ref, where), block_rows(g_ref, where)))
        return (
            jnp.concatenate([pair[0] for pair in pairs], axis=0),
            jnp.concatenate([pair[1] for pair in pairs], axis=0),
        )

    def key_side(keys, values, blocks, allowed):
        stack, outer = stacks(blocks)
        probs = jnp.exp(dense_right_t(keys, stack))
        if allowed is not None:
            probs = jnp.where(allowed, probs, 0.0)
        scored = (probs * dense_right_t(values, outer)).astype(bf16)
        return dense_mul(scored, stack), dense_mul(probs.astype(bf16), outer)

    def put(here, grads):
        dk_ref[here, :] += grads[0]
        dv_ref[here, :] += grads[1]

    key_local = lax.broadcasted_iota(jnp.int32, (rows, 6 * STACK), 0) // BLOCK
    turn = lax.broadcasted_iota(jnp.int32, (rows, 6 * STACK), 1) // STACK
    for a in range(4):
        first = 2 * (place ^ PEERS[a])
        here = slice(rows * a, rows * (a + 1))
        blocks = [0, 1, jnp.maximum(first - 1, 0), first, first + 1, jnp.minimum(first + 2, block_total - 1)]
        key_block = first + key_local
        block = first - 3 + turn
        near = (key_block - block <= 1) & (block - key_block <= 1) & (block >= 2) & (block < block_total)
        allowed = ((turn < 2) | near) & (key_block >= 2)
        keys = block_rows(k_ref, first, 2)
        values = block_rows(v_ref, first, 2)
        dk_ref[here, :], dv_ref[here, :] = key_side(keys, values, blocks, allowed)

    pair_total = pair_ref[0]

    def random_pairs(step, carry):
        grads = []
        for k in range(4):
            number = 4 * step + k
            live = number < pair_total
            code = pair_ref[jnp.minimum(number, pair_total - 1) + 1]
            target = code // 65536
            block = code - target * 65536
            start = ((((target // 2) ^ place) >> 3) & 3) * rows + (target & 1) * BLOCK
            grads.append(
                (
                    pl.ds(pl.multiple_of(start, BLOCK), BLOCK),
                    key_side(block_rows(k_ref, target), block_rows(v_ref, target), (block,), live),
                )
            )
        for here, parts in grads:
            put(here, parts)
        return carry

    lax.fori_loop(0, (pair_total + 3) // 4, random_pairs, 0)

    @pl.when((place & ~24) == 0)
    def _():
        here = pl.ds(pl.multiple_of(group * rows, rows), rows)
        keys = block_rows(k_ref, 0, 2)
        values = block_rows(v_ref, 0, 2)

        def every(step, carry):
            put(here, key_side(keys, values, [4 * step + k for k in range(4)], None))
            return carry

        lax.fori_loop(0, block_total // 4, every, 0, unroll=2)

    data = lanes(rows) < SHARE
    for a in range(4):
        here = slice(rows * a, rows * (a + 1))
        grad_ref[here, :WIDE] = dq_ref[here, :]
        grad_ref[here, WIDE : 2 * WIDE] = jnp.where(data, dk_ref[here, :], 0.0).astype(bf16)
        grad_ref[here, 2 * WIDE :] = jnp.where(data, dv_ref[here, :], 0.0).astype(bf16)
    put_tokens(fast, tok_refs, tok_ref)
    tokens = tok_ref[...]
    lead = WIDE // 4
    terms = []
    ups = []
    for j in range(3):
        high = slice(WIDE * j + WIDE // 2, WIDE * (j + 1))
        grad = grad_ref[:, WIDE * j : WIDE * (j + 1)]
        reduced = dense_mul(tokens, w_ref[:, high]).astype(bf16)
        grad_reduced = dense_right_t(grad, u_ref[j]).astype(bf16)
        terms.append(dense_left_t(grad_reduced, tokens)[lead : lead + RANK])
        up = dense_left_t(reduced, grad)[lead : lead + RANK, :SHARE]
        ups.append(jnp.concatenate([jnp.where(group == g, up, 0.0) for g in range(4)], axis=1))
        grad_ref[:, high] = grad_ref[:, high] + grad_reduced
    terms += ups + [jnp.zeros((RANK, D), f32)] * 2
    core = (place >> 1) & 1
    quarter = plane_quarter(place)
    for part, value in enumerate(terms):
        early = early_ref[EARLY_PART * part : EARLY_PART * (part + 1), :]
        where = (((part // 4) ^ core) * 4 + ((part % 4) ^ quarter)) if fast else part
        terms_ref[where, :RANK] = value
        terms_ref[where, RANK:] = early
    near_ref[...] = terms_ref[:4]
    away_ref[...] = terms_ref[4:].astype(away_ref.dtype)
    for n, a in enumerate((0, 2, 1, 3)):
        part = dense_right_t(grad_ref[rows * a : rows * (a + 1), :], w_ref[...]).astype(bf16)
        part_refs[n // 2][rows * (n % 2) : rows * (n % 2 + 1), :] = part


def normal(hidden):
    center = hidden - jnp.mean(hidden, axis=-1, keepdims=True)
    root = lax.rsqrt(jnp.mean(center * center, axis=-1, keepdims=True) + norm_eps)
    return center * root, root


def normal_back(grad, normed, root):
    mean = jnp.mean(grad, axis=-1, keepdims=True)
    return root * (grad - mean - normed * jnp.mean(grad * normed, axis=-1, keepdims=True))


def middle_kernel(
    fast,
    meta_ref,
    ctx_refs,
    tok_ref,
    cot_ref,
    late_hbm,
    gain_ref,
    down_table,
    up_table,
    inner_down_table,
    inner_up_table,
    outer_down_table,
    outer_up_table,
    wide_ref,
    out_ref,
    grad_ref,
    piece_refs,
    terms_ref,
    hold_ref,
    pre_ref,
    act_ref,
    late_ref,
    sems,
):
    group = meta_ref[2]
    chosen = meta_ref[3]
    rows = tok_ref.shape[0]
    down_ref = down_table.at[chosen, 3]
    up_ref = up_table.at[chosen, 3]
    inner_down_ref = inner_down_table.at[chosen]
    inner_up_ref = inner_up_table.at[chosen]
    outer_down_ref = outer_down_table.at[chosen]
    outer_up_ref = outer_up_table.at[chosen]
    share = D // (FF // D)
    places = [(slice(None), slice(D * c, D * (c + 1))) for c in range(1 + FF // D)]
    if fast:
        places += [(slice(share * c, share * (c + 1)), slice(D + FF, D + 2 * FF)) for c in range(FF // D)]
    copies = [
        pltpu.make_async_copy(late_hbm.at[place], late_ref.at[place], sems.at[n]) for n, place in enumerate(places)
    ]
    order = [0] + [n for c in range(FF // D) for n in (1 + c, 1 + FF // D + c) if n < len(copies)]
    for n in order:
        copies[n].start()

    def build(c):
        copies[1 + FF // D + c].wait()
        slab = 24
        for pair in range(share // (2 * slab)):
            first = share * c + 2 * slab * pair
            block = late_ref[first : first + 2 * slab, D + FF :].astype(f32)
            cut = [
                block[slab * side : slab * (side + 1), D * n : D * (n + 1)]
                for side in range(2)
                for n in range(FF // D)
            ]
            wide_ref[4 * first : 4 * first + 8 * slab, :] = jnp.concatenate(cut, axis=0).astype(bf16)

    for a in range(4):
        hold_ref[a] = ctx_refs[a][...]
    context = jnp.concatenate([hold_ref[group ^ g][:, :SHARE] for g in range(4)], axis=1)
    context_red = dense_right_t(context, down_ref[...]).astype(bf16)
    copies[0].wait()
    attended = dense_mul(context, late_ref[:, :D]) + dense_mul(context_red, up_ref[...])
    first, first_root = normal(tok_ref[...].astype(f32) + attended)
    first_norm = first * gain_ref[0:1, :] + gain_ref[1:2, :]
    first_low = first_norm.astype(bf16)
    inner_red = dense_right_t(first_low, inner_down_ref[...]).astype(bf16)
    outer_red = jnp.zeros((rows, RANK), f32)
    outer_out = jnp.zeros((rows, D), f32)
    for c in range(FF // D):
        here = slice(D * c, D * (c + 1))
        copies[1 + c].wait()
        if fast:
            build(c)
        pre = dense_mul(first_low, late_ref[:, D * (c + 1) : D * (c + 2)]) + dense_mul(
            inner_red, inner_up_ref[:, here]
        )
        pre_ref[:, here] = pre
        active = (0.5 * pre * (1.0 + lax.erf(pre * 0.7071067811865476))).astype(bf16)
        act_ref[:, here] = active
        outer_red = outer_red + dense_right_t(active, outer_down_ref[:, here])
        outer_out = outer_out + dense_mul(active, wide_ref[here, :])
    outer_red = outer_red.astype(bf16)
    outer_out = outer_out + dense_mul(outer_red, outer_up_ref[...])
    second, second_root = normal(first_norm + outer_out)
    position = meta_ref[0] * rows + lax.broadcasted_iota(jnp.int32, (rows, D), 0)
    valid = (position < meta_ref[1]).astype(f32)
    out_ref[...] = ((second * gain_ref[2:3, :] + gain_ref[3:4, :]) * valid).astype(bf16)
    grad_second = normal_back(valid * cot_ref[...].astype(f32) * gain_ref[2:3, :], second, second_root)
    grad_outer = grad_second.astype(bf16)
    first_up = RANK * 3
    first_down = RANK * (3 + FF // D)
    terms_ref[first_down + RANK * (FF // D) :, :] = dense_left_t(outer_red, grad_outer)
    outer_grad_red = dense_right_t(grad_outer, outer_up_ref[...]).astype(bf16)
    inner_grad_red = jnp.zeros((rows, RANK), f32)
    grad_first = grad_second
    for c in range(FF // D):
        here = slice(D * c, D * (c + 1))
        grad_active = dense_right_t(grad_outer, wide_ref[here, :]) + dense_mul(
            outer_grad_red, outer_down_ref[:, here]
        )
        pre = pre_ref[:, here]
        slope = 0.5 * (1.0 + lax.erf(pre * 0.7071067811865476)) + pre * (
            0.3989422804014327 * jnp.exp(-0.5 * pre * pre)
        )
        grad_inner = (slope * grad_active).astype(bf16)
        terms_ref[first_up + RANK * c : first_up + RANK * (c + 1), :] = dense_left_t(inner_red, grad_inner)
        terms_ref[first_down + RANK * c : first_down + RANK * (c + 1), :] = dense_left_t(
            outer_grad_red, act_ref[:, here]
        )
        inner_grad_red = inner_grad_red + dense_right_t(grad_inner, inner_up_ref[:, here])
        grad_first = grad_first + dense_right_t(grad_inner, late_ref[:, D * (c + 1) : D * (c + 2)])
    inner_grad_red = inner_grad_red.astype(bf16)
    terms_ref[2 * RANK : 3 * RANK, :] = dense_left_t(inner_grad_red, first_low)
    grad_first = grad_first + dense_mul(inner_grad_red, inner_down_ref[...])
    grad_attended = normal_back(grad_first * gain_ref[0:1, :], first, first_root)
    grad_ref[...] = grad_attended
    grad_low = grad_attended.astype(bf16)
    context_grad_red = dense_right_t(grad_low, up_ref[...]).astype(bf16)
    terms_ref[:RANK, :] = dense_left_t(context_grad_red, context)
    terms_ref[RANK : 2 * RANK, :] = dense_left_t(context_red, grad_low)
    grad_context = (
        dense_right_t(grad_low, late_ref[:, :D]) + dense_mul(context_grad_red, down_ref[...])
    ).astype(bf16)
    blank = jnp.zeros((rows, WIDE - SHARE), bf16)
    for g in range(4):
        hold_ref[group ^ g] = jnp.concatenate([grad_context[:, SHARE * g : SHARE * (g + 1)], blank], axis=1)
    for a in range(4):
        piece_refs[a][...] = hold_ref[a]


def spread_kernel(meta_ref, *refs):
    part_refs = refs[:8]
    outs = refs[14:20]
    sum_ref, sems = refs[20:]
    quarter = plane_quarter(meta_ref[0])
    core = (meta_ref[0] >> 1) & 1
    chosen = meta_ref[3]
    for n in range(8):
        part = (core ^ (n // 4)) * 4 + (quarter ^ (n % 4))
        sum_ref[pl.ds(pl.multiple_of(part * RANK, RANK), RANK), :] = part_refs[n][:RANK, :].astype(f32)
        sum_ref[pl.ds(pl.multiple_of(LATE_ROWS + part * EARLY_PART, 8), EARLY_PART), :] = part_refs[n][RANK:, :].astype(f32)
    places = [outs[0].at[chosen, j] for j in range(3)] + [outs[1].at[chosen, j] for j in range(3)]
    places += [None, None, outs[0].at[chosen, 3], outs[1].at[chosen, 3], outs[2].at[chosen]]
    places += [outs[n].at[chosen, :, pl.ds(D * c, D)] for n in (3, 4) for c in range(FF // D)]
    places.append(outs[5].at[chosen])
    copies = [
        pltpu.make_async_copy(sum_ref.at[pl.ds(RANK * n, RANK), :], where, sems.at[n])
        for n, where in enumerate(places)
        if where is not None
    ]
    for copy in copies:
        copy.start()
    for copy in copies:
        copy.wait()


LATE_ROWS = 8 * RANK
EARLY_KINDS = 12
EARLY_PART = EARLY_KINDS * RANK // 8
ANY = pl.BlockSpec(memory_space=pl.ANY)
SMEM = pl.BlockSpec(memory_space=pltpu.SMEM)
VMEM = pl.BlockSpec(memory_space=pltpu.VMEM)


def shards(
    tokens,
    cotangent,
    w_query,
    w_key,
    w_value,
    w_output,
    w_inner,
    w_outer,
    gain_first,
    shift_first,
    gain_second,
    shift_second,
    attn_down,
    attn_up,
    inner_down,
    inner_up,
    outer_down,
    outer_up,
    lengths,
    rand_blocks,
    adapter_pick,
):
    device_total = lax.axis_size("seq") * lax.axis_size("head")
    local_rows = tokens.shape[0]
    seq_total = lengths.shape[0]
    members = device_total // seq_total
    rows_total = members * local_rows
    block_total = rows_total // BLOCK
    chunk = 4 * local_rows
    index = lax.axis_index("seq") * lax.axis_size("head") + lax.axis_index("head")
    place = index % members
    seq_number = index // members
    group = (place >> 3) & 3
    seq_length = lengths[seq_number]
    chosen = adapter_pick[seq_number]
    fast = device_total == 32 and members == 32
    together = lax.optimization_barrier

    def send(value, even, odd):
        return lax.ppermute(
            value, AXES, [(j, j ^ (odd if (j >> 1) & 1 else even)) for j in range(device_total)]
        )

    def swap(value, mask):
        return send(value, mask, mask)

    def one(value):
        return send(value, 4, 1)

    def two(value):
        return send(value, 1, 4)

    def exchange(pieces, masks=PEERS):
        return [pieces[0]] + [swap(pieces[a], masks[a]) for a in range(1, 4)]

    def gather_start(value):
        if not fast:
            masks = [slab_offset(n, place, False) for n in range(members // 4)]
            return [value] + [swap(value, mask) for mask in masks[1:]]
        return [value, one(value), two(value)]

    def gather_end(slabs):
        if not fast:
            return slabs
        slabs = slabs + [two(slabs[1])]
        return slabs + [swap(slab, 2) for slab in slabs]

    def gather_direct(value):
        return gather_start(value) + ([swap(value, 5)] if fast else [])

    def gather_hand(slabs):
        return slabs + [swap(slab, 2) for slab in slabs] if fast else slabs

    def gather_all(value):
        return lax.all_gather(value, AXES, axis=0, tiled=True)

    def share_columns(table, which=group):
        return lax.dynamic_slice_in_dim(table, which * SHARE, SHARE, table.ndim - 1)

    slab = D // device_total
    meta = jnp.stack([place, seq_length, group, chosen]).astype(jnp.int32)
    if fast:
        late_local, *slices = pl.pallas_call(
            pack_kernel,
            in_specs=[SMEM] + [VMEM] * 6,
            out_specs=[VMEM] * 5,
            out_shape=[jax.ShapeDtypeStruct((slab, D + 2 * FF), bf16)]
            + [jax.ShapeDtypeStruct((slab, 3 * WIDE), bf16)] * 4,
            name="pack",
        )(rand_blocks, w_query, w_key, w_value, w_output, w_inner, w_outer)
        late = gather_all(late_local)
        mine = exchange(slices)
        far_tokens = swap(tokens, PEERS[2])
        near_tokens = swap(jnp.concatenate([tokens, far_tokens], axis=0), PEERS[1])
        token_refs = [tokens, far_tokens, near_tokens]
        w_slabs = gather_hand(gather_direct(jnp.concatenate(mine, axis=0)))
    else:
        late = gather_all(
            jnp.concatenate([w_output, w_inner] + [w_outer[slab * c : slab * (c + 1)] for c in range(FF // D)], axis=1)
        )
        full_qkv = gather_all(jnp.concatenate([w_query, w_key, w_value], axis=1))
        rand_all = lax.all_gather(rand_blocks, "seq", axis=0, tiled=True)
        rand_flat = lax.dynamic_slice_in_dim(rand_all, seq_number * block_total, block_total, 0).reshape(-1)
        token_refs = exchange([tokens] * 4)
        w_slabs = [
            jnp.concatenate(
                [
                    jnp.pad(share_columns(full_qkv[:, D * j : D * (j + 1)]), ((0, 0), (0, WIDE - SHARE)))
                    for j in range(3)
                ],
                axis=1,
            )
        ]

    wide_rows = jax.ShapeDtypeStruct((rows_total, WIDE), bf16)
    piece_shapes = [jax.ShapeDtypeStruct((local_rows, WIDE), bf16)] * 4
    side_weight, side_up, query_own, pair_own, rand_table = pl.pallas_call(
        functools.partial(project_kernel, fast),
        in_specs=[SMEM] + [VMEM] * (2 + len(token_refs) + len(w_slabs)),
        out_specs=[VMEM] * 5,
        out_shape=[
            jax.ShapeDtypeStruct((D, 3 * WIDE), bf16),
            jax.ShapeDtypeStruct((3, WIDE // 2, WIDE), bf16),
            jax.ShapeDtypeStruct((chunk, WIDE), bf16),
            jax.ShapeDtypeStruct((chunk, 2 * SHARE), bf16),
            jax.ShapeDtypeStruct((32, WIDE // 2), jnp.int32),
        ],
        scratch_shapes=[pltpu.VMEM((chunk, D), bf16), pltpu.VMEM((D, 3 * WIDE), f32)],
        compiler_params=pltpu.CompilerParams(vmem_limit_bytes=VMEM_LIMIT),
        name="project",
    )(meta, attn_down, attn_up, *token_refs, *w_slabs)
    if fast:
        rand_flat = rand_table
    pair_list = pl.pallas_call(
        functools.partial(collect_kernel, fast, block_total),
        in_specs=[SMEM, SMEM],
        out_specs=SMEM,
        out_shape=jax.ShapeDtypeStruct((3 * block_total + 8,), jnp.int32),
        name="collect",
    )(meta, rand_flat)
    pair_slabs = gather_start(pair_own)
    pair_list, pair_slabs[1] = together((pair_list, pair_slabs[1]))
    pair_slabs = gather_end(pair_slabs)
    key_all, value_all, *ctx, aux = pl.pallas_call(
        functools.partial(attend_kernel, fast),
        in_specs=[SMEM, SMEM] + [VMEM] * (1 + len(pair_slabs)),
        out_specs=[VMEM] * 7,
        out_shape=[wide_rows] * 2 + piece_shapes + [jax.ShapeDtypeStruct((chunk, WIDE), f32)],
        scratch_shapes=[pltpu.VMEM((rows_total // chunk, (2 if fast else 1) * STACK, chunk), f32)],
        compiler_params=pltpu.CompilerParams(vmem_limit_bytes=VMEM_LIMIT),
        name="attend",
    )(meta, rand_flat, query_own, *pair_slabs)
    ctx_pieces = exchange(ctx)

    gains = jnp.stack([gain_first, shift_first, gain_second, shift_second])
    middle_in = [tokens, cotangent, late, gains, attn_down, attn_up, inner_down, inner_up, outer_down, outer_up]
    wide_shape = [pltpu.VMEM((FF, D), bf16)]
    if not fast:
        middle_in.append(
            late[:, D + FF :].reshape(device_total, slab, FF // D, D).transpose(0, 2, 1, 3).reshape(FF, D)
        )
        wide_shape = []
    count = len(middle_in)

    def middle(meta_ref, *refs):
        ins, outs, scratch = refs[4 : 4 + count], refs[4 + count : 11 + count], refs[11 + count :]
        wide_ref = scratch[-1] if fast else ins[-1]
        middle_kernel(
            fast, meta_ref, refs[:4], *ins[:10], wide_ref, *outs[:2], outs[2:6], outs[6], *scratch[:5]
        )


    output, grad_attended, *grad_pieces, early_terms = pl.pallas_call(
        middle,
        in_specs=[SMEM] + [VMEM] * 6 + [ANY] + [VMEM] * (count - 3),
        out_specs=[VMEM] * 7,
        out_shape=[
            jax.ShapeDtypeStruct((local_rows, D), bf16),
            jax.ShapeDtypeStruct((local_rows, D), f32),
        ]
        + piece_shapes
        + [jax.ShapeDtypeStruct((EARLY_KINDS * RANK, D), f32)],
        scratch_shapes=[
            pltpu.VMEM((4, local_rows, WIDE), bf16),
            pltpu.VMEM((local_rows, FF), f32),
            pltpu.VMEM((local_rows, FF), bf16),
            pltpu.VMEM(late.shape, bf16),
            pltpu.SemaphoreType.DMA((1 + 2 * (FF // D),)),
        ]
        + wide_shape,
        compiler_params=pltpu.CompilerParams(vmem_limit_bytes=VMEM_LIMIT),
        name="middle",
    )(meta, *ctx_pieces, *middle_in)
    query_send, grad_pieces[0] = together((query_own, grad_pieces[0]))
    query_slabs = gather_hand(gather_direct(query_send))
    grad_wide = pl.pallas_call(
        delta_kernel,
        in_specs=[VMEM] * 5,
        out_specs=VMEM,
        out_shape=jax.ShapeDtypeStruct((chunk, WIDE), bf16),
        name="delta",
    )(*exchange(grad_pieces), aux)
    def reduced(terms):
        paired = terms[0] + swap(terms[1], 2)
        moved = exchange([paired[a] for a in range(4)])
        part = (moved[0] + moved[1]) + (moved[2] + moved[3])
        moved = [part] + [swap(part, depth) for depth in DEPTHS[1:]]
        return (moved[0] + moved[1]) + (moved[2] + moved[3])

    grad_slabs = gather_start(grad_wide)
    out_shapes = [
        jax.ShapeDtypeStruct(shape, f32)
        for shape in (
            (ADAPTERS, 4, RANK, D),
            (ADAPTERS, 4, RANK, D),
            (ADAPTERS, RANK, D),
            (ADAPTERS, RANK, FF),
            (ADAPTERS, RANK, FF),
            (ADAPTERS, RANK, D),
        )
    ]
    zero_shapes = out_shapes if fast else []
    query_grad, *zeros = pl.pallas_call(
        functools.partial(near_kernel, fast),
        in_specs=[SMEM, SMEM] + [VMEM] * 4,
        out_specs=[VMEM] + [ANY] * len(zero_shapes),
        out_shape=[jax.ShapeDtypeStruct((chunk, WIDE), bf16)] + zero_shapes,
        scratch_shapes=[pltpu.VMEM((4, RANK, D), f32), pltpu.SemaphoreType.DMA((ADAPTERS * 12,))],
        compiler_params=pltpu.CompilerParams(vmem_limit_bytes=VMEM_LIMIT),
        cost_estimate=pl.CostEstimate(flops=12000000000, bytes_accessed=8000000, transcendentals=1000000),
        name="near",
    )(meta, rand_flat, query_own, key_all, value_all, grad_wide)
    query_grad, *grad_slabs = together((query_grad, *grad_slabs))
    grad_slabs = gather_end(grad_slabs)
    kept, given, near_terms, away_terms = pl.pallas_call(
        functools.partial(far_kernel, fast),
        in_specs=[SMEM, SMEM] + [VMEM] * (6 + len(token_refs) + 2 * len(grad_slabs)),
        out_specs=[VMEM] * 4,
        out_shape=[jax.ShapeDtypeStruct((2 * local_rows, D), bf16)] * 2
        + [jax.ShapeDtypeStruct((4, RANK + EARLY_PART, D), kind) for kind in (f32, bf16 if fast else f32)],
        scratch_shapes=[
            pltpu.VMEM((rows_total, WIDE), bf16),
            pltpu.VMEM((rows_total, WIDE), bf16),
            pltpu.VMEM((chunk, WIDE), f32),
            pltpu.VMEM((chunk, WIDE), f32),
            pltpu.VMEM((chunk, 3 * WIDE), bf16),
            pltpu.VMEM((chunk, D), bf16),
            pltpu.VMEM((8, RANK + EARLY_PART, D), f32),
        ],
        compiler_params=pltpu.CompilerParams(vmem_limit_bytes=VMEM_LIMIT),
        name="far",
    )(
        meta,
        pair_list,
        key_all,
        value_all,
        query_grad,
        side_weight,
        side_up,
        early_terms,
        *token_refs,
        *query_slabs,
        *grad_slabs,
    )
    kept = kept.astype(f32) + swap(given, PEERS[1]).astype(f32)
    passed = swap(kept[local_rows:].astype(bf16), PEERS[2])
    grad_tokens = grad_attended + (kept[:local_rows] + passed.astype(f32))

    if fast:
        paired = near_terms + swap(away_terms, 2).astype(f32)
        moved = [paired[0]] + [swap(paired[a].astype(bf16), PLANE[a]).astype(f32) for a in range(1, 4)]
        part = ((moved[0] + moved[1]) + (moved[2] + moved[3])).astype(bf16)
        moved = [piece.astype(f32) for piece in exchange([part] * 4)]
        part = ((moved[0] + moved[1]) + (moved[2] + moved[3])).astype(bf16)
        part_list = exchange([part] * 4, PLANE)
        part_list = part_list + [swap(value, 2) for value in part_list]
        sums = pl.pallas_call(
            spread_kernel,
            in_specs=[SMEM] + [VMEM] * 8 + [ANY] * 6,
            out_specs=[ANY] * 6,
            out_shape=out_shapes,
            scratch_shapes=[
                pltpu.VMEM((LATE_ROWS + EARLY_KINDS * RANK, D), f32),
                pltpu.SemaphoreType.DMA((8 + EARLY_KINDS,)),
            ],
            input_output_aliases={9 + n: n for n in range(6)},
            name="spread",
        )(meta, *part_list, *zeros)
        return (output, grad_tokens, *sums)

    terms = jnp.concatenate([near_terms, away_terms], axis=0)
    terms = jnp.concatenate([terms[:, :RANK].reshape(-1, D), terms[:, RANK:].reshape(-1, D)], axis=0)
    slots = (jnp.arange(seq_total) == seq_number).astype(f32)[:, None, None]
    every = lax.psum(slots * terms[None], AXES)

    def spread(kinds, width):
        def term(s):
            rows = jnp.concatenate([every[s, kind * RANK : (kind + width // D) * RANK] for kind in kinds], axis=0)
            value = rows.reshape(len(kinds), width // D, RANK, D).transpose(0, 2, 1, 3)
            value = value.reshape(len(kinds), RANK, width)
            return (jnp.arange(ADAPTERS) == adapter_pick[s]).astype(f32)[:, None, None, None] * value[None]

        return functools.reduce(lambda x, y: x + y, [term(s) for s in range(seq_total)])

    wide = FF // D
    sums = [
        spread((0, 1, 2, 8), D),
        spread((3, 4, 5, 9), D),
        spread((10,), D),
        spread((11,), FF),
        spread((11 + wide,), FF),
        spread((11 + 2 * wide,), D),
    ]
    return (
        output,
        grad_tokens,
        *[value.reshape(leaf.shape) for value, leaf in zip(sums, out_shapes, strict=True)],
    )


def solution(mesh):
    rows = P(AXES, None)
    placed = (rows,) * 8 + (P(),) * 11 + (P("seq", None), P())
    return jax.shard_map(
        shards,
        mesh=mesh,
        in_specs=placed,
        out_specs=(rows, rows) + (P(),) * 6,
        check_vma=False,
    )
```

```python
import functools

import jax
import jax.numpy as jnp
from jax import lax
from jax.experimental import pallas as pl
from jax.experimental.pallas import tpu as pltpu
from jax.sharding import PartitionSpec as P

D = 768
HEADS = 12
HDIM = 64
BLOCK = 64
ADAPTERS = 8
RANK = 16
FF = 3072

PEERS = (0, 8, 16, 24)
PLANE = (0, 1, 4, 5)
GROUP_HEADS = HEADS // 4
SHARE = GROUP_HEADS * HDIM
WIDE = 256
LSE_LANE = SHARE
DEL_LANE = SHARE + 9
MASK_LANE = SHARE + 18
FLOOR = -1e30
STACK = GROUP_HEADS * BLOCK
AXES = ("seq", "head")
norm_eps = 1e-12
f32 = jnp.float32
bf16 = jnp.bfloat16
VMEM_LIMIT = 60 * 1024 * 1024


def dense_mul(left_op, right_op):
    return jnp.dot(left_op, right_op, preferred_element_type=f32)


def dense_right_t(left_op, right_op):
    return lax.dot_general(left_op, right_op, (((1,), (1,)), ((), ())), preferred_element_type=f32)


def dense_left_t(left_op, right_op):
    return lax.dot_general(left_op, right_op, (((0,), (0,)), ((), ())), preferred_element_type=f32)


def lanes(rows):
    return lax.broadcasted_iota(jnp.int32, (rows, WIDE), 1)


def head_lanes(lane, head):
    return (lane >= HDIM * head) & (lane < HDIM * (head + 1))


def part_lanes(lane, first, head):
    return (lane >= first + 3 * head) & (lane < first + 3 * head + 3)


def project_rows(raw, u_ref):
    lane = lanes(raw.shape[0])
    data = lane < SHARE

    def part(j):
        piece = raw[:, WIDE * j : WIDE * (j + 1)]
        return (piece + dense_mul(piece[:, WIDE // 2 :].astype(bf16), u_ref[j])).astype(bf16).astype(f32)

    query = jnp.where(data, part(0) * 0.125, jnp.where(lane == MASK_LANE, 1.0, 0.0)).astype(bf16)
    return query, jnp.concatenate([part(1)[:, :SHARE], part(2)[:, :SHARE]], axis=1).astype(bf16)


def widen_pair(pair, position, seq_length):
    lane = lanes(pair.shape[0])
    data = lane < SHARE
    blank = jnp.zeros((pair.shape[0], WIDE - SHARE), bf16)
    key = jnp.concatenate([pair[:, :SHARE], blank], axis=1)
    value = jnp.concatenate([pair[:, SHARE:], blank], axis=1)
    mask = jnp.where(position < seq_length, 0.0, FLOOR)
    key_side = jnp.where(lane < DEL_LANE, 1.0, jnp.where(lane == MASK_LANE, mask, 0.0)).astype(bf16)
    value_side = jnp.where((lane >= DEL_LANE) & (lane < MASK_LANE), 1.0, 0.0).astype(bf16)
    return jnp.where(data, key, key_side), jnp.where(data, value, value_side)


def slab_offset(n, place, fast):
    if not fast:
        return (n & 7) | ((n >> 3) << 5)
    core = (place >> 1) & 1
    near = 4 - 3 * core if n < 4 else 1 + 3 * core
    return (0, near, 5 - near, 5)[n % 4] ^ (2 * (n // 4))


def slab_row(offset):
    return (offset & 7) | ((offset >> 5) << 3)


def plane_quarter(place):
    return (place & 1) | ((place >> 1) & 2)


def rand_at(fast, rand_ref, block, r):
    if not fast:
        return rand_ref[block * 3 + r]
    return rand_ref[(block // 4) * 2, WIDE // 4 + (block & 3) * 3 + r]


def pack_kernel(rand_ref, query_ref, key_ref, value_ref, output_ref, inner_ref, outer_ref, late_ref, *slice_refs):
    slab = query_ref.shape[0]
    group = ((lax.axis_index("seq") * lax.axis_size("head") + lax.axis_index("head")) >> 3) & 3
    late_ref[:, :D] = output_ref[...]
    late_ref[:, D : D + FF] = inner_ref[...]
    outer = outer_ref[...].astype(f32)
    for c in range(FF // D):
        late_ref[:, D + FF + D * c : D + FF + D * (c + 1)] = outer[slab * c : slab * (c + 1)].astype(bf16)
    spare = (slab, WIDE - SHARE)
    lane = lax.broadcasted_iota(jnp.int32, spare, 1)
    marks = jnp.zeros(spare, f32)
    for n in range(12):
        marks = jnp.where(lane == n, rand_ref[n // 3, n % 3].astype(f32), marks)
    marks = jnp.where(lax.broadcasted_iota(jnp.int32, spare, 0) == 0, marks, 0.0)
    sources = [ref[...].astype(f32) for ref in (query_ref, key_ref, value_ref)]
    for p in range(4):
        pieces = []
        for source in sources:
            mine = source[:, :SHARE]
            for g in range(1, 4):
                mine = jnp.where((group ^ p) == g, source[:, SHARE * g : SHARE * (g + 1)], mine)
            pieces += [mine, marks]
        slice_refs[p][...] = jnp.concatenate(pieces, axis=1).astype(bf16)


def put_tokens(fast, token_refs, tok_ref):
    rows = 2 * BLOCK
    if fast:
        own, far, near = token_refs
        parts = [own[...], near[:rows, :], far[...], near[rows:, :]]
    else:
        parts = [ref[...] for ref in token_refs]
    for a in range(4):
        tok_ref[rows * a : rows * (a + 1), :] = parts[a]


def project_kernel(fast, meta_ref, down_ref, up_ref, *refs):
    count = 3 if fast else 4
    tok_refs, refs = refs[:count], refs[count:]
    w_refs, (w_ref, down_stack_ref, up_stack_ref, q_ref, pair_ref, rand_ref, u_ref, tok_ref, wide_ref) = refs[:-9], refs[-9:]
    place = meta_ref[0]
    group = meta_ref[2]
    chosen = meta_ref[3]
    half = WIDE // 2
    lead = WIDE // 4
    rand_ref[...] = jnp.zeros_like(rand_ref)
    if fast:
        slab = D // 32
        for n, piece in enumerate(w_refs):
            rows = piece[...].astype(f32)
            for a in range(4):
                device = place ^ slab_offset(n, place, fast) ^ PEERS[a]
                wide_ref[pl.ds(pl.multiple_of(device * slab, 8), slab), :] = rows[slab * a : slab * (a + 1)]
                rand_ref[pl.ds(device, 1), :] = rows[slab * a : slab * a + 1, half:WIDE].astype(jnp.int32)
    else:
        wide_ref[...] = w_refs[0][...].astype(f32)
    own = lax.broadcasted_iota(jnp.int32, (D, half), 1) < lead
    above = jnp.zeros((lead, D), f32)
    below = jnp.zeros((half - lead - RANK, D), f32)
    side = jnp.zeros((RANK, WIDE - SHARE), f32)
    downs = []
    ups = []
    for j in range(3):
        low = slice(WIDE * j, WIDE * j + half)
        high = slice(WIDE * j + half, WIDE * (j + 1))
        turned = jnp.concatenate([above, down_ref[chosen, j].astype(f32), below], axis=0).T
        w_ref[:, low] = wide_ref[:, low].astype(bf16)
        w_ref[:, high] = jnp.where(own, wide_ref[:, high], turned).astype(bf16)
        up = up_ref[chosen, j].astype(f32)
        mine = jnp.zeros((RANK, SHARE), f32)
        for g in range(4):
            mine = mine + jnp.where(group == g, up[:, SHARE * g : SHARE * (g + 1)], 0.0)
        mine = jnp.concatenate([mine, side], axis=1)
        u_ref[j] = jnp.concatenate([above[:, :WIDE], mine, below[:, :WIDE]], axis=0).astype(bf16)
        downs.append(down_ref[chosen, j].astype(f32))
        ups.append(jnp.concatenate([mine if n == j else jnp.zeros_like(mine) for n in range(3)], axis=1))
    rest = jnp.zeros((half - 3 * RANK, D), f32)
    down_stack_ref[...] = jnp.concatenate(downs + [rest], axis=0).astype(bf16)
    up_stack_ref[...] = jnp.concatenate(ups + [rest], axis=0).astype(bf16)
    put_tokens(fast, tok_refs, tok_ref)
    q_ref[...], pair_ref[...] = project_rows(dense_mul(tok_ref[...], w_ref[...]), u_ref)


def block_rows(ref, block, count=1):
    return ref[pl.ds(pl.multiple_of(block * BLOCK, BLOCK), count * BLOCK), :]


def merge_heads(stacked):
    lane = lanes(BLOCK)
    total = jnp.zeros((BLOCK, WIDE), f32)
    for head in range(GROUP_HEADS):
        total = jnp.where(head_lanes(lane, head), stacked[BLOCK * head : BLOCK * (head + 1)], total)
    return total


def key_set(ref, picks, block, block_total, fill):
    own = block_rows(ref, block)
    left = block_rows(ref, jnp.maximum(block - 1, 0))
    right = block_rows(ref, jnp.minimum(block + 1, block_total - 1))
    if fill:
        blank = jnp.where(lanes(BLOCK) == MASK_LANE, FLOOR, 0.0).astype(bf16)
        left = jnp.where(block - 1 >= 2, left, blank)
        right = jnp.where(block + 1 < block_total, right, blank)
    rand = [block_rows(ref, pick) for pick in picks]
    return jnp.concatenate([own, left, right, block_rows(ref, 0, 2)] + rand, axis=0)


def own_block(place, t):
    return 2 * (place ^ PEERS[t // 2]) + t % 2


def attend_kernel(fast, meta_ref, rand_ref, q_ref, *refs):
    slab_refs, (k_ref, v_ref, *ctx_refs, aux_ref, s_ref) = refs[:-8], refs[-8:]
    place = meta_ref[0]
    piece = 2 * BLOCK
    for n, slab_ref in enumerate(slab_refs):
        for a in range(4):
            device = place ^ slab_offset(n, place, fast) ^ PEERS[a]
            here = pl.ds(pl.multiple_of(device * piece, piece), piece)
            position = device * piece + lax.broadcasted_iota(jnp.int32, (piece, WIDE), 0)
            k_ref[here, :], v_ref[here, :] = widen_pair(
                slab_ref[piece * a : piece * (a + 1), :], position, meta_ref[1]
            )
    total_rows = k_ref.shape[0]
    block_total = total_rows // BLOCK
    chunks = total_rows // (8 * BLOCK)

    def queries(t):
        rows = q_ref[pl.ds(t * BLOCK, BLOCK), :]
        lane = lanes(BLOCK)
        blank = jnp.zeros_like(rows)
        return jnp.concatenate(
            [
                jnp.where(head_lanes(lane, head) | (lane == MASK_LANE), rows, blank)
                for head in range(GROUP_HEADS)
            ],
            axis=0,
        )

    def finish(t, low, exact, top, total):
        lane = lanes(BLOCK)
        rows = pl.ds(t * BLOCK, BLOCK)
        ctx_refs[t // 2][pl.ds((t % 2) * BLOCK, BLOCK), :] = merge_heads(low).astype(bf16)
        aux = merge_heads(exact)
        lse = top + jnp.log(total)
        for head in range(GROUP_HEADS):
            aux = jnp.where(lane == LSE_LANE + head, lse[BLOCK * head : BLOCK * (head + 1)], aux)
        aux_ref[rows, :] = aux

    def split(probs):
        low = probs.astype(bf16)
        return low, (probs - low.astype(f32)).astype(bf16)

    def sparse(t):
        block = own_block(place, t)
        picks = [rand_at(fast, rand_ref, block, r) for r in range(3)]
        scores = dense_right_t(queries(t), key_set(k_ref, picks, block, block_total, True))
        top = jnp.max(scores, axis=1, keepdims=True)
        weights = jnp.exp(scores - top)
        total = jnp.sum(weights, axis=1, keepdims=True)
        low, rest = split(weights * (1.0 / total))
        values = key_set(v_ref, picks, block, block_total, False)
        context = dense_mul(low, values)
        return context, context + dense_mul(rest, values), top, total

    for a in range(4):

        @pl.when((place ^ PEERS[a]) != 0)
        def _(a=a):
            results = [sparse(2 * a), sparse(2 * a + 1)]
            finish(2 * a, *results[0])
            finish(2 * a + 1, *results[1])

    at_once = s_ref.shape[1] // STACK

    def full(a, first):
        stack = jnp.concatenate([queries(2 * a + first + n) for n in range(at_once)], axis=0)
        height = at_once * STACK

        def score(c, state):
            top, total, tops = state
            part = dense_right_t(stack, block_rows(k_ref, c * 8, 8))
            here = jnp.max(part, axis=1, keepdims=True)
            weights = jnp.exp(part - here)
            s_ref[c] = weights
            later = jnp.maximum(top, here)
            total = total * jnp.exp(top - later) + jnp.sum(weights, axis=1, keepdims=True) * jnp.exp(here - later)
            return later, total, jnp.where(turn == c, here, tops)

        turn = lax.broadcasted_iota(jnp.int32, (height, 128), 1)
        top, total, tops = lax.fori_loop(
            0,
            chunks,
            score,
            (jnp.full((height, 1), FLOOR, f32), jnp.zeros((height, 1), f32), jnp.full((height, 128), FLOOR, f32)),
        )
        scales = jnp.exp(tops - top) * (1.0 / total)

        def mix(c, state):
            scale = jnp.sum(jnp.where(turn == c, scales, 0.0), axis=1, keepdims=True)
            low, rest = split(s_ref[c] * scale)
            values = block_rows(v_ref, c * 8, 8)
            return (state[0] + dense_mul(low, values), state[1] + dense_mul(rest, values))

        zero = jnp.zeros((height, WIDE), f32)
        context, rest = lax.fori_loop(0, chunks, mix, (zero, zero), unroll=4)
        for n in range(at_once):
            here = slice(STACK * n, STACK * (n + 1))
            finish(2 * a + first + n, context[here], (context + rest)[here], top[here], total[here])

    for a in range(4):

        @pl.when((place ^ PEERS[a]) == 0)
        def _(a=a):
            for first in range(0, 2, at_once):
                full(a, first)


DENSE_ROWS = 96


def fold_rows(rows):
    last = rows[DENSE_ROWS:]
    beside = jnp.concatenate([last[:, HDIM * h : HDIM * (h + 1)] for h in range(GROUP_HEADS)], axis=0)
    return jnp.concatenate([rows[:DENSE_ROWS], beside], axis=1)


def unfold_rows(folded):
    beside = folded[:, SHARE:]
    count = DENSE_ROWS // GROUP_HEADS
    last = jnp.concatenate([beside[count * h : count * (h + 1)] for h in range(GROUP_HEADS)], axis=1)
    rows = jnp.concatenate([folded[:, :SHARE], last], axis=0)
    return jnp.concatenate([rows, jnp.zeros((rows.shape[0], WIDE - SHARE), rows.dtype)], axis=1)


def split_parts(value):
    high = value.astype(bf16).astype(f32)
    middle = (value - high).astype(bf16).astype(f32)
    return (high, middle, value - high - middle)


def delta_kernel(*refs):
    grad_refs, aux_ref, out_ref = refs[:4], refs[4], refs[5]
    rows = 2 * BLOCK
    lane = lanes(rows)
    for a in range(4):
        here = pl.ds(a * rows, rows)
        grad = unfold_rows(grad_refs[a][...]).astype(f32)
        aux = aux_ref[here, :]
        result = jnp.where(lane < SHARE, grad, 0.0)
        product = grad * aux
        for head in range(GROUP_HEADS):
            delta = jnp.sum(jnp.where(head_lanes(lane, head), product, 0.0), axis=1, keepdims=True)
            lse = jnp.sum(jnp.where(lane == LSE_LANE + head, aux, 0.0), axis=1, keepdims=True)
            for p, value in enumerate(split_parts(lse)):
                result = jnp.where(lane == LSE_LANE + 3 * head + p, -value, result)
            for p, value in enumerate(split_parts(delta)):
                result = jnp.where(lane == DEL_LANE + 3 * head + p, -value, result)
        out_ref[here, :] = result.astype(bf16)


def query_stacks(rows, grads):
    lane = lanes(BLOCK)
    blank = jnp.zeros_like(rows)
    queries = []
    outers = []
    for head in range(GROUP_HEADS):
        here = head_lanes(lane, head)
        queries.append(
            jnp.where(
                here | (lane == MASK_LANE), rows, jnp.where(part_lanes(lane, LSE_LANE, head), grads, blank)
            )
        )
        outers.append(jnp.where(here | part_lanes(lane, DEL_LANE, head), grads, blank))
    return jnp.concatenate(queries, axis=0), jnp.concatenate(outers, axis=0)


def near_kernel(fast, meta_ref, rand_ref, q_ref, k_ref, v_ref, g_ref, dq_ref, *refs):
    zero_outs, (blank_ref, sems) = refs[:-2], refs[-2:]
    place = meta_ref[0]
    block_total = k_ref.shape[0] // BLOCK
    copies = []
    if zero_outs:
        blank_ref[...] = jnp.zeros_like(blank_ref)
        for n, where in enumerate(zero_outs):
            shape = where.shape
            source = blank_ref if len(shape) == 4 else blank_ref.at[0 : shape[2] // D]
            for adapter in range(ADAPTERS):
                if len(shape) == 4:
                    copies.append((blank_ref, where.at[adapter], n))
                else:
                    for c in range(shape[2] // D):
                        copies.append((blank_ref.at[c], where.at[adapter, :, pl.ds(D * c, D)], n))
        copies = [pltpu.make_async_copy(source, where, sems.at[n]) for n, (source, where, _) in enumerate(copies)]
        for copy in copies:
            copy.start()

    def query_side(stack, outer, keys, values):
        probs = jnp.exp(dense_right_t(stack, keys))
        scored = (probs * dense_right_t(outer, values)).astype(bf16)
        return dense_mul(scored, keys)

    def put_query(t, stacked):
        dq_ref[pl.ds(t * BLOCK, BLOCK), :] = (merge_heads(stacked) * 0.125).astype(bf16)

    def stacks(t):
        here = slice(t * BLOCK, (t + 1) * BLOCK)
        return query_stacks(q_ref[here, :], g_ref[here, :])

    def sparse(t):
        block = own_block(place, t)
        picks = [rand_at(fast, rand_ref, block, r) for r in range(3)]
        return query_side(
            *stacks(t),
            key_set(k_ref, picks, block, block_total, True),
            key_set(v_ref, picks, block, block_total, False),
        )

    for a in range(4):

        @pl.when((place ^ PEERS[a]) != 0)
        def _(a=a):
            results = [sparse(2 * a), sparse(2 * a + 1)]
            put_query(2 * a, results[0])
            put_query(2 * a + 1, results[1])

        @pl.when((place ^ PEERS[a]) == 0)
        def _(a=a):
            pairs = [stacks(2 * a), stacks(2 * a + 1)]
            stack = jnp.concatenate([pair[0] for pair in pairs], axis=0)
            outer = jnp.concatenate([pair[1] for pair in pairs], axis=0)

            def add(c, total):
                return total + query_side(stack, outer, block_rows(k_ref, c * 8, 8), block_rows(v_ref, c * 8, 8))

            total = lax.fori_loop(0, block_total // 8, add, jnp.zeros((2 * STACK, WIDE), f32), unroll=4)
            put_query(2 * a, total[:STACK])
            put_query(2 * a + 1, total[STACK:])

    for copy in copies:
        copy.wait()


def collect_kernel(fast, block_total, meta_ref, rand_ref, pair_ref):
    place = meta_ref[0]

    def collect(block, count):
        for r in range(3):
            target = rand_at(fast, rand_ref, block, r)
            mine = (((target // 2) ^ place) & ~24) == 0

            @pl.when(mine)
            def _(target=target, count=count):
                pair_ref[count + 1] = target * 65536 + block

            count = count + mine.astype(jnp.int32)
        return count

    pair_ref[0] = lax.fori_loop(2, block_total, collect, jnp.int32(0))


def far_kernel(fast, meta_ref, pair_ref, k_ref, v_ref, dq_ref, w_ref, down_ref, up_ref, early_ref, *refs):
    count = 3 if fast else 4
    tok_refs, refs = refs[:count], refs[count:]
    slab_refs, refs = refs[:-11], refs[-11:]
    part_refs, near_ref, away_ref, refs = refs[:2], refs[2], refs[3], refs[4:]
    q_ref, g_ref, dk_ref, dv_ref, grad_ref, tok_ref, terms_ref = refs
    place = meta_ref[0]
    group = meta_ref[2]
    block_total = k_ref.shape[0] // BLOCK
    count = len(slab_refs) // 2
    rows = 2 * BLOCK
    for n in range(count):
        here = pl.ds(pl.multiple_of(slab_row(slab_offset(n, place, fast)) * 4 * rows, rows), 4 * rows)
        q_ref[here, :] = slab_refs[n][...]
        g_ref[here, :] = slab_refs[count + n][...]

    def stacks(blocks):
        pairs = []
        for block in blocks:
            other = (block // 2) ^ place
            where = slab_row(other) * 8 + ((other >> 3) & 3) * 2 + (block & 1)
            pairs.append(query_stacks(block_rows(q_ref, where), block_rows(g_ref, where)))
        return (
            jnp.concatenate([pair[0] for pair in pairs], axis=0),
            jnp.concatenate([pair[1] for pair in pairs], axis=0),
        )

    def key_side(keys, values, blocks, allowed):
        stack, outer = stacks(blocks)
        probs = jnp.exp(dense_right_t(keys, stack))
        if allowed is not None:
            probs = jnp.where(allowed, probs, 0.0)
        scored = (probs * dense_right_t(values, outer)).astype(bf16)
        return dense_mul(scored, stack), dense_mul(probs.astype(bf16), outer)

    def put(here, grads):
        dk_ref[here, :] += grads[0]
        dv_ref[here, :] += grads[1]

    key_local = lax.broadcasted_iota(jnp.int32, (rows, 6 * STACK), 0) // BLOCK
    turn = lax.broadcasted_iota(jnp.int32, (rows, 6 * STACK), 1) // STACK
    for a in range(4):
        first = 2 * (place ^ PEERS[a])
        here = slice(rows * a, rows * (a + 1))
        blocks = [0, 1, jnp.maximum(first - 1, 0), first, first + 1, jnp.minimum(first + 2, block_total - 1)]
        key_block = first + key_local
        block = first - 3 + turn
        near = (key_block - block <= 1) & (block - key_block <= 1) & (block >= 2) & (block < block_total)
        allowed = ((turn < 2) | near) & (key_block >= 2)
        keys = block_rows(k_ref, first, 2)
        values = block_rows(v_ref, first, 2)
        dk_ref[here, :], dv_ref[here, :] = key_side(keys, values, blocks, allowed)

    pair_total = pair_ref[0]

    def random_pairs(step, carry):
        grads = []
        for k in range(4):
            number = 4 * step + k
            live = number < pair_total
            code = pair_ref[jnp.minimum(number, pair_total - 1) + 1]
            target = code // 65536
            block = code - target * 65536
            start = ((((target // 2) ^ place) >> 3) & 3) * rows + (target & 1) * BLOCK
            grads.append(
                (
                    pl.ds(pl.multiple_of(start, BLOCK), BLOCK),
                    key_side(block_rows(k_ref, target), block_rows(v_ref, target), (block,), live),
                )
            )
        for here, parts in grads:
            put(here, parts)
        return carry

    lax.fori_loop(0, (pair_total + 3) // 4, random_pairs, 0)

    @pl.when((place & ~24) == 0)
    def _():
        here = pl.ds(pl.multiple_of(group * rows, rows), rows)
        keys = block_rows(k_ref, 0, 2)
        values = block_rows(v_ref, 0, 2)

        def every(step, carry):
            put(here, key_side(keys, values, [4 * step + k for k in range(4)], None))
            return carry

        lax.fori_loop(0, block_total // 4, every, 0, unroll=4)

    data = lanes(rows) < SHARE
    for a in range(4):
        here = slice(rows * a, rows * (a + 1))
        grad_ref[here, :WIDE] = dq_ref[here, :]
        grad_ref[here, WIDE : 2 * WIDE] = jnp.where(data, dk_ref[here, :], 0.0).astype(bf16)
        grad_ref[here, 2 * WIDE :] = jnp.where(data, dv_ref[here, :], 0.0).astype(bf16)
    put_tokens(fast, tok_refs, tok_ref)
    tokens = tok_ref[...]
    grad = grad_ref[...]
    reduced = dense_right_t(tokens, down_ref[...]).astype(bf16)
    grad_reduced = dense_right_t(grad, up_ref[...]).astype(bf16)
    down_terms = dense_left_t(grad_reduced, tokens)
    up_terms = dense_left_t(reduced, grad)
    terms = [down_terms[RANK * j : RANK * (j + 1)] for j in range(3)]
    ups = []
    for j in range(3):
        up = up_terms[RANK * j : RANK * (j + 1), WIDE * j : WIDE * j + SHARE]
        ups.append(jnp.concatenate([jnp.where(group == g, up, 0.0) for g in range(4)], axis=1))
    terms += ups + [jnp.zeros((RANK, D), f32)] * 2
    core = (place >> 1) & 1
    quarter = plane_quarter(place)
    for part, value in enumerate(terms):
        early = early_ref[EARLY_PART * part : EARLY_PART * (part + 1), :]
        where = (((part // 4) ^ core) * 4 + ((part % 4) ^ quarter)) if fast else part
        terms_ref[where, :RANK] = value
        terms_ref[where, RANK:] = early
    near_ref[...] = terms_ref[:4]
    away_ref[...] = terms_ref[4:].astype(away_ref.dtype)
    for n, a in enumerate((0, 2, 1, 3)):
        here = slice(rows * a, rows * (a + 1))
        part = (dense_right_t(grad[here], w_ref[...]) + dense_mul(grad_reduced[here], down_ref[...])).astype(bf16)
        part_refs[n // 2][rows * (n % 2) : rows * (n % 2 + 1), :] = part


def normal(hidden):
    center = hidden - jnp.mean(hidden, axis=-1, keepdims=True)
    root = lax.rsqrt(jnp.mean(center * center, axis=-1, keepdims=True) + norm_eps)
    return center * root, root


def normal_back(grad, normed, root):
    mean = jnp.mean(grad, axis=-1, keepdims=True)
    return root * (grad - mean - normed * jnp.mean(grad * normed, axis=-1, keepdims=True))


def select_kernel(meta_ref, *refs):
    chosen = meta_ref[3]
    tables, (down_ref, up_ref, *rest) = refs[:6], refs[6:]
    down_ref[...] = tables[0][chosen, 3]
    up_ref[...] = tables[1][chosen, 3]
    for table, ref in zip(tables[2:], rest, strict=True):
        ref[...] = table[chosen]


def middle_kernel(
    fast,
    meta_ref,
    ctx_refs,
    tok_ref,
    cot_ref,
    late_hbm,
    gain_ref,
    down_ref,
    up_ref,
    inner_down_ref,
    inner_up_ref,
    outer_down_ref,
    outer_up_ref,
    wide_ref,
    out_ref,
    grad_ref,
    piece_refs,
    terms_ref,
    hold_ref,
    pre_ref,
    act_ref,
    late_ref,
    sems,
):
    group = meta_ref[2]
    rows = tok_ref.shape[0]
    share = D // (FF // D)
    places = [(slice(None), slice(D * c, D * (c + 1))) for c in range(1 + FF // D)]
    if fast:
        places += [(slice(share * c, share * (c + 1)), slice(D + FF, D + 2 * FF)) for c in range(FF // D)]
    copies = [
        pltpu.make_async_copy(late_hbm.at[place], late_ref.at[place], sems.at[n]) for n, place in enumerate(places)
    ]
    order = [0] + [n for c in range(FF // D) for n in (1 + c, 1 + FF // D + c) if n < len(copies)]
    for n in order:
        copies[n].start()

    def build(c):
        copies[1 + FF // D + c].wait()
        slab = 24
        for pair in range(share // (2 * slab)):
            first = share * c + 2 * slab * pair
            block = late_ref[first : first + 2 * slab, D + FF :].astype(f32)
            cut = [
                block[slab * side : slab * (side + 1), D * n : D * (n + 1)]
                for side in range(2)
                for n in range(FF // D)
            ]
            wide_ref[4 * first : 4 * first + 8 * slab, :] = jnp.concatenate(cut, axis=0).astype(bf16)

    for a in range(4):
        hold_ref[a] = ctx_refs[a][...]
    context = jnp.concatenate([hold_ref[group ^ g][:, :SHARE] for g in range(4)], axis=1)
    context_red = dense_right_t(context, down_ref[...]).astype(bf16)
    copies[0].wait()
    attended = dense_mul(context, late_ref[:, :D]) + dense_mul(context_red, up_ref[...])
    first, first_root = normal(tok_ref[...].astype(f32) + attended)
    first_norm = first * gain_ref[0:1, :] + gain_ref[1:2, :]
    first_low = first_norm.astype(bf16)
    inner_red = dense_right_t(first_low, inner_down_ref[...]).astype(bf16)
    outer_red = jnp.zeros((rows, RANK), f32)
    outer_out = jnp.zeros((rows, D), f32)
    for c in range(FF // D):
        here = slice(D * c, D * (c + 1))
        copies[1 + c].wait()
        if fast:
            build(c)
        pre = dense_mul(first_low, late_ref[:, D * (c + 1) : D * (c + 2)]) + dense_mul(
            inner_red, inner_up_ref[:, here]
        )
        pre_ref[:, here] = pre
        active = (0.5 * pre * (1.0 + lax.erf(pre * 0.7071067811865476))).astype(bf16)
        act_ref[:, here] = active
        outer_red = outer_red + dense_right_t(active, outer_down_ref[:, here])
        outer_out = outer_out + dense_mul(active, wide_ref[here, :])
    outer_red = outer_red.astype(bf16)
    outer_out = outer_out + dense_mul(outer_red, outer_up_ref[...])
    second, second_root = normal(first_norm + outer_out)
    position = meta_ref[0] * rows + lax.broadcasted_iota(jnp.int32, (rows, D), 0)
    valid = (position < meta_ref[1]).astype(f32)
    out_ref[...] = ((second * gain_ref[2:3, :] + gain_ref[3:4, :]) * valid).astype(bf16)
    grad_second = normal_back(valid * cot_ref[...].astype(f32) * gain_ref[2:3, :], second, second_root)
    grad_outer = grad_second.astype(bf16)
    first_up = RANK * 3
    first_down = RANK * (3 + FF // D)
    terms_ref[first_down + RANK * (FF // D) :, :] = dense_left_t(outer_red, grad_outer)
    outer_grad_red = dense_right_t(grad_outer, outer_up_ref[...]).astype(bf16)
    inner_grad_red = jnp.zeros((rows, RANK), f32)
    grad_first = grad_second
    for c in range(FF // D):
        here = slice(D * c, D * (c + 1))
        grad_active = dense_right_t(grad_outer, wide_ref[here, :]) + dense_mul(
            outer_grad_red, outer_down_ref[:, here]
        )
        pre = pre_ref[:, here]
        slope = 0.5 * (1.0 + lax.erf(pre * 0.7071067811865476)) + pre * (
            0.3989422804014327 * jnp.exp(-0.5 * pre * pre)
        )
        grad_inner = (slope * grad_active).astype(bf16)
        terms_ref[first_up + RANK * c : first_up + RANK * (c + 1), :] = dense_left_t(inner_red, grad_inner)
        terms_ref[first_down + RANK * c : first_down + RANK * (c + 1), :] = dense_left_t(
            outer_grad_red, act_ref[:, here]
        )
        inner_grad_red = inner_grad_red + dense_right_t(grad_inner, inner_up_ref[:, here])
        grad_first = grad_first + dense_right_t(grad_inner, late_ref[:, D * (c + 1) : D * (c + 2)])
    inner_grad_red = inner_grad_red.astype(bf16)
    terms_ref[2 * RANK : 3 * RANK, :] = dense_left_t(inner_grad_red, first_low)
    grad_first = grad_first + dense_mul(inner_grad_red, inner_down_ref[...])
    grad_attended = normal_back(grad_first * gain_ref[0:1, :], first, first_root)
    grad_ref[...] = grad_attended
    grad_low = grad_attended.astype(bf16)
    context_grad_red = dense_right_t(grad_low, up_ref[...]).astype(bf16)
    terms_ref[:RANK, :] = dense_left_t(context_grad_red, context)
    terms_ref[RANK : 2 * RANK, :] = dense_left_t(context_red, grad_low)
    grad_context = (
        dense_right_t(grad_low, late_ref[:, :D]) + dense_mul(context_grad_red, down_ref[...])
    ).astype(bf16)
    for g in range(4):
        hold_ref[group ^ g, :DENSE_ROWS, :] = fold_rows(grad_context[:, SHARE * g : SHARE * (g + 1)])
    for a in range(4):
        piece_refs[a][...] = hold_ref[a, :DENSE_ROWS, :]


def spread_kernel(meta_ref, *refs):
    part_refs = refs[:8]
    outs = refs[14:20]
    sum_ref, sems = refs[20:]
    quarter = plane_quarter(meta_ref[0])
    core = (meta_ref[0] >> 1) & 1
    chosen = meta_ref[3]
    for n in range(8):
        part = (core ^ (n // 4)) * 4 + (quarter ^ (n % 4))
        sum_ref[pl.ds(pl.multiple_of(part * RANK, RANK), RANK), :] = part_refs[n][:RANK, :].astype(f32)
        sum_ref[pl.ds(pl.multiple_of(LATE_ROWS + part * EARLY_PART, 8), EARLY_PART), :] = part_refs[n][RANK:, :].astype(f32)
    places = [outs[0].at[chosen, j] for j in range(3)] + [outs[1].at[chosen, j] for j in range(3)]
    places += [None, None, outs[0].at[chosen, 3], outs[1].at[chosen, 3], outs[2].at[chosen]]
    places += [outs[n].at[chosen, :, pl.ds(D * c, D)] for n in (3, 4) for c in range(FF // D)]
    places.append(outs[5].at[chosen])
    copies = [
        pltpu.make_async_copy(sum_ref.at[pl.ds(RANK * n, RANK), :], where, sems.at[n])
        for n, where in enumerate(places)
        if where is not None
    ]
    for copy in copies:
        copy.start()
    for copy in copies:
        copy.wait()


LATE_ROWS = 8 * RANK
EARLY_KINDS = 12
EARLY_PART = EARLY_KINDS * RANK // 8
ANY = pl.BlockSpec(memory_space=pl.ANY)
SMEM = pl.BlockSpec(memory_space=pltpu.SMEM)
VMEM = pl.BlockSpec(memory_space=pltpu.VMEM)


def shards(
    tokens,
    cotangent,
    w_query,
    w_key,
    w_value,
    w_output,
    w_inner,
    w_outer,
    gain_first,
    shift_first,
    gain_second,
    shift_second,
    attn_down,
    attn_up,
    inner_down,
    inner_up,
    outer_down,
    outer_up,
    lengths,
    rand_blocks,
    adapter_pick,
):
    device_total = lax.axis_size("seq") * lax.axis_size("head")
    local_rows = tokens.shape[0]
    seq_total = lengths.shape[0]
    members = device_total // seq_total
    rows_total = members * local_rows
    block_total = rows_total // BLOCK
    chunk = 4 * local_rows
    index = lax.axis_index("seq") * lax.axis_size("head") + lax.axis_index("head")
    place = index % members
    seq_number = index // members
    group = (place >> 3) & 3
    seq_length = lengths[seq_number]
    chosen = adapter_pick[seq_number]
    fast = device_total == 32 and members == 32
    together = lax.optimization_barrier

    def send(value, even, odd):
        return lax.ppermute(
            value, AXES, [(j, j ^ (odd if (j >> 1) & 1 else even)) for j in range(device_total)]
        )

    def swap(value, mask):
        return send(value, mask, mask)

    def one(value):
        return send(value, 4, 1)

    def two(value):
        return send(value, 1, 4)

    def exchange(pieces, masks=PEERS):
        return [pieces[0]] + [swap(pieces[a], masks[a]) for a in range(1, 4)]

    def gather_start(value):
        if not fast:
            masks = [slab_offset(n, place, False) for n in range(members // 4)]
            return [value] + [swap(value, mask) for mask in masks[1:]]
        return [value, one(value), two(value)]

    def gather_end(slabs):
        if not fast:
            return slabs
        slabs = slabs + [two(slabs[1])]
        return slabs + [swap(slab, 2) for slab in slabs]

    def gather_direct(value):
        return gather_start(value) + ([swap(value, 5)] if fast else [])

    def gather_hand(slabs):
        return slabs + [swap(slab, 2) for slab in slabs] if fast else slabs

    def gather_all(value):
        return lax.all_gather(value, AXES, axis=0, tiled=True)

    def share_columns(table, which=group):
        return lax.dynamic_slice_in_dim(table, which * SHARE, SHARE, table.ndim - 1)

    slab = D // device_total
    meta = jnp.stack([place, seq_length, group, chosen]).astype(jnp.int32)
    if fast:
        late_local, *slices = pl.pallas_call(
            pack_kernel,
            in_specs=[SMEM] + [VMEM] * 6,
            out_specs=[VMEM] * 5,
            out_shape=[jax.ShapeDtypeStruct((slab, D + 2 * FF), bf16)]
            + [jax.ShapeDtypeStruct((slab, 3 * WIDE), bf16)] * 4,
            name="pack",
        )(rand_blocks, w_query, w_key, w_value, w_output, w_inner, w_outer)
        late = gather_all(late_local)
        mine = exchange(slices)
        far_tokens = swap(tokens, PEERS[2])
        near_tokens = swap(jnp.concatenate([tokens, far_tokens], axis=0), PEERS[1])
        token_refs = [tokens, far_tokens, near_tokens]
        w_slabs = gather_hand(gather_direct(jnp.concatenate(mine, axis=0)))
    else:
        late = gather_all(
            jnp.concatenate([w_output, w_inner] + [w_outer[slab * c : slab * (c + 1)] for c in range(FF // D)], axis=1)
        )
        full_qkv = gather_all(jnp.concatenate([w_query, w_key, w_value], axis=1))
        rand_all = lax.all_gather(rand_blocks, "seq", axis=0, tiled=True)
        rand_flat = lax.dynamic_slice_in_dim(rand_all, seq_number * block_total, block_total, 0).reshape(-1)
        token_refs = exchange([tokens] * 4)
        w_slabs = [
            jnp.concatenate(
                [
                    jnp.pad(share_columns(full_qkv[:, D * j : D * (j + 1)]), ((0, 0), (0, WIDE - SHARE)))
                    for j in range(3)
                ],
                axis=1,
            )
        ]

    wide_rows = jax.ShapeDtypeStruct((rows_total, WIDE), bf16)
    piece_shapes = [jax.ShapeDtypeStruct((local_rows, WIDE), bf16)] * 4
    side_weight, down_stack, up_stack, query_own, pair_own, rand_table = pl.pallas_call(
        functools.partial(project_kernel, fast),
        in_specs=[SMEM] + [VMEM] * (2 + len(token_refs) + len(w_slabs)),
        out_specs=[VMEM] * 6,
        out_shape=[
            jax.ShapeDtypeStruct((D, 3 * WIDE), bf16),
            jax.ShapeDtypeStruct((WIDE // 2, D), bf16),
            jax.ShapeDtypeStruct((WIDE // 2, 3 * WIDE), bf16),
            jax.ShapeDtypeStruct((chunk, WIDE), bf16),
            jax.ShapeDtypeStruct((chunk, 2 * SHARE), bf16),
            jax.ShapeDtypeStruct((32, WIDE // 2), jnp.int32),
        ],
        scratch_shapes=[
            pltpu.VMEM((3, WIDE // 2, WIDE), bf16),
            pltpu.VMEM((chunk, D), bf16),
            pltpu.VMEM((D, 3 * WIDE), f32),
        ],
        compiler_params=pltpu.CompilerParams(vmem_limit_bytes=VMEM_LIMIT),
        name="project",
    )(meta, attn_down, attn_up, *token_refs, *w_slabs)
    if fast:
        rand_flat = rand_table
    pair_list = pl.pallas_call(
        functools.partial(collect_kernel, fast, block_total),
        in_specs=[SMEM, SMEM],
        out_specs=SMEM,
        out_shape=jax.ShapeDtypeStruct((3 * block_total + 8,), jnp.int32),
        name="collect",
    )(meta, rand_flat)
    pair_slabs = gather_start(pair_own)
    pair_list, pair_slabs[1] = together((pair_list, pair_slabs[1]))
    pair_slabs = gather_end(pair_slabs)
    key_all, value_all, *ctx, aux = pl.pallas_call(
        functools.partial(attend_kernel, fast),
        in_specs=[SMEM, SMEM] + [VMEM] * (1 + len(pair_slabs)),
        out_specs=[VMEM] * 7,
        out_shape=[wide_rows] * 2 + piece_shapes + [jax.ShapeDtypeStruct((chunk, WIDE), f32)],
        scratch_shapes=[pltpu.VMEM((rows_total // chunk, (2 if fast else 1) * STACK, chunk), f32)],
        compiler_params=pltpu.CompilerParams(vmem_limit_bytes=VMEM_LIMIT),
        name="attend",
    )(meta, rand_flat, query_own, *pair_slabs)
    *tables, ctx[1] = together((attn_down, attn_up, inner_down, inner_up, outer_down, outer_up, ctx[1]))
    ctx_pieces = exchange(ctx)

    gains = jnp.stack([gain_first, shift_first, gain_second, shift_second])
    chosen_maps = pl.pallas_call(
        select_kernel,
        in_specs=[SMEM] + [VMEM] * 6,
        out_specs=[VMEM] * 6,
        out_shape=[jax.ShapeDtypeStruct((RANK, width), bf16) for width in (D, D, D, FF, FF, D)],
        name="select",
    )(meta, *tables)
    *chosen_maps, late = together((*chosen_maps, late))
    middle_in = [tokens, cotangent, late, gains, *chosen_maps]
    wide_shape = [pltpu.VMEM((FF, D), bf16)]
    if not fast:
        middle_in.append(
            late[:, D + FF :].reshape(device_total, slab, FF // D, D).transpose(0, 2, 1, 3).reshape(FF, D)
        )
        wide_shape = []
    count = len(middle_in)

    def middle(meta_ref, *refs):
        ins, outs, scratch = refs[4 : 4 + count], refs[4 + count : 11 + count], refs[11 + count :]
        wide_ref = scratch[-1] if fast else ins[-1]
        middle_kernel(
            fast, meta_ref, refs[:4], *ins[:10], wide_ref, *outs[:2], outs[2:6], outs[6], *scratch[:5]
        )


    output, grad_attended, *grad_pieces, early_terms = pl.pallas_call(
        middle,
        in_specs=[SMEM] + [VMEM] * 6 + [ANY] + [VMEM] * (count - 3),
        out_specs=[VMEM] * 7,
        out_shape=[
            jax.ShapeDtypeStruct((local_rows, D), bf16),
            jax.ShapeDtypeStruct((local_rows, D), f32),
        ]
        + [jax.ShapeDtypeStruct((DENSE_ROWS, WIDE), bf16)] * 4
        + [jax.ShapeDtypeStruct((EARLY_KINDS * RANK, D), f32)],
        scratch_shapes=[
            pltpu.VMEM((4, local_rows, WIDE), bf16),
            pltpu.VMEM((local_rows, FF), f32),
            pltpu.VMEM((local_rows, FF), bf16),
            pltpu.VMEM(late.shape, bf16),
            pltpu.SemaphoreType.DMA((1 + 2 * (FF // D),)),
        ]
        + wide_shape,
        compiler_params=pltpu.CompilerParams(vmem_limit_bytes=VMEM_LIMIT),
        name="middle",
    )(meta, *ctx_pieces, *middle_in)
    query_send, grad_pieces[0] = together((query_own, grad_pieces[0]))
    query_slabs = gather_hand(gather_direct(query_send))
    grad_wide = pl.pallas_call(
        delta_kernel,
        in_specs=[VMEM] * 5,
        out_specs=VMEM,
        out_shape=jax.ShapeDtypeStruct((chunk, WIDE), bf16),
        name="delta",
    )(*exchange(grad_pieces), aux)
    def reduced(terms):
        paired = terms[0] + swap(terms[1], 2)
        moved = exchange([paired[a] for a in range(4)])
        part = (moved[0] + moved[1]) + (moved[2] + moved[3])
        moved = [part] + [swap(part, depth) for depth in DEPTHS[1:]]
        return (moved[0] + moved[1]) + (moved[2] + moved[3])

    grad_slabs = gather_start(grad_wide)
    out_shapes = [
        jax.ShapeDtypeStruct(shape, f32)
        for shape in (
            (ADAPTERS, 4, RANK, D),
            (ADAPTERS, 4, RANK, D),
            (ADAPTERS, RANK, D),
            (ADAPTERS, RANK, FF),
            (ADAPTERS, RANK, FF),
            (ADAPTERS, RANK, D),
        )
    ]
    zero_shapes = out_shapes if fast else []
    query_grad, *zeros = pl.pallas_call(
        functools.partial(near_kernel, fast),
        in_specs=[SMEM, SMEM] + [VMEM] * 4,
        out_specs=[VMEM] + [ANY] * len(zero_shapes),
        out_shape=[jax.ShapeDtypeStruct((chunk, WIDE), bf16)] + zero_shapes,
        scratch_shapes=[pltpu.VMEM((4, RANK, D), f32), pltpu.SemaphoreType.DMA((ADAPTERS * 12,))],
        compiler_params=pltpu.CompilerParams(vmem_limit_bytes=VMEM_LIMIT),
        cost_estimate=pl.CostEstimate(flops=12000000000, bytes_accessed=8000000, transcendentals=1000000),
        name="near",
    )(meta, rand_flat, query_own, key_all, value_all, grad_wide)
    query_grad, *grad_slabs = together((query_grad, *grad_slabs))
    grad_slabs = gather_end(grad_slabs)
    kept, given, near_terms, away_terms = pl.pallas_call(
        functools.partial(far_kernel, fast),
        in_specs=[SMEM, SMEM] + [VMEM] * (7 + len(token_refs) + 2 * len(grad_slabs)),
        out_specs=[VMEM] * 4,
        out_shape=[jax.ShapeDtypeStruct((2 * local_rows, D), bf16)] * 2
        + [jax.ShapeDtypeStruct((4, RANK + EARLY_PART, D), kind) for kind in (f32, bf16 if fast else f32)],
        scratch_shapes=[
            pltpu.VMEM((rows_total, WIDE), bf16),
            pltpu.VMEM((rows_total, WIDE), bf16),
            pltpu.VMEM((chunk, WIDE), f32),
            pltpu.VMEM((chunk, WIDE), f32),
            pltpu.VMEM((chunk, 3 * WIDE), bf16),
            pltpu.VMEM((chunk, D), bf16),
            pltpu.VMEM((8, RANK + EARLY_PART, D), f32),
        ],
        compiler_params=pltpu.CompilerParams(vmem_limit_bytes=VMEM_LIMIT),
        name="far",
    )(
        meta,
        pair_list,
        key_all,
        value_all,
        query_grad,
        side_weight,
        down_stack,
        up_stack,
        early_terms,
        *token_refs,
        *query_slabs,
        *grad_slabs,
    )
    kept = kept.astype(f32) + swap(given, PEERS[1]).astype(f32)
    passed = swap(kept[local_rows:].astype(bf16), PEERS[2])
    grad_tokens = grad_attended + (kept[:local_rows] + passed.astype(f32))

    if fast:
        paired = near_terms + swap(away_terms, 2).astype(f32)
        moved = [paired[0]] + [swap(paired[a].astype(bf16), PLANE[a]).astype(f32) for a in range(1, 4)]
        part = ((moved[0] + moved[1]) + (moved[2] + moved[3])).astype(bf16)
        moved = [piece.astype(f32) for piece in exchange([part] * 4)]
        part = ((moved[0] + moved[1]) + (moved[2] + moved[3])).astype(bf16)
        part_list = exchange([part] * 4, PLANE)
        part_list = part_list + [swap(value, 2) for value in part_list]
        sums = pl.pallas_call(
            spread_kernel,
            in_specs=[SMEM] + [VMEM] * 8 + [ANY] * 6,
            out_specs=[ANY] * 6,
            out_shape=out_shapes,
            scratch_shapes=[
                pltpu.VMEM((LATE_ROWS + EARLY_KINDS * RANK, D), f32),
                pltpu.SemaphoreType.DMA((8 + EARLY_KINDS,)),
            ],
            input_output_aliases={9 + n: n for n in range(6)},
            name="spread",
        )(meta, *part_list, *zeros)
        return (output, grad_tokens, *sums)

    terms = jnp.concatenate([near_terms, away_terms], axis=0)
    terms = jnp.concatenate([terms[:, :RANK].reshape(-1, D), terms[:, RANK:].reshape(-1, D)], axis=0)
    slots = (jnp.arange(seq_total) == seq_number).astype(f32)[:, None, None]
    every = lax.psum(slots * terms[None], AXES)

    def spread(kinds, width):
        def term(s):
            rows = jnp.concatenate([every[s, kind * RANK : (kind + width // D) * RANK] for kind in kinds], axis=0)
            value = rows.reshape(len(kinds), width // D, RANK, D).transpose(0, 2, 1, 3)
            value = value.reshape(len(kinds), RANK, width)
            return (jnp.arange(ADAPTERS) == adapter_pick[s]).astype(f32)[:, None, None, None] * value[None]

        return functools.reduce(lambda x, y: x + y, [term(s) for s in range(seq_total)])

    wide = FF // D
    sums = [
        spread((0, 1, 2, 8), D),
        spread((3, 4, 5, 9), D),
        spread((10,), D),
        spread((11,), FF),
        spread((11 + wide,), FF),
        spread((11 + 2 * wide,), D),
    ]
    return (
        output,
        grad_tokens,
        *[value.reshape(leaf.shape) for value, leaf in zip(sums, out_shapes, strict=True)],
    )


def solution(mesh):
    rows = P(AXES, None)
    placed = (rows,) * 8 + (P(),) * 11 + (P("seq", None), P())
    return jax.shard_map(
        shards,
        mesh=mesh,
        in_specs=placed,
        out_specs=(rows, rows) + (P(),) * 6,
        check_vma=False,
    )
```

```python
import functools

import jax
import jax.numpy as jnp
from jax import lax
from jax.experimental import pallas as pl
from jax.experimental.pallas import tpu as pltpu
from jax.sharding import PartitionSpec as P

D = 768
HEADS = 12
HDIM = 64
BLOCK = 64
ADAPTERS = 8
RANK = 16
FF = 3072

PEERS = (0, 8, 16, 24)
PLANE = (0, 1, 4, 5)
GROUP_HEADS = HEADS // 4
SHARE = GROUP_HEADS * HDIM
WIDE = 256
LSE_LANE = SHARE
DEL_LANE = SHARE + 9
MASK_LANE = SHARE + 18
FLOOR = -1e30
STACK = GROUP_HEADS * BLOCK
AXES = ("seq", "head")
norm_eps = 1e-12
f32 = jnp.float32
bf16 = jnp.bfloat16
VMEM_LIMIT = 60 * 1024 * 1024


def dense_mul(left_op, right_op):
    return jnp.dot(left_op, right_op, preferred_element_type=f32)


def dense_right_t(left_op, right_op):
    return lax.dot_general(left_op, right_op, (((1,), (1,)), ((), ())), preferred_element_type=f32)


def dense_left_t(left_op, right_op):
    return lax.dot_general(left_op, right_op, (((0,), (0,)), ((), ())), preferred_element_type=f32)


def lanes(rows):
    return lax.broadcasted_iota(jnp.int32, (rows, WIDE), 1)


def head_lanes(lane, head):
    return (lane >= HDIM * head) & (lane < HDIM * (head + 1))


def part_lanes(lane, first, head):
    return (lane >= first + 3 * head) & (lane < first + 3 * head + 3)


def project_rows(raw, u_ref):
    lane = lanes(raw.shape[0])
    data = lane < SHARE

    def part(j):
        piece = raw[:, WIDE * j : WIDE * (j + 1)]
        return (piece + dense_mul(piece[:, WIDE // 2 :].astype(bf16), u_ref[j])).astype(bf16).astype(f32)

    query = jnp.where(data, part(0) * 0.125, jnp.where(lane == MASK_LANE, 1.0, 0.0)).astype(bf16)
    return query, jnp.concatenate([part(1)[:, :SHARE], part(2)[:, :SHARE]], axis=1).astype(bf16)


def widen_pair(pair, position, seq_length):
    lane = lanes(pair.shape[0])
    data = lane < SHARE
    blank = jnp.zeros((pair.shape[0], WIDE - SHARE), bf16)
    key = jnp.concatenate([pair[:, :SHARE], blank], axis=1)
    value = jnp.concatenate([pair[:, SHARE:], blank], axis=1)
    mask = jnp.where(position < seq_length, 0.0, FLOOR)
    key_side = jnp.where(lane < DEL_LANE, 1.0, jnp.where(lane == MASK_LANE, mask, 0.0)).astype(bf16)
    value_side = jnp.where((lane >= DEL_LANE) & (lane < MASK_LANE), 1.0, 0.0).astype(bf16)
    return jnp.where(data, key, key_side), jnp.where(data, value, value_side)


def slab_offset(n, place, fast):
    if not fast:
        return (n & 7) | ((n >> 3) << 5)
    core = (place >> 1) & 1
    near = 4 - 3 * core if n < 4 else 1 + 3 * core
    return (0, near, 5 - near, 5)[n % 4] ^ (2 * (n // 4))


def slab_row(offset):
    return (offset & 7) | ((offset >> 5) << 3)


def plane_quarter(place):
    return (place & 1) | ((place >> 1) & 2)


def rand_at(fast, rand_ref, block, r):
    if not fast:
        return rand_ref[block * 3 + r]
    return rand_ref[(block // 4) * 2, WIDE // 4 + (block & 3) * 3 + r]


def pack_kernel(rand_ref, query_ref, key_ref, value_ref, output_ref, inner_ref, outer_ref, late_ref, *slice_refs):
    slab = query_ref.shape[0]
    group = ((lax.axis_index("seq") * lax.axis_size("head") + lax.axis_index("head")) >> 3) & 3
    late_ref[:, :D] = output_ref[...]
    late_ref[:, D : D + FF] = inner_ref[...]
    outer = outer_ref[...].astype(f32)
    for c in range(FF // D):
        late_ref[:, D + FF + D * c : D + FF + D * (c + 1)] = outer[slab * c : slab * (c + 1)].astype(bf16)
    spare = (slab, WIDE - SHARE)
    lane = lax.broadcasted_iota(jnp.int32, spare, 1)
    marks = jnp.zeros(spare, f32)
    for n in range(12):
        marks = jnp.where(lane == n, rand_ref[n // 3, n % 3].astype(f32), marks)
    marks = jnp.where(lax.broadcasted_iota(jnp.int32, spare, 0) == 0, marks, 0.0)
    sources = [ref[...].astype(f32) for ref in (query_ref, key_ref, value_ref)]
    for p in range(4):
        pieces = []
        for source in sources:
            mine = source[:, :SHARE]
            for g in range(1, 4):
                mine = jnp.where((group ^ p) == g, source[:, SHARE * g : SHARE * (g + 1)], mine)
            pieces += [mine, marks]
        slice_refs[p][...] = jnp.concatenate(pieces, axis=1).astype(bf16)


def put_tokens(fast, token_refs, tok_ref):
    rows = 2 * BLOCK
    if fast:
        own, far, near = token_refs
        parts = [own[...], near[:rows, :], far[...], near[rows:, :]]
    else:
        parts = [ref[...] for ref in token_refs]
    for a in range(4):
        tok_ref[rows * a : rows * (a + 1), :] = parts[a]


def project_kernel(fast, meta_ref, down_ref, up_ref, *refs):
    count = 3 if fast else 4
    tok_refs, refs = refs[:count], refs[count:]
    w_refs, (w_ref, down_stack_ref, up_stack_ref, q_ref, pair_ref, rand_ref, u_ref, tok_ref, wide_ref) = refs[:-9], refs[-9:]
    place = meta_ref[0]
    group = meta_ref[2]
    chosen = meta_ref[3]
    half = WIDE // 2
    lead = WIDE // 4
    rand_ref[...] = jnp.zeros_like(rand_ref)
    if fast:
        slab = D // 32
        for n, piece in enumerate(w_refs):
            rows = piece[...].astype(f32)
            for a in range(4):
                device = place ^ slab_offset(n, place, fast) ^ PEERS[a]
                wide_ref[pl.ds(pl.multiple_of(device * slab, 8), slab), :] = rows[slab * a : slab * (a + 1)]
                rand_ref[pl.ds(device, 1), :] = rows[slab * a : slab * a + 1, half:WIDE].astype(jnp.int32)
    else:
        wide_ref[...] = w_refs[0][...].astype(f32)
    own = lax.broadcasted_iota(jnp.int32, (D, half), 1) < lead
    above = jnp.zeros((lead, D), f32)
    below = jnp.zeros((half - lead - RANK, D), f32)
    side = jnp.zeros((RANK, WIDE - SHARE), f32)
    downs = []
    ups = []
    for j in range(3):
        low = slice(WIDE * j, WIDE * j + half)
        high = slice(WIDE * j + half, WIDE * (j + 1))
        turned = jnp.concatenate([above, down_ref[chosen, j].astype(f32), below], axis=0).T
        w_ref[:, low] = wide_ref[:, low].astype(bf16)
        w_ref[:, high] = jnp.where(own, wide_ref[:, high], turned).astype(bf16)
        up = up_ref[chosen, j].astype(f32)
        mine = jnp.zeros((RANK, SHARE), f32)
        for g in range(4):
            mine = mine + jnp.where(group == g, up[:, SHARE * g : SHARE * (g + 1)], 0.0)
        mine = jnp.concatenate([mine, side], axis=1)
        u_ref[j] = jnp.concatenate([above[:, :WIDE], mine, below[:, :WIDE]], axis=0).astype(bf16)
        downs.append(down_ref[chosen, j].astype(f32))
        ups.append(jnp.concatenate([mine if n == j else jnp.zeros_like(mine) for n in range(3)], axis=1))
    rest = jnp.zeros((half - 3 * RANK, D), f32)
    down_stack_ref[...] = jnp.concatenate(downs + [rest], axis=0).astype(bf16)
    up_stack_ref[...] = jnp.concatenate(ups + [rest], axis=0).astype(bf16)
    put_tokens(fast, tok_refs, tok_ref)
    q_ref[...], pair_ref[...] = project_rows(dense_mul(tok_ref[...], w_ref[...]), u_ref)


def block_rows(ref, block, count=1):
    return ref[pl.ds(pl.multiple_of(block * BLOCK, BLOCK), count * BLOCK), :]


def merge_heads(stacked):
    lane = lanes(BLOCK)
    total = jnp.zeros((BLOCK, WIDE), f32)
    for head in range(GROUP_HEADS):
        total = jnp.where(head_lanes(lane, head), stacked[BLOCK * head : BLOCK * (head + 1)], total)
    return total


def key_set(ref, picks, block, block_total, fill):
    own = block_rows(ref, block)
    left = block_rows(ref, jnp.maximum(block - 1, 0))
    right = block_rows(ref, jnp.minimum(block + 1, block_total - 1))
    if fill:
        blank = jnp.where(lanes(BLOCK) == MASK_LANE, FLOOR, 0.0).astype(bf16)
        left = jnp.where(block - 1 >= 2, left, blank)
        right = jnp.where(block + 1 < block_total, right, blank)
    rand = [block_rows(ref, pick) for pick in picks]
    return jnp.concatenate([own, left, right, block_rows(ref, 0, 2)] + rand, axis=0)


def own_block(place, t):
    return 2 * (place ^ PEERS[t // 2]) + t % 2


def attend_kernel(fast, meta_ref, rand_ref, q_ref, *refs):
    slab_refs, (k_ref, v_ref, *ctx_refs, aux_ref, s_ref) = refs[:-8], refs[-8:]
    place = meta_ref[0]
    piece = 2 * BLOCK
    for n, slab_ref in enumerate(slab_refs):
        for a in range(4):
            device = place ^ slab_offset(n, place, fast) ^ PEERS[a]
            here = pl.ds(pl.multiple_of(device * piece, piece), piece)
            position = device * piece + lax.broadcasted_iota(jnp.int32, (piece, WIDE), 0)
            k_ref[here, :], v_ref[here, :] = widen_pair(
                slab_ref[piece * a : piece * (a + 1), :], position, meta_ref[1]
            )
    total_rows = k_ref.shape[0]
    block_total = total_rows // BLOCK
    chunks = total_rows // (8 * BLOCK)

    def queries(t):
        rows = q_ref[pl.ds(t * BLOCK, BLOCK), :]
        lane = lanes(BLOCK)
        blank = jnp.zeros_like(rows)
        return jnp.concatenate(
            [
                jnp.where(head_lanes(lane, head) | (lane == MASK_LANE), rows, blank)
                for head in range(GROUP_HEADS)
            ],
            axis=0,
        )

    def finish(t, low, exact, top, total):
        lane = lanes(BLOCK)
        rows = pl.ds(t * BLOCK, BLOCK)
        ctx_refs[t // 2][pl.ds((t % 2) * BLOCK, BLOCK), :] = merge_heads(low).astype(bf16)
        aux = merge_heads(exact)
        lse = top + jnp.log(total)
        for head in range(GROUP_HEADS):
            aux = jnp.where(lane == LSE_LANE + head, lse[BLOCK * head : BLOCK * (head + 1)], aux)
        aux_ref[rows, :] = aux

    def split(probs):
        low = probs.astype(bf16)
        return low, (probs - low.astype(f32)).astype(bf16)

    def sparse(t):
        block = own_block(place, t)
        picks = [rand_at(fast, rand_ref, block, r) for r in range(3)]
        scores = dense_right_t(queries(t), key_set(k_ref, picks, block, block_total, True))
        top = jnp.max(scores, axis=1, keepdims=True)
        weights = jnp.exp(scores - top)
        total = jnp.sum(weights, axis=1, keepdims=True)
        low, rest = split(weights * (1.0 / total))
        values = key_set(v_ref, picks, block, block_total, False)
        context = dense_mul(low, values)
        return context, context + dense_mul(rest, values), top, total

    for a in range(4):

        @pl.when((place ^ PEERS[a]) != 0)
        def _(a=a):
            results = [sparse(2 * a), sparse(2 * a + 1)]
            finish(2 * a, *results[0])
            finish(2 * a + 1, *results[1])

    at_once = s_ref.shape[1] // STACK

    def full(a, first):
        stack = jnp.concatenate([queries(2 * a + first + n) for n in range(at_once)], axis=0)
        height = at_once * STACK

        def score(c, state):
            top, total, tops = state
            part = dense_right_t(stack, block_rows(k_ref, c * 8, 8))
            here = jnp.max(part, axis=1, keepdims=True)
            weights = jnp.exp(part - here)
            s_ref[c] = weights
            later = jnp.maximum(top, here)
            total = total * jnp.exp(top - later) + jnp.sum(weights, axis=1, keepdims=True) * jnp.exp(here - later)
            return later, total, jnp.where(turn == c, here, tops)

        turn = lax.broadcasted_iota(jnp.int32, (height, 128), 1)
        top, total, tops = lax.fori_loop(
            0,
            chunks,
            score,
            (jnp.full((height, 1), FLOOR, f32), jnp.zeros((height, 1), f32), jnp.full((height, 128), FLOOR, f32)),
        )
        scales = jnp.exp(tops - top) * (1.0 / total)

        def mix(c, state):
            scale = jnp.sum(jnp.where(turn == c, scales, 0.0), axis=1, keepdims=True)
            low, rest = split(s_ref[c] * scale)
            values = block_rows(v_ref, c * 8, 8)
            return (state[0] + dense_mul(low, values), state[1] + dense_mul(rest, values))

        zero = jnp.zeros((height, WIDE), f32)
        context, rest = lax.fori_loop(0, chunks, mix, (zero, zero), unroll=4)
        for n in range(at_once):
            here = slice(STACK * n, STACK * (n + 1))
            finish(2 * a + first + n, context[here], (context + rest)[here], top[here], total[here])

    for a in range(4):

        @pl.when((place ^ PEERS[a]) == 0)
        def _(a=a):
            for first in range(0, 2, at_once):
                full(a, first)


DENSE_ROWS = 96


def fold_rows(rows):
    last = rows[DENSE_ROWS:]
    beside = jnp.concatenate([last[:, HDIM * h : HDIM * (h + 1)] for h in range(GROUP_HEADS)], axis=0)
    return jnp.concatenate([rows[:DENSE_ROWS], beside], axis=1)


def unfold_rows(folded):
    beside = folded[:, SHARE:]
    count = DENSE_ROWS // GROUP_HEADS
    last = jnp.concatenate([beside[count * h : count * (h + 1)] for h in range(GROUP_HEADS)], axis=1)
    rows = jnp.concatenate([folded[:, :SHARE], last], axis=0)
    return jnp.concatenate([rows, jnp.zeros((rows.shape[0], WIDE - SHARE), rows.dtype)], axis=1)


def split_parts(value):
    high = value.astype(bf16).astype(f32)
    middle = (value - high).astype(bf16).astype(f32)
    return (high, middle, value - high - middle)


def delta_kernel(*refs):
    grad_refs, aux_ref, out_ref = refs[:4], refs[4], refs[5]
    rows = 2 * BLOCK
    lane = lanes(rows)
    for a in range(4):
        here = pl.ds(a * rows, rows)
        grad = unfold_rows(grad_refs[a][...]).astype(f32)
        aux = aux_ref[here, :]
        result = jnp.where(lane < SHARE, grad, 0.0)
        product = grad * aux
        for head in range(GROUP_HEADS):
            delta = jnp.sum(jnp.where(head_lanes(lane, head), product, 0.0), axis=1, keepdims=True)
            lse = jnp.sum(jnp.where(lane == LSE_LANE + head, aux, 0.0), axis=1, keepdims=True)
            for p, value in enumerate(split_parts(lse)):
                result = jnp.where(lane == LSE_LANE + 3 * head + p, -value, result)
            for p, value in enumerate(split_parts(delta)):
                result = jnp.where(lane == DEL_LANE + 3 * head + p, -value, result)
        out_ref[here, :] = result.astype(bf16)


def query_stacks(rows, grads):
    lane = lanes(BLOCK)
    blank = jnp.zeros_like(rows)
    queries = []
    outers = []
    for head in range(GROUP_HEADS):
        here = head_lanes(lane, head)
        queries.append(
            jnp.where(
                here | (lane == MASK_LANE), rows, jnp.where(part_lanes(lane, LSE_LANE, head), grads, blank)
            )
        )
        outers.append(jnp.where(here | part_lanes(lane, DEL_LANE, head), grads, blank))
    return jnp.concatenate(queries, axis=0), jnp.concatenate(outers, axis=0)


def near_kernel(fast, meta_ref, rand_ref, q_ref, k_ref, v_ref, g_ref, dq_ref, *refs):
    zero_outs, (blank_ref, sems) = refs[:-2], refs[-2:]
    place = meta_ref[0]
    block_total = k_ref.shape[0] // BLOCK
    copies = []
    if zero_outs:
        blank_ref[...] = jnp.zeros_like(blank_ref)
        for n, where in enumerate(zero_outs):
            shape = where.shape
            source = blank_ref if len(shape) == 4 else blank_ref.at[0 : shape[2] // D]
            for adapter in range(ADAPTERS):
                if len(shape) == 4:
                    copies.append((blank_ref, where.at[adapter], n))
                else:
                    for c in range(shape[2] // D):
                        copies.append((blank_ref.at[c], where.at[adapter, :, pl.ds(D * c, D)], n))
        copies = [pltpu.make_async_copy(source, where, sems.at[n]) for n, (source, where, _) in enumerate(copies)]
        for copy in copies:
            copy.start()

    def query_side(stack, outer, keys, values):
        probs = jnp.exp(dense_right_t(stack, keys))
        scored = (probs * dense_right_t(outer, values)).astype(bf16)
        return dense_mul(scored, keys)

    def place_of(a, k):
        return pl.ds(pl.multiple_of((2 * a + k) * BLOCK, BLOCK), BLOCK)

    def put_query(a, k, stacked):
        dq_ref[place_of(a, k), :] = (merge_heads(stacked) * 0.125).astype(bf16)

    def stacks(a, k):
        here = place_of(a, k)
        return query_stacks(q_ref[here, :], g_ref[here, :])

    def sparse(a, k):
        block = 2 * (place ^ (8 * a)) + k
        picks = [rand_at(fast, rand_ref, block, r) for r in range(3)]
        return query_side(
            *stacks(a, k),
            key_set(k_ref, picks, block, block_total, True),
            key_set(v_ref, picks, block, block_total, False),
        )

    def piece(a, carry):
        @pl.when((place ^ (8 * a)) != 0)
        def _():
            results = [sparse(a, 0), sparse(a, 1)]
            put_query(a, 0, results[0])
            put_query(a, 1, results[1])

        @pl.when((place ^ (8 * a)) == 0)
        def _():
            pairs = [stacks(a, 0), stacks(a, 1)]
            stack = jnp.concatenate([pair[0] for pair in pairs], axis=0)
            outer = jnp.concatenate([pair[1] for pair in pairs], axis=0)

            def add(c, total):
                return total + query_side(stack, outer, block_rows(k_ref, c * 8, 8), block_rows(v_ref, c * 8, 8))

            total = lax.fori_loop(0, block_total // 8, add, jnp.zeros((2 * STACK, WIDE), f32), unroll=2)
            put_query(a, 0, total[:STACK])
            put_query(a, 1, total[STACK:])

        return carry

    lax.fori_loop(0, 4, piece, 0)
    for copy in copies:
        copy.wait()


def collect_kernel(fast, block_total, meta_ref, rand_ref, pair_ref):
    place = meta_ref[0]

    def collect(block, count):
        for r in range(3):
            target = rand_at(fast, rand_ref, block, r)
            mine = (((target // 2) ^ place) & ~24) == 0

            @pl.when(mine)
            def _(target=target, count=count):
                pair_ref[count + 1] = target * 65536 + block

            count = count + mine.astype(jnp.int32)
        return count

    pair_ref[0] = lax.fori_loop(2, block_total, collect, jnp.int32(0))


def far_kernel(fast, meta_ref, pair_ref, k_ref, v_ref, dq_ref, w_ref, down_ref, up_ref, early_ref, *refs):
    count = 3 if fast else 4
    tok_refs, refs = refs[:count], refs[count:]
    slab_refs, refs = refs[:-11], refs[-11:]
    part_refs, near_ref, away_ref, refs = refs[:2], refs[2], refs[3], refs[4:]
    q_ref, g_ref, dk_ref, dv_ref, grad_ref, tok_ref, terms_ref = refs
    place = meta_ref[0]
    group = meta_ref[2]
    block_total = k_ref.shape[0] // BLOCK
    count = len(slab_refs) // 2
    rows = 2 * BLOCK
    for n in range(count):
        here = pl.ds(pl.multiple_of(slab_row(slab_offset(n, place, fast)) * 4 * rows, rows), 4 * rows)
        q_ref[here, :] = slab_refs[n][...]
        g_ref[here, :] = slab_refs[count + n][...]

    def stacks(blocks):
        pairs = []
        for block in blocks:
            other = (block // 2) ^ place
            where = slab_row(other) * 8 + ((other >> 3) & 3) * 2 + (block & 1)
            pairs.append(query_stacks(block_rows(q_ref, where), block_rows(g_ref, where)))
        return (
            jnp.concatenate([pair[0] for pair in pairs], axis=0),
            jnp.concatenate([pair[1] for pair in pairs], axis=0),
        )

    def key_side(keys, values, blocks, allowed):
        stack, outer = stacks(blocks)
        probs = jnp.exp(dense_right_t(keys, stack))
        if allowed is not None:
            probs = jnp.where(allowed, probs, 0.0)
        scored = (probs * dense_right_t(values, outer)).astype(bf16)
        return dense_mul(scored, stack), dense_mul(probs.astype(bf16), outer)

    def put(here, grads):
        dk_ref[here, :] += grads[0]
        dv_ref[here, :] += grads[1]

    key_local = lax.broadcasted_iota(jnp.int32, (rows, 6 * STACK), 0) // BLOCK
    turn = lax.broadcasted_iota(jnp.int32, (rows, 6 * STACK), 1) // STACK
    for a in range(4):
        first = 2 * (place ^ PEERS[a])
        here = slice(rows * a, rows * (a + 1))
        blocks = [0, 1, jnp.maximum(first - 1, 0), first, first + 1, jnp.minimum(first + 2, block_total - 1)]
        key_block = first + key_local
        block = first - 3 + turn
        near = (key_block - block <= 1) & (block - key_block <= 1) & (block >= 2) & (block < block_total)
        allowed = ((turn < 2) | near) & (key_block >= 2)
        keys = block_rows(k_ref, first, 2)
        values = block_rows(v_ref, first, 2)
        dk_ref[here, :], dv_ref[here, :] = key_side(keys, values, blocks, allowed)

    pair_total = pair_ref[0]

    def random_pairs(step, carry):
        grads = []
        for k in range(4):
            number = 4 * step + k
            live = number < pair_total
            code = pair_ref[jnp.minimum(number, pair_total - 1) + 1]
            target = code // 65536
            block = code - target * 65536
            start = ((((target // 2) ^ place) >> 3) & 3) * rows + (target & 1) * BLOCK
            grads.append(
                (
                    pl.ds(pl.multiple_of(start, BLOCK), BLOCK),
                    key_side(block_rows(k_ref, target), block_rows(v_ref, target), (block,), live),
                )
            )
        for here, parts in grads:
            put(here, parts)
        return carry

    lax.fori_loop(0, (pair_total + 3) // 4, random_pairs, 0)

    @pl.when((place & ~24) == 0)
    def _():
        here = pl.ds(pl.multiple_of(group * rows, rows), rows)
        keys = block_rows(k_ref, 0, 2)
        values = block_rows(v_ref, 0, 2)

        def every(step, carry):
            put(here, key_side(keys, values, [4 * step + k for k in range(4)], None))
            return carry

        lax.fori_loop(0, block_total // 4, every, 0, unroll=4)

    data = lanes(rows) < SHARE
    for a in range(4):
        here = slice(rows * a, rows * (a + 1))
        grad_ref[here, :WIDE] = dq_ref[here, :]
        grad_ref[here, WIDE : 2 * WIDE] = jnp.where(data, dk_ref[here, :], 0.0).astype(bf16)
        grad_ref[here, 2 * WIDE :] = jnp.where(data, dv_ref[here, :], 0.0).astype(bf16)
    put_tokens(fast, tok_refs, tok_ref)
    tokens = tok_ref[...]
    grad = grad_ref[...]
    reduced = dense_right_t(tokens, down_ref[...]).astype(bf16)
    grad_reduced = dense_right_t(grad, up_ref[...]).astype(bf16)
    down_terms = dense_left_t(grad_reduced, tokens)
    up_terms = dense_left_t(reduced, grad)
    terms = [down_terms[RANK * j : RANK * (j + 1)] for j in range(3)]
    ups = []
    for j in range(3):
        up = up_terms[RANK * j : RANK * (j + 1), WIDE * j : WIDE * j + SHARE]
        ups.append(jnp.concatenate([jnp.where(group == g, up, 0.0) for g in range(4)], axis=1))
    terms += ups + [jnp.zeros((RANK, D), f32)] * 2
    core = (place >> 1) & 1
    quarter = plane_quarter(place)
    for part, value in enumerate(terms):
        early = early_ref[EARLY_PART * part : EARLY_PART * (part + 1), :]
        where = (((part // 4) ^ core) * 4 + ((part % 4) ^ quarter)) if fast else part
        terms_ref[where, :RANK] = value
        terms_ref[where, RANK:] = early
    near_ref[...] = terms_ref[:4]
    away_ref[...] = terms_ref[4:].astype(away_ref.dtype)
    for n, a in enumerate((0, 2, 1, 3)):
        here = slice(rows * a, rows * (a + 1))
        part = (dense_right_t(grad[here], w_ref[...]) + dense_mul(grad_reduced[here], down_ref[...])).astype(bf16)
        part_refs[n // 2][rows * (n % 2) : rows * (n % 2 + 1), :] = part


def normal(hidden):
    center = hidden - jnp.mean(hidden, axis=-1, keepdims=True)
    root = lax.rsqrt(jnp.mean(center * center, axis=-1, keepdims=True) + norm_eps)
    return center * root, root


def normal_back(grad, normed, root):
    mean = jnp.mean(grad, axis=-1, keepdims=True)
    return root * (grad - mean - normed * jnp.mean(grad * normed, axis=-1, keepdims=True))


def select_kernel(meta_ref, *refs):
    chosen = meta_ref[3]
    tables, (down_ref, up_ref, *rest) = refs[:6], refs[6:]
    down_ref[...] = tables[0][chosen, 3]
    up_ref[...] = tables[1][chosen, 3]
    for table, ref in zip(tables[2:], rest, strict=True):
        ref[...] = table[chosen]


def middle_kernel(
    fast,
    meta_ref,
    ctx_refs,
    tok_ref,
    cot_ref,
    late_hbm,
    gain_ref,
    down_ref,
    up_ref,
    inner_down_ref,
    inner_up_ref,
    outer_down_ref,
    outer_up_ref,
    wide_ref,
    out_ref,
    grad_ref,
    piece_refs,
    terms_ref,
    hold_ref,
    pre_ref,
    act_ref,
    late_ref,
    sems,
):
    group = meta_ref[2]
    rows = tok_ref.shape[0]
    share = D // (FF // D)
    places = [(slice(None), slice(D * c, D * (c + 1))) for c in range(1 + FF // D)]
    if fast:
        places += [(slice(share * c, share * (c + 1)), slice(D + FF, D + 2 * FF)) for c in range(FF // D)]
    copies = [
        pltpu.make_async_copy(late_hbm.at[place], late_ref.at[place], sems.at[n]) for n, place in enumerate(places)
    ]
    order = [0] + [n for c in range(FF // D) for n in (1 + c, 1 + FF // D + c) if n < len(copies)]
    for n in order:
        copies[n].start()

    def build(c):
        copies[1 + FF // D + c].wait()
        slab = 24
        for pair in range(share // (2 * slab)):
            first = share * c + 2 * slab * pair
            block = late_ref[first : first + 2 * slab, D + FF :].astype(f32)
            cut = [
                block[slab * side : slab * (side + 1), D * n : D * (n + 1)]
                for side in range(2)
                for n in range(FF // D)
            ]
            wide_ref[4 * first : 4 * first + 8 * slab, :] = jnp.concatenate(cut, axis=0).astype(bf16)

    for a in range(4):
        hold_ref[a] = ctx_refs[a][...]
    context = jnp.concatenate([hold_ref[group ^ g][:, :SHARE] for g in range(4)], axis=1)
    context_red = dense_right_t(context, down_ref[...]).astype(bf16)
    copies[0].wait()
    attended = dense_mul(context, late_ref[:, :D]) + dense_mul(context_red, up_ref[...])
    first, first_root = normal(tok_ref[...].astype(f32) + attended)
    first_norm = first * gain_ref[0:1, :] + gain_ref[1:2, :]
    first_low = first_norm.astype(bf16)
    inner_red = dense_right_t(first_low, inner_down_ref[...]).astype(bf16)
    outer_red = jnp.zeros((rows, RANK), f32)
    outer_out = jnp.zeros((rows, D), f32)
    for c in range(FF // D):
        here = slice(D * c, D * (c + 1))
        copies[1 + c].wait()
        if fast:
            build(c)
        pre = dense_mul(first_low, late_ref[:, D * (c + 1) : D * (c + 2)]) + dense_mul(
            inner_red, inner_up_ref[:, here]
        )
        pre_ref[:, here] = pre
        active = (0.5 * pre * (1.0 + lax.erf(pre * 0.7071067811865476))).astype(bf16)
        act_ref[:, here] = active
        outer_red = outer_red + dense_right_t(active, outer_down_ref[:, here])
        outer_out = outer_out + dense_mul(active, wide_ref[here, :])
    outer_red = outer_red.astype(bf16)
    outer_out = outer_out + dense_mul(outer_red, outer_up_ref[...])
    second, second_root = normal(first_norm + outer_out)
    position = meta_ref[0] * rows + lax.broadcasted_iota(jnp.int32, (rows, D), 0)
    valid = (position < meta_ref[1]).astype(f32)
    out_ref[...] = ((second * gain_ref[2:3, :] + gain_ref[3:4, :]) * valid).astype(bf16)
    grad_second = normal_back(valid * cot_ref[...].astype(f32) * gain_ref[2:3, :], second, second_root)
    grad_outer = grad_second.astype(bf16)
    first_up = RANK * 3
    first_down = RANK * (3 + FF // D)
    terms_ref[first_down + RANK * (FF // D) :, :] = dense_left_t(outer_red, grad_outer)
    outer_grad_red = dense_right_t(grad_outer, outer_up_ref[...]).astype(bf16)
    inner_grad_red = jnp.zeros((rows, RANK), f32)
    grad_first = grad_second
    for c in range(FF // D):
        here = slice(D * c, D * (c + 1))
        grad_active = dense_right_t(grad_outer, wide_ref[here, :]) + dense_mul(
            outer_grad_red, outer_down_ref[:, here]
        )
        pre = pre_ref[:, here]
        slope = 0.5 * (1.0 + lax.erf(pre * 0.7071067811865476)) + pre * (
            0.3989422804014327 * jnp.exp(-0.5 * pre * pre)
        )
        grad_inner = (slope * grad_active).astype(bf16)
        terms_ref[first_up + RANK * c : first_up + RANK * (c + 1), :] = dense_left_t(inner_red, grad_inner)
        terms_ref[first_down + RANK * c : first_down + RANK * (c + 1), :] = dense_left_t(
            outer_grad_red, act_ref[:, here]
        )
        inner_grad_red = inner_grad_red + dense_right_t(grad_inner, inner_up_ref[:, here])
        grad_first = grad_first + dense_right_t(grad_inner, late_ref[:, D * (c + 1) : D * (c + 2)])
    inner_grad_red = inner_grad_red.astype(bf16)
    terms_ref[2 * RANK : 3 * RANK, :] = dense_left_t(inner_grad_red, first_low)
    grad_first = grad_first + dense_mul(inner_grad_red, inner_down_ref[...])
    grad_attended = normal_back(grad_first * gain_ref[0:1, :], first, first_root)
    grad_ref[...] = grad_attended
    grad_low = grad_attended.astype(bf16)
    context_grad_red = dense_right_t(grad_low, up_ref[...]).astype(bf16)
    terms_ref[:RANK, :] = dense_left_t(context_grad_red, context)
    terms_ref[RANK : 2 * RANK, :] = dense_left_t(context_red, grad_low)
    grad_context = (
        dense_right_t(grad_low, late_ref[:, :D]) + dense_mul(context_grad_red, down_ref[...])
    ).astype(bf16)
    for g in range(4):
        hold_ref[group ^ g, :DENSE_ROWS, :] = fold_rows(grad_context[:, SHARE * g : SHARE * (g + 1)])
    for a in range(4):
        piece_refs[a][...] = hold_ref[a, :DENSE_ROWS, :]


def spread_kernel(meta_ref, *refs):
    part_refs = refs[:8]
    outs = refs[14:20]
    sum_ref, sems = refs[20:]
    quarter = plane_quarter(meta_ref[0])
    core = (meta_ref[0] >> 1) & 1
    chosen = meta_ref[3]
    for n in range(8):
        part = (core ^ (n // 4)) * 4 + (quarter ^ (n % 4))
        sum_ref[pl.ds(pl.multiple_of(part * RANK, RANK), RANK), :] = part_refs[n][:RANK, :].astype(f32)
        sum_ref[pl.ds(pl.multiple_of(LATE_ROWS + part * EARLY_PART, 8), EARLY_PART), :] = part_refs[n][RANK:, :].astype(f32)
    places = [outs[0].at[chosen, j] for j in range(3)] + [outs[1].at[chosen, j] for j in range(3)]
    places += [None, None, outs[0].at[chosen, 3], outs[1].at[chosen, 3], outs[2].at[chosen]]
    places += [outs[n].at[chosen, :, pl.ds(D * c, D)] for n in (3, 4) for c in range(FF // D)]
    places.append(outs[5].at[chosen])
    copies = [
        pltpu.make_async_copy(sum_ref.at[pl.ds(RANK * n, RANK), :], where, sems.at[n])
        for n, where in enumerate(places)
        if where is not None
    ]
    for copy in copies:
        copy.start()
    for copy in copies:
        copy.wait()


LATE_ROWS = 8 * RANK
EARLY_KINDS = 12
EARLY_PART = EARLY_KINDS * RANK // 8
ANY = pl.BlockSpec(memory_space=pl.ANY)
SMEM = pl.BlockSpec(memory_space=pltpu.SMEM)
VMEM = pl.BlockSpec(memory_space=pltpu.VMEM)


def shards(
    tokens,
    cotangent,
    w_query,
    w_key,
    w_value,
    w_output,
    w_inner,
    w_outer,
    gain_first,
    shift_first,
    gain_second,
    shift_second,
    attn_down,
    attn_up,
    inner_down,
    inner_up,
    outer_down,
    outer_up,
    lengths,
    rand_blocks,
    adapter_pick,
):
    device_total = lax.axis_size("seq") * lax.axis_size("head")
    local_rows = tokens.shape[0]
    seq_total = lengths.shape[0]
    members = device_total // seq_total
    rows_total = members * local_rows
    block_total = rows_total // BLOCK
    chunk = 4 * local_rows
    index = lax.axis_index("seq") * lax.axis_size("head") + lax.axis_index("head")
    place = index % members
    seq_number = index // members
    group = (place >> 3) & 3
    seq_length = lengths[seq_number]
    chosen = adapter_pick[seq_number]
    fast = device_total == 32 and members == 32
    together = lax.optimization_barrier

    def send(value, even, odd):
        return lax.ppermute(
            value, AXES, [(j, j ^ (odd if (j >> 1) & 1 else even)) for j in range(device_total)]
        )

    def swap(value, mask):
        return send(value, mask, mask)

    def one(value):
        return send(value, 4, 1)

    def two(value):
        return send(value, 1, 4)

    def exchange(pieces, masks=PEERS):
        return [pieces[0]] + [swap(pieces[a], masks[a]) for a in range(1, 4)]

    def gather_start(value):
        if not fast:
            masks = [slab_offset(n, place, False) for n in range(members // 4)]
            return [value] + [swap(value, mask) for mask in masks[1:]]
        return [value, one(value), two(value)]

    def gather_end(slabs):
        if not fast:
            return slabs
        slabs = slabs + [two(slabs[1])]
        return slabs + [swap(slab, 2) for slab in slabs]

    def gather_direct(value):
        return gather_start(value) + ([swap(value, 5)] if fast else [])

    def gather_hand(slabs):
        return slabs + [swap(slab, 2) for slab in slabs] if fast else slabs

    def gather_all(value):
        return lax.all_gather(value, AXES, axis=0, tiled=True)

    def share_columns(table, which=group):
        return lax.dynamic_slice_in_dim(table, which * SHARE, SHARE, table.ndim - 1)

    slab = D // device_total
    meta = jnp.stack([place, seq_length, group, chosen]).astype(jnp.int32)
    if fast:
        late_local, *slices = pl.pallas_call(
            pack_kernel,
            in_specs=[SMEM] + [VMEM] * 6,
            out_specs=[VMEM] * 5,
            out_shape=[jax.ShapeDtypeStruct((slab, D + 2 * FF), bf16)]
            + [jax.ShapeDtypeStruct((slab, 3 * WIDE), bf16)] * 4,
            name="pack",
        )(rand_blocks, w_query, w_key, w_value, w_output, w_inner, w_outer)
        late = gather_all(late_local)
        mine = exchange(slices)
        far_tokens = swap(tokens, PEERS[2])
        near_tokens = swap(jnp.concatenate([tokens, far_tokens], axis=0), PEERS[1])
        token_refs = [tokens, far_tokens, near_tokens]
        w_slabs = gather_hand(gather_direct(jnp.concatenate(mine, axis=0)))
    else:
        late = gather_all(
            jnp.concatenate([w_output, w_inner] + [w_outer[slab * c : slab * (c + 1)] for c in range(FF // D)], axis=1)
        )
        full_qkv = gather_all(jnp.concatenate([w_query, w_key, w_value], axis=1))
        rand_all = lax.all_gather(rand_blocks, "seq", axis=0, tiled=True)
        rand_flat = lax.dynamic_slice_in_dim(rand_all, seq_number * block_total, block_total, 0).reshape(-1)
        token_refs = exchange([tokens] * 4)
        w_slabs = [
            jnp.concatenate(
                [
                    jnp.pad(share_columns(full_qkv[:, D * j : D * (j + 1)]), ((0, 0), (0, WIDE - SHARE)))
                    for j in range(3)
                ],
                axis=1,
            )
        ]

    wide_rows = jax.ShapeDtypeStruct((rows_total, WIDE), bf16)
    piece_shapes = [jax.ShapeDtypeStruct((local_rows, WIDE), bf16)] * 4
    side_weight, down_stack, up_stack, query_own, pair_own, rand_table = pl.pallas_call(
        functools.partial(project_kernel, fast),
        in_specs=[SMEM] + [VMEM] * (2 + len(token_refs) + len(w_slabs)),
        out_specs=[VMEM] * 6,
        out_shape=[
            jax.ShapeDtypeStruct((D, 3 * WIDE), bf16),
            jax.ShapeDtypeStruct((WIDE // 2, D), bf16),
            jax.ShapeDtypeStruct((WIDE // 2, 3 * WIDE), bf16),
            jax.ShapeDtypeStruct((chunk, WIDE), bf16),
            jax.ShapeDtypeStruct((chunk, 2 * SHARE), bf16),
            jax.ShapeDtypeStruct((32, WIDE // 2), jnp.int32),
        ],
        scratch_shapes=[
            pltpu.VMEM((3, WIDE // 2, WIDE), bf16),
            pltpu.VMEM((chunk, D), bf16),
            pltpu.VMEM((D, 3 * WIDE), f32),
        ],
        compiler_params=pltpu.CompilerParams(vmem_limit_bytes=VMEM_LIMIT),
        name="project",
    )(meta, attn_down, attn_up, *token_refs, *w_slabs)
    if fast:
        rand_flat = rand_table
    pair_list = pl.pallas_call(
        functools.partial(collect_kernel, fast, block_total),
        in_specs=[SMEM, SMEM],
        out_specs=SMEM,
        out_shape=jax.ShapeDtypeStruct((3 * block_total + 8,), jnp.int32),
        name="collect",
    )(meta, rand_flat)
    pair_slabs = gather_start(pair_own)
    pair_list, pair_slabs[1] = together((pair_list, pair_slabs[1]))
    pair_slabs = gather_end(pair_slabs)
    key_all, value_all, *ctx, aux = pl.pallas_call(
        functools.partial(attend_kernel, fast),
        in_specs=[SMEM, SMEM] + [VMEM] * (1 + len(pair_slabs)),
        out_specs=[VMEM] * 7,
        out_shape=[wide_rows] * 2 + piece_shapes + [jax.ShapeDtypeStruct((chunk, WIDE), f32)],
        scratch_shapes=[pltpu.VMEM((rows_total // chunk, (2 if fast else 1) * STACK, chunk), f32)],
        compiler_params=pltpu.CompilerParams(vmem_limit_bytes=VMEM_LIMIT),
        name="attend",
    )(meta, rand_flat, query_own, *pair_slabs)
    *tables, ctx[1] = together((attn_down, attn_up, inner_down, inner_up, outer_down, outer_up, ctx[1]))
    ctx_pieces = exchange(ctx)

    gains = jnp.stack([gain_first, shift_first, gain_second, shift_second])
    chosen_maps = pl.pallas_call(
        select_kernel,
        in_specs=[SMEM] + [VMEM] * 6,
        out_specs=[VMEM] * 6,
        out_shape=[jax.ShapeDtypeStruct((RANK, width), bf16) for width in (D, D, D, FF, FF, D)],
        name="select",
    )(meta, *tables)
    *chosen_maps, late = together((*chosen_maps, late))
    middle_in = [tokens, cotangent, late, gains, *chosen_maps]
    wide_shape = [pltpu.VMEM((FF, D), bf16)]
    if not fast:
        middle_in.append(
            late[:, D + FF :].reshape(device_total, slab, FF // D, D).transpose(0, 2, 1, 3).reshape(FF, D)
        )
        wide_shape = []
    count = len(middle_in)

    def middle(meta_ref, *refs):
        ins, outs, scratch = refs[4 : 4 + count], refs[4 + count : 11 + count], refs[11 + count :]
        wide_ref = scratch[-1] if fast else ins[-1]
        middle_kernel(
            fast, meta_ref, refs[:4], *ins[:10], wide_ref, *outs[:2], outs[2:6], outs[6], *scratch[:5]
        )


    output, grad_attended, *grad_pieces, early_terms = pl.pallas_call(
        middle,
        in_specs=[SMEM] + [VMEM] * 6 + [ANY] + [VMEM] * (count - 3),
        out_specs=[VMEM] * 7,
        out_shape=[
            jax.ShapeDtypeStruct((local_rows, D), bf16),
            jax.ShapeDtypeStruct((local_rows, D), f32),
        ]
        + [jax.ShapeDtypeStruct((DENSE_ROWS, WIDE), bf16)] * 4
        + [jax.ShapeDtypeStruct((EARLY_KINDS * RANK, D), f32)],
        scratch_shapes=[
            pltpu.VMEM((4, local_rows, WIDE), bf16),
            pltpu.VMEM((local_rows, FF), f32),
            pltpu.VMEM((local_rows, FF), bf16),
            pltpu.VMEM(late.shape, bf16),
            pltpu.SemaphoreType.DMA((1 + 2 * (FF // D),)),
        ]
        + wide_shape,
        compiler_params=pltpu.CompilerParams(vmem_limit_bytes=VMEM_LIMIT),
        name="middle",
    )(meta, *ctx_pieces, *middle_in)
    query_send, grad_pieces[0] = together((query_own, grad_pieces[0]))
    query_slabs = gather_hand(gather_direct(query_send))
    grad_wide = pl.pallas_call(
        delta_kernel,
        in_specs=[VMEM] * 5,
        out_specs=VMEM,
        out_shape=jax.ShapeDtypeStruct((chunk, WIDE), bf16),
        name="delta",
    )(*exchange(grad_pieces), aux)
    def reduced(terms):
        paired = terms[0] + swap(terms[1], 2)
        moved = exchange([paired[a] for a in range(4)])
        part = (moved[0] + moved[1]) + (moved[2] + moved[3])
        moved = [part] + [swap(part, depth) for depth in DEPTHS[1:]]
        return (moved[0] + moved[1]) + (moved[2] + moved[3])

    grad_slabs = gather_start(grad_wide)
    out_shapes = [
        jax.ShapeDtypeStruct(shape, f32)
        for shape in (
            (ADAPTERS, 4, RANK, D),
            (ADAPTERS, 4, RANK, D),
            (ADAPTERS, RANK, D),
            (ADAPTERS, RANK, FF),
            (ADAPTERS, RANK, FF),
            (ADAPTERS, RANK, D),
        )
    ]
    zero_shapes = out_shapes if fast else []
    query_grad, *zeros = pl.pallas_call(
        functools.partial(near_kernel, fast),
        in_specs=[SMEM, SMEM] + [VMEM] * 4,
        out_specs=[VMEM] + [ANY] * len(zero_shapes),
        out_shape=[jax.ShapeDtypeStruct((chunk, WIDE), bf16)] + zero_shapes,
        scratch_shapes=[pltpu.VMEM((4, RANK, D), f32), pltpu.SemaphoreType.DMA((ADAPTERS * 12,))],
        compiler_params=pltpu.CompilerParams(vmem_limit_bytes=VMEM_LIMIT),
        cost_estimate=pl.CostEstimate(flops=12000000000, bytes_accessed=8000000, transcendentals=1000000),
        name="near",
    )(meta, rand_flat, query_own, key_all, value_all, grad_wide)
    query_grad, *grad_slabs = together((query_grad, *grad_slabs))
    grad_slabs = gather_end(grad_slabs)
    kept, given, near_terms, away_terms = pl.pallas_call(
        functools.partial(far_kernel, fast),
        in_specs=[SMEM, SMEM] + [VMEM] * (7 + len(token_refs) + 2 * len(grad_slabs)),
        out_specs=[VMEM] * 4,
        out_shape=[jax.ShapeDtypeStruct((2 * local_rows, D), bf16)] * 2
        + [jax.ShapeDtypeStruct((4, RANK + EARLY_PART, D), kind) for kind in (f32, bf16 if fast else f32)],
        scratch_shapes=[
            pltpu.VMEM((rows_total, WIDE), bf16),
            pltpu.VMEM((rows_total, WIDE), bf16),
            pltpu.VMEM((chunk, WIDE), f32),
            pltpu.VMEM((chunk, WIDE), f32),
            pltpu.VMEM((chunk, 3 * WIDE), bf16),
            pltpu.VMEM((chunk, D), bf16),
            pltpu.VMEM((8, RANK + EARLY_PART, D), f32),
        ],
        compiler_params=pltpu.CompilerParams(vmem_limit_bytes=VMEM_LIMIT),
        name="far",
    )(
        meta,
        pair_list,
        key_all,
        value_all,
        query_grad,
        side_weight,
        down_stack,
        up_stack,
        early_terms,
        *token_refs,
        *query_slabs,
        *grad_slabs,
    )
    kept = kept.astype(f32) + swap(given, PEERS[1]).astype(f32)
    passed = swap(kept[local_rows:].astype(bf16), PEERS[2])
    grad_tokens = grad_attended + (kept[:local_rows] + passed.astype(f32))

    if fast:
        paired = near_terms + swap(away_terms, 2).astype(f32)
        moved = [paired[0]] + [swap(paired[a].astype(bf16), PLANE[a]).astype(f32) for a in range(1, 4)]
        part = ((moved[0] + moved[1]) + (moved[2] + moved[3])).astype(bf16)
        moved = [piece.astype(f32) for piece in exchange([part] * 4)]
        part = ((moved[0] + moved[1]) + (moved[2] + moved[3])).astype(bf16)
        part_list = exchange([part] * 4, PLANE)
        part_list = part_list + [swap(value, 2) for value in part_list]
        sums = pl.pallas_call(
            spread_kernel,
            in_specs=[SMEM] + [VMEM] * 8 + [ANY] * 6,
            out_specs=[ANY] * 6,
            out_shape=out_shapes,
            scratch_shapes=[
                pltpu.VMEM((LATE_ROWS + EARLY_KINDS * RANK, D), f32),
                pltpu.SemaphoreType.DMA((8 + EARLY_KINDS,)),
            ],
            input_output_aliases={9 + n: n for n in range(6)},
            name="spread",
        )(meta, *part_list, *zeros)
        return (output, grad_tokens, *sums)

    terms = jnp.concatenate([near_terms, away_terms], axis=0)
    terms = jnp.concatenate([terms[:, :RANK].reshape(-1, D), terms[:, RANK:].reshape(-1, D)], axis=0)
    slots = (jnp.arange(seq_total) == seq_number).astype(f32)[:, None, None]
    every = lax.psum(slots * terms[None], AXES)

    def spread(kinds, width):
        def term(s):
            rows = jnp.concatenate([every[s, kind * RANK : (kind + width // D) * RANK] for kind in kinds], axis=0)
            value = rows.reshape(len(kinds), width // D, RANK, D).transpose(0, 2, 1, 3)
            value = value.reshape(len(kinds), RANK, width)
            return (jnp.arange(ADAPTERS) == adapter_pick[s]).astype(f32)[:, None, None, None] * value[None]

        return functools.reduce(lambda x, y: x + y, [term(s) for s in range(seq_total)])

    wide = FF // D
    sums = [
        spread((0, 1, 2, 8), D),
        spread((3, 4, 5, 9), D),
        spread((10,), D),
        spread((11,), FF),
        spread((11 + wide,), FF),
        spread((11 + 2 * wide,), D),
    ]
    return (
        output,
        grad_tokens,
        *[value.reshape(leaf.shape) for value, leaf in zip(sums, out_shapes, strict=True)],
    )


def solution(mesh):
    rows = P(AXES, None)
    placed = (rows,) * 8 + (P(),) * 11 + (P("seq", None), P())
    return jax.shard_map(
        shards,
        mesh=mesh,
        in_specs=placed,
        out_specs=(rows, rows) + (P(),) * 6,
        check_vma=False,
    )
```

```python
import functools

import jax
import jax.numpy as jnp
from jax import lax
from jax.experimental import pallas as pl
from jax.experimental.pallas import tpu as pltpu
from jax.sharding import PartitionSpec as P

D = 768
HEADS = 12
HDIM = 64
BLOCK = 64
ADAPTERS = 8
RANK = 16
FF = 3072

PEERS = (0, 8, 16, 24)
PLANE = (0, 1, 4, 5)
GROUP_HEADS = HEADS // 4
SHARE = GROUP_HEADS * HDIM
WIDE = 256
LSE_LANE = SHARE
DEL_LANE = SHARE + 9
MASK_LANE = SHARE + 18
FLOOR = -1e30
STACK = GROUP_HEADS * BLOCK
AXES = ("seq", "head")
norm_eps = 1e-12
f32 = jnp.float32
bf16 = jnp.bfloat16
VMEM_LIMIT = 60 * 1024 * 1024


def dense_mul(left_op, right_op):
    return jnp.dot(left_op, right_op, preferred_element_type=f32)


def dense_right_t(left_op, right_op):
    return lax.dot_general(left_op, right_op, (((1,), (1,)), ((), ())), preferred_element_type=f32)


def dense_left_t(left_op, right_op):
    return lax.dot_general(left_op, right_op, (((0,), (0,)), ((), ())), preferred_element_type=f32)


def lanes(rows):
    return lax.broadcasted_iota(jnp.int32, (rows, WIDE), 1)


def head_lanes(lane, head):
    return (lane >= HDIM * head) & (lane < HDIM * (head + 1))


def part_lanes(lane, first, head):
    return (lane >= first + 3 * head) & (lane < first + 3 * head + 3)


def project_rows(raw, u_ref):
    lane = lanes(raw.shape[0])
    data = lane < SHARE

    def part(j):
        piece = raw[:, WIDE * j : WIDE * (j + 1)]
        return (piece + dense_mul(piece[:, WIDE // 2 :].astype(bf16), u_ref[j])).astype(bf16).astype(f32)

    query = jnp.where(data, part(0) * 0.125, jnp.where(lane == MASK_LANE, 1.0, 0.0)).astype(bf16)
    return query, jnp.concatenate([part(1)[:, :SHARE], part(2)[:, :SHARE]], axis=1).astype(bf16)


def widen_pair(pair, position, seq_length):
    lane = lanes(pair.shape[0])
    data = lane < SHARE
    blank = jnp.zeros((pair.shape[0], WIDE - SHARE), bf16)
    key = jnp.concatenate([pair[:, :SHARE], blank], axis=1)
    value = jnp.concatenate([pair[:, SHARE:], blank], axis=1)
    mask = jnp.where(position < seq_length, 0.0, FLOOR)
    key_side = jnp.where(lane < DEL_LANE, 1.0, jnp.where(lane == MASK_LANE, mask, 0.0)).astype(bf16)
    value_side = jnp.where((lane >= DEL_LANE) & (lane < MASK_LANE), 1.0, 0.0).astype(bf16)
    return jnp.where(data, key, key_side), jnp.where(data, value, value_side)


def slab_offset(n, place, fast):
    if not fast:
        return (n & 7) | ((n >> 3) << 5)
    core = (place >> 1) & 1
    near = 4 - 3 * core if n < 4 else 1 + 3 * core
    return (0, near, 5 - near, 5)[n % 4] ^ (2 * (n // 4))


def slab_row(offset):
    return (offset & 7) | ((offset >> 5) << 3)


def plane_quarter(place):
    return (place & 1) | ((place >> 1) & 2)


def rand_at(fast, rand_ref, block, r):
    if not fast:
        return rand_ref[block * 3 + r]
    return rand_ref[(block // 4) * 2, WIDE // 4 + (block & 3) * 3 + r]


def pack_kernel(rand_ref, query_ref, key_ref, value_ref, output_ref, inner_ref, outer_ref, late_ref, *slice_refs):
    slab = query_ref.shape[0]
    group = ((lax.axis_index("seq") * lax.axis_size("head") + lax.axis_index("head")) >> 3) & 3
    late_ref[:, :D] = output_ref[...]
    late_ref[:, D : D + FF] = inner_ref[...]
    outer = outer_ref[...].astype(f32)
    for c in range(FF // D):
        late_ref[:, D + FF + D * c : D + FF + D * (c + 1)] = outer[slab * c : slab * (c + 1)].astype(bf16)
    spare = (slab, WIDE - SHARE)
    lane = lax.broadcasted_iota(jnp.int32, spare, 1)
    marks = jnp.zeros(spare, f32)
    for n in range(12):
        marks = jnp.where(lane == n, rand_ref[n // 3, n % 3].astype(f32), marks)
    marks = jnp.where(lax.broadcasted_iota(jnp.int32, spare, 0) == 0, marks, 0.0)
    sources = [ref[...].astype(f32) for ref in (query_ref, key_ref, value_ref)]
    for p in range(4):
        pieces = []
        for source in sources:
            mine = source[:, :SHARE]
            for g in range(1, 4):
                mine = jnp.where((group ^ p) == g, source[:, SHARE * g : SHARE * (g + 1)], mine)
            pieces += [mine, marks]
        slice_refs[p][...] = jnp.concatenate(pieces, axis=1).astype(bf16)


def put_tokens(fast, token_refs, tok_ref):
    rows = 2 * BLOCK
    if fast:
        own, far, near = token_refs
        parts = [own[...], near[:rows, :], far[...], near[rows:, :]]
    else:
        parts = [ref[...] for ref in token_refs]
    for a in range(4):
        tok_ref[rows * a : rows * (a + 1), :] = parts[a]


def project_kernel(fast, meta_ref, down_ref, up_ref, *refs):
    count = 3 if fast else 4
    tok_refs, refs = refs[:count], refs[count:]
    w_refs, (w_ref, down_stack_ref, up_stack_ref, q_ref, pair_ref, rand_ref, u_ref, tok_ref, wide_ref) = refs[:-9], refs[-9:]
    place = meta_ref[0]
    group = meta_ref[2]
    chosen = meta_ref[3]
    half = WIDE // 2
    lead = WIDE // 4
    rand_ref[...] = jnp.zeros_like(rand_ref)
    if fast:
        slab = D // 32
        for n, piece in enumerate(w_refs):
            rows = piece[...].astype(f32)
            for a in range(4):
                device = place ^ slab_offset(n, place, fast) ^ PEERS[a]
                wide_ref[pl.ds(pl.multiple_of(device * slab, 8), slab), :] = rows[slab * a : slab * (a + 1)]
                rand_ref[pl.ds(device, 1), :] = rows[slab * a : slab * a + 1, half:WIDE].astype(jnp.int32)
    else:
        wide_ref[...] = w_refs[0][...].astype(f32)
    own = lax.broadcasted_iota(jnp.int32, (D, half), 1) < lead
    above = jnp.zeros((lead, D), f32)
    below = jnp.zeros((half - lead - RANK, D), f32)
    side = jnp.zeros((RANK, WIDE - SHARE), f32)
    downs = []
    ups = []
    for j in range(3):
        low = slice(WIDE * j, WIDE * j + half)
        high = slice(WIDE * j + half, WIDE * (j + 1))
        turned = jnp.concatenate([above, down_ref[chosen, j].astype(f32), below], axis=0).T
        w_ref[:, low] = wide_ref[:, low].astype(bf16)
        w_ref[:, high] = jnp.where(own, wide_ref[:, high], turned).astype(bf16)
        up = up_ref[chosen, j].astype(f32)
        mine = jnp.zeros((RANK, SHARE), f32)
        for g in range(4):
            mine = mine + jnp.where(group == g, up[:, SHARE * g : SHARE * (g + 1)], 0.0)
        mine = jnp.concatenate([mine, side], axis=1)
        u_ref[j] = jnp.concatenate([above[:, :WIDE], mine, below[:, :WIDE]], axis=0).astype(bf16)
        downs.append(down_ref[chosen, j].astype(f32))
        ups.append(jnp.concatenate([mine if n == j else jnp.zeros_like(mine) for n in range(3)], axis=1))
    rest = jnp.zeros((half - 3 * RANK, D), f32)
    down_stack_ref[...] = jnp.concatenate(downs + [rest], axis=0).astype(bf16)
    up_stack_ref[...] = jnp.concatenate(ups + [rest], axis=0).astype(bf16)
    put_tokens(fast, tok_refs, tok_ref)
    q_ref[...], pair_ref[...] = project_rows(dense_mul(tok_ref[...], w_ref[...]), u_ref)


def block_rows(ref, block, count=1):
    return ref[pl.ds(pl.multiple_of(block * BLOCK, BLOCK), count * BLOCK), :]


def merge_heads(stacked):
    lane = lanes(BLOCK)
    total = jnp.zeros((BLOCK, WIDE), f32)
    for head in range(GROUP_HEADS):
        total = jnp.where(head_lanes(lane, head), stacked[BLOCK * head : BLOCK * (head + 1)], total)
    return total


def key_set(ref, picks, block, block_total, fill):
    own = block_rows(ref, block)
    left = block_rows(ref, jnp.maximum(block - 1, 0))
    right = block_rows(ref, jnp.minimum(block + 1, block_total - 1))
    if fill:
        blank = jnp.where(lanes(BLOCK) == MASK_LANE, FLOOR, 0.0).astype(bf16)
        left = jnp.where(block - 1 >= 2, left, blank)
        right = jnp.where(block + 1 < block_total, right, blank)
    rand = [block_rows(ref, pick) for pick in picks]
    return jnp.concatenate([own, left, right, block_rows(ref, 0, 2)] + rand, axis=0)


def own_block(place, t):
    return 2 * (place ^ PEERS[t // 2]) + t % 2


def attend_kernel(fast, meta_ref, rand_ref, q_ref, *refs):
    slab_refs, (k_ref, v_ref, *ctx_refs, aux_ref, s_ref) = refs[:-8], refs[-8:]
    place = meta_ref[0]
    piece = 2 * BLOCK
    for n, slab_ref in enumerate(slab_refs):
        for a in range(4):
            device = place ^ slab_offset(n, place, fast) ^ PEERS[a]
            here = pl.ds(pl.multiple_of(device * piece, piece), piece)
            position = device * piece + lax.broadcasted_iota(jnp.int32, (piece, WIDE), 0)
            k_ref[here, :], v_ref[here, :] = widen_pair(
                slab_ref[piece * a : piece * (a + 1), :], position, meta_ref[1]
            )
    total_rows = k_ref.shape[0]
    block_total = total_rows // BLOCK
    chunks = total_rows // (8 * BLOCK)

    def queries(t):
        rows = q_ref[pl.ds(t * BLOCK, BLOCK), :]
        lane = lanes(BLOCK)
        blank = jnp.zeros_like(rows)
        return jnp.concatenate(
            [
                jnp.where(head_lanes(lane, head) | (lane == MASK_LANE), rows, blank)
                for head in range(GROUP_HEADS)
            ],
            axis=0,
        )

    def finish(t, low, exact, top, total):
        lane = lanes(BLOCK)
        rows = pl.ds(t * BLOCK, BLOCK)
        ctx_refs[t // 2][pl.ds((t % 2) * BLOCK, BLOCK), :] = merge_heads(low).astype(bf16)
        aux = merge_heads(exact)
        lse = top + jnp.log(total)
        for head in range(GROUP_HEADS):
            aux = jnp.where(lane == LSE_LANE + head, lse[BLOCK * head : BLOCK * (head + 1)], aux)
        aux_ref[rows, :] = aux

    def split(probs):
        low = probs.astype(bf16)
        return low, (probs - low.astype(f32)).astype(bf16)

    def sparse(t):
        block = own_block(place, t)
        picks = [rand_at(fast, rand_ref, block, r) for r in range(3)]
        scores = dense_right_t(queries(t), key_set(k_ref, picks, block, block_total, True))
        top = jnp.max(scores, axis=1, keepdims=True)
        weights = jnp.exp(scores - top)
        total = jnp.sum(weights, axis=1, keepdims=True)
        low, rest = split(weights * (1.0 / total))
        values = key_set(v_ref, picks, block, block_total, False)
        context = dense_mul(low, values)
        return context, context + dense_mul(rest, values), top, total

    for a in range(4):

        @pl.when((place ^ PEERS[a]) != 0)
        def _(a=a):
            results = [sparse(2 * a), sparse(2 * a + 1)]
            finish(2 * a, *results[0])
            finish(2 * a + 1, *results[1])

    at_once = s_ref.shape[1] // STACK

    def full(a, first):
        stack = jnp.concatenate([queries(2 * a + first + n) for n in range(at_once)], axis=0)
        height = at_once * STACK

        def score(c, state):
            top, total, tops = state
            part = dense_right_t(stack, block_rows(k_ref, c * 8, 8))
            here = jnp.max(part, axis=1, keepdims=True)
            weights = jnp.exp(part - here)
            s_ref[c] = weights
            later = jnp.maximum(top, here)
            total = total * jnp.exp(top - later) + jnp.sum(weights, axis=1, keepdims=True) * jnp.exp(here - later)
            return later, total, jnp.where(turn == c, here, tops)

        turn = lax.broadcasted_iota(jnp.int32, (height, 128), 1)
        top, total, tops = lax.fori_loop(
            0,
            chunks,
            score,
            (jnp.full((height, 1), FLOOR, f32), jnp.zeros((height, 1), f32), jnp.full((height, 128), FLOOR, f32)),
        )
        scales = jnp.exp(tops - top) * (1.0 / total)

        def mix(c, state):
            scale = jnp.sum(jnp.where(turn == c, scales, 0.0), axis=1, keepdims=True)
            low, rest = split(s_ref[c] * scale)
            values = block_rows(v_ref, c * 8, 8)
            return (state[0] + dense_mul(low, values), state[1] + dense_mul(rest, values))

        zero = jnp.zeros((height, WIDE), f32)
        context, rest = lax.fori_loop(0, chunks, mix, (zero, zero), unroll=4)
        for n in range(at_once):
            here = slice(STACK * n, STACK * (n + 1))
            finish(2 * a + first + n, context[here], (context + rest)[here], top[here], total[here])

    for a in range(4):

        @pl.when((place ^ PEERS[a]) == 0)
        def _(a=a):
            for first in range(0, 2, at_once):
                full(a, first)


DENSE_ROWS = 96


def fold_rows(rows):
    last = rows[DENSE_ROWS:]
    beside = jnp.concatenate([last[:, HDIM * h : HDIM * (h + 1)] for h in range(GROUP_HEADS)], axis=0)
    return jnp.concatenate([rows[:DENSE_ROWS], beside], axis=1)


def unfold_rows(folded):
    beside = folded[:, SHARE:]
    count = DENSE_ROWS // GROUP_HEADS
    last = jnp.concatenate([beside[count * h : count * (h + 1)] for h in range(GROUP_HEADS)], axis=1)
    rows = jnp.concatenate([folded[:, :SHARE], last], axis=0)
    return jnp.concatenate([rows, jnp.zeros((rows.shape[0], WIDE - SHARE), rows.dtype)], axis=1)


def split_parts(value):
    high = value.astype(bf16).astype(f32)
    middle = (value - high).astype(bf16).astype(f32)
    return (high, middle, value - high - middle)


def delta_kernel(*refs):
    grad_refs, aux_ref, out_ref = refs[:4], refs[4], refs[5]
    rows = 2 * BLOCK
    lane = lanes(rows)
    for a in range(4):
        here = pl.ds(a * rows, rows)
        grad = unfold_rows(grad_refs[a][...]).astype(f32)
        aux = aux_ref[here, :]
        result = jnp.where(lane < SHARE, grad, 0.0)
        product = grad * aux
        for head in range(GROUP_HEADS):
            delta = jnp.sum(jnp.where(head_lanes(lane, head), product, 0.0), axis=1, keepdims=True)
            lse = jnp.sum(jnp.where(lane == LSE_LANE + head, aux, 0.0), axis=1, keepdims=True)
            for p, value in enumerate(split_parts(lse)):
                result = jnp.where(lane == LSE_LANE + 3 * head + p, -value, result)
            for p, value in enumerate(split_parts(delta)):
                result = jnp.where(lane == DEL_LANE + 3 * head + p, -value, result)
        out_ref[here, :] = result.astype(bf16)


def query_stacks(rows, grads):
    lane = lanes(BLOCK)
    blank = jnp.zeros_like(rows)
    queries = []
    outers = []
    for head in range(GROUP_HEADS):
        here = head_lanes(lane, head)
        queries.append(
            jnp.where(
                here | (lane == MASK_LANE), rows, jnp.where(part_lanes(lane, LSE_LANE, head), grads, blank)
            )
        )
        outers.append(jnp.where(here | part_lanes(lane, DEL_LANE, head), grads, blank))
    return jnp.concatenate(queries, axis=0), jnp.concatenate(outers, axis=0)


def near_kernel(fast, meta_ref, rand_ref, q_ref, k_ref, v_ref, g_ref, dq_ref, *refs):
    zero_outs, (blank_ref, sems) = refs[:-2], refs[-2:]
    place = meta_ref[0]
    block_total = k_ref.shape[0] // BLOCK
    copies = []
    if zero_outs:
        blank_ref[...] = jnp.zeros_like(blank_ref)
        for n, where in enumerate(zero_outs):
            shape = where.shape
            source = blank_ref if len(shape) == 4 else blank_ref.at[0 : shape[2] // D]
            for adapter in range(ADAPTERS):
                if len(shape) == 4:
                    copies.append((blank_ref, where.at[adapter], n))
                else:
                    for c in range(shape[2] // D):
                        copies.append((blank_ref.at[c], where.at[adapter, :, pl.ds(D * c, D)], n))
        copies = [pltpu.make_async_copy(source, where, sems.at[n]) for n, (source, where, _) in enumerate(copies)]
        for copy in copies:
            copy.start()

    def query_side(stack, outer, keys, values):
        probs = jnp.exp(dense_right_t(stack, keys))
        scored = (probs * dense_right_t(outer, values)).astype(bf16)
        return dense_mul(scored, keys)

    def place_of(a, k):
        return pl.ds(pl.multiple_of((2 * a + k) * BLOCK, BLOCK), BLOCK)

    def put_query(a, k, stacked):
        dq_ref[place_of(a, k), :] = (merge_heads(stacked) * 0.125).astype(bf16)

    def stacks(a, k):
        here = place_of(a, k)
        return query_stacks(q_ref[here, :], g_ref[here, :])

    def sparse(a, k):
        block = 2 * (place ^ (8 * a)) + k
        picks = [rand_at(fast, rand_ref, block, r) for r in range(3)]
        return query_side(
            *stacks(a, k),
            key_set(k_ref, picks, block, block_total, True),
            key_set(v_ref, picks, block, block_total, False),
        )

    def piece(a, carry):
        @pl.when((place ^ (8 * a)) != 0)
        def _():
            results = [sparse(a, 0), sparse(a, 1)]
            put_query(a, 0, results[0])
            put_query(a, 1, results[1])

        @pl.when((place ^ (8 * a)) == 0)
        def _():
            pairs = [stacks(a, 0), stacks(a, 1)]
            stack = jnp.concatenate([pair[0] for pair in pairs], axis=0)
            outer = jnp.concatenate([pair[1] for pair in pairs], axis=0)

            def add(c, total):
                return total + query_side(stack, outer, block_rows(k_ref, c * 16, 16), block_rows(v_ref, c * 16, 16))

            total = lax.fori_loop(0, block_total // 16, add, jnp.zeros((2 * STACK, WIDE), f32), unroll=2)
            put_query(a, 0, total[:STACK])
            put_query(a, 1, total[STACK:])

        return carry

    lax.fori_loop(0, 4, piece, 0)
    for copy in copies:
        copy.wait()


def collect_kernel(fast, block_total, meta_ref, rand_ref, pair_ref):
    place = meta_ref[0]

    def collect(block, count):
        for r in range(3):
            target = rand_at(fast, rand_ref, block, r)
            mine = (((target // 2) ^ place) & ~24) == 0

            @pl.when(mine)
            def _(target=target, count=count):
                pair_ref[count + 1] = target * 65536 + block

            count = count + mine.astype(jnp.int32)
        return count

    pair_ref[0] = lax.fori_loop(2, block_total, collect, jnp.int32(0))


def far_kernel(fast, meta_ref, pair_ref, k_ref, v_ref, dq_ref, w_ref, down_ref, up_ref, early_ref, *refs):
    count = 3 if fast else 4
    tok_refs, refs = refs[:count], refs[count:]
    slab_refs, refs = refs[:-11], refs[-11:]
    part_refs, near_ref, away_ref, refs = refs[:2], refs[2], refs[3], refs[4:]
    q_ref, g_ref, dk_ref, dv_ref, grad_ref, tok_ref, terms_ref = refs
    place = meta_ref[0]
    group = meta_ref[2]
    block_total = k_ref.shape[0] // BLOCK
    count = len(slab_refs) // 2
    rows = 2 * BLOCK
    for n in range(count):
        here = pl.ds(pl.multiple_of(slab_row(slab_offset(n, place, fast)) * 4 * rows, rows), 4 * rows)
        q_ref[here, :] = slab_refs[n][...]
        g_ref[here, :] = slab_refs[count + n][...]

    def stacks(blocks):
        pairs = []
        for block in blocks:
            other = (block // 2) ^ place
            where = slab_row(other) * 8 + ((other >> 3) & 3) * 2 + (block & 1)
            pairs.append(query_stacks(block_rows(q_ref, where), block_rows(g_ref, where)))
        return (
            jnp.concatenate([pair[0] for pair in pairs], axis=0),
            jnp.concatenate([pair[1] for pair in pairs], axis=0),
        )

    def key_side(keys, values, blocks, allowed):
        stack, outer = stacks(blocks)
        probs = jnp.exp(dense_right_t(keys, stack))
        if allowed is not None:
            probs = jnp.where(allowed, probs, 0.0)
        scored = (probs * dense_right_t(values, outer)).astype(bf16)
        return dense_mul(scored, stack), dense_mul(probs.astype(bf16), outer)

    def put(here, grads):
        dk_ref[here, :] += grads[0]
        dv_ref[here, :] += grads[1]

    key_local = lax.broadcasted_iota(jnp.int32, (rows, 6 * STACK), 0) // BLOCK
    turn = lax.broadcasted_iota(jnp.int32, (rows, 6 * STACK), 1) // STACK
    for a in range(4):
        first = 2 * (place ^ PEERS[a])
        here = slice(rows * a, rows * (a + 1))
        blocks = [0, 1, jnp.maximum(first - 1, 0), first, first + 1, jnp.minimum(first + 2, block_total - 1)]
        key_block = first + key_local
        block = first - 3 + turn
        near = (key_block - block <= 1) & (block - key_block <= 1) & (block >= 2) & (block < block_total)
        allowed = ((turn < 2) | near) & (key_block >= 2)
        keys = block_rows(k_ref, first, 2)
        values = block_rows(v_ref, first, 2)
        dk_ref[here, :], dv_ref[here, :] = key_side(keys, values, blocks, allowed)

    pair_total = pair_ref[0]

    def random_pairs(step, carry):
        grads = []
        for k in range(4):
            number = 4 * step + k
            live = number < pair_total
            code = pair_ref[jnp.minimum(number, pair_total - 1) + 1]
            target = code // 65536
            block = code - target * 65536
            start = ((((target // 2) ^ place) >> 3) & 3) * rows + (target & 1) * BLOCK
            grads.append(
                (
                    pl.ds(pl.multiple_of(start, BLOCK), BLOCK),
                    key_side(block_rows(k_ref, target), block_rows(v_ref, target), (block,), live),
                )
            )
        for here, parts in grads:
            put(here, parts)
        return carry

    lax.fori_loop(0, (pair_total + 3) // 4, random_pairs, 0)

    @pl.when((place & ~24) == 0)
    def _():
        here = pl.ds(pl.multiple_of(group * rows, rows), rows)
        keys = block_rows(k_ref, 0, 2)
        values = block_rows(v_ref, 0, 2)

        def every(step, carry):
            put(here, key_side(keys, values, [4 * step + k for k in range(4)], None))
            return carry

        lax.fori_loop(0, block_total // 4, every, 0, unroll=4)

    data = lanes(rows) < SHARE
    for a in range(4):
        here = slice(rows * a, rows * (a + 1))
        grad_ref[here, :WIDE] = dq_ref[here, :]
        grad_ref[here, WIDE : 2 * WIDE] = jnp.where(data, dk_ref[here, :], 0.0).astype(bf16)
        grad_ref[here, 2 * WIDE :] = jnp.where(data, dv_ref[here, :], 0.0).astype(bf16)
    put_tokens(fast, tok_refs, tok_ref)
    tokens = tok_ref[...]
    grad = grad_ref[...]
    reduced = dense_right_t(tokens, down_ref[...]).astype(bf16)
    grad_reduced = dense_right_t(grad, up_ref[...]).astype(bf16)
    down_terms = dense_left_t(grad_reduced, tokens)
    up_terms = dense_left_t(reduced, grad)
    terms = [down_terms[RANK * j : RANK * (j + 1)] for j in range(3)]
    ups = []
    for j in range(3):
        up = up_terms[RANK * j : RANK * (j + 1), WIDE * j : WIDE * j + SHARE]
        ups.append(jnp.concatenate([jnp.where(group == g, up, 0.0) for g in range(4)], axis=1))
    terms += ups + [jnp.zeros((RANK, D), f32)] * 2
    core = (place >> 1) & 1
    quarter = plane_quarter(place)
    for part, value in enumerate(terms):
        early = early_ref[EARLY_PART * part : EARLY_PART * (part + 1), :]
        where = (((part // 4) ^ core) * 4 + ((part % 4) ^ quarter)) if fast else part
        terms_ref[where, :RANK] = value
        terms_ref[where, RANK:] = early
    near_ref[...] = terms_ref[:4]
    away_ref[...] = terms_ref[4:].astype(away_ref.dtype)
    for n, a in enumerate((0, 2, 1, 3)):
        here = slice(rows * a, rows * (a + 1))
        part = (dense_right_t(grad[here], w_ref[...]) + dense_mul(grad_reduced[here], down_ref[...])).astype(bf16)
        part_refs[n // 2][rows * (n % 2) : rows * (n % 2 + 1), :] = part


def normal(hidden):
    center = hidden - jnp.mean(hidden, axis=-1, keepdims=True)
    root = lax.rsqrt(jnp.mean(center * center, axis=-1, keepdims=True) + norm_eps)
    return center * root, root


def normal_back(grad, normed, root):
    mean = jnp.mean(grad, axis=-1, keepdims=True)
    return root * (grad - mean - normed * jnp.mean(grad * normed, axis=-1, keepdims=True))


def select_kernel(meta_ref, *refs):
    chosen = meta_ref[3]
    tables, (down_ref, up_ref, *rest) = refs[:6], refs[6:]
    down_ref[...] = tables[0][chosen, 3]
    up_ref[...] = tables[1][chosen, 3]
    for table, ref in zip(tables[2:], rest, strict=True):
        ref[...] = table[chosen]


def middle_kernel(
    fast,
    meta_ref,
    ctx_refs,
    tok_ref,
    cot_ref,
    late_hbm,
    gain_ref,
    down_ref,
    up_ref,
    inner_down_ref,
    inner_up_ref,
    outer_down_ref,
    outer_up_ref,
    wide_ref,
    out_ref,
    grad_ref,
    piece_refs,
    terms_ref,
    hold_ref,
    pre_ref,
    act_ref,
    late_ref,
    sems,
):
    group = meta_ref[2]
    rows = tok_ref.shape[0]
    share = D // (FF // D)
    places = [(slice(None), slice(D * c, D * (c + 1))) for c in range(1 + FF // D)]
    if fast:
        places += [(slice(share * c, share * (c + 1)), slice(D + FF, D + 2 * FF)) for c in range(FF // D)]
    copies = [
        pltpu.make_async_copy(late_hbm.at[place], late_ref.at[place], sems.at[n]) for n, place in enumerate(places)
    ]
    order = [0] + [n for c in range(FF // D) for n in (1 + c, 1 + FF // D + c) if n < len(copies)]
    for n in order:
        copies[n].start()

    def build(c):
        copies[1 + FF // D + c].wait()
        slab = 24
        for pair in range(share // (2 * slab)):
            first = share * c + 2 * slab * pair
            block = late_ref[first : first + 2 * slab, D + FF :].astype(f32)
            cut = [
                block[slab * side : slab * (side + 1), D * n : D * (n + 1)]
                for side in range(2)
                for n in range(FF // D)
            ]
            wide_ref[4 * first : 4 * first + 8 * slab, :] = jnp.concatenate(cut, axis=0).astype(bf16)

    for a in range(4):
        hold_ref[a] = ctx_refs[a][...]
    context = jnp.concatenate([hold_ref[group ^ g][:, :SHARE] for g in range(4)], axis=1)
    context_red = dense_right_t(context, down_ref[...]).astype(bf16)
    copies[0].wait()
    attended = dense_mul(context, late_ref[:, :D]) + dense_mul(context_red, up_ref[...])
    first, first_root = normal(tok_ref[...].astype(f32) + attended)
    first_norm = first * gain_ref[0:1, :] + gain_ref[1:2, :]
    first_low = first_norm.astype(bf16)
    inner_red = dense_right_t(first_low, inner_down_ref[...]).astype(bf16)
    outer_red = jnp.zeros((rows, RANK), f32)
    outer_out = jnp.zeros((rows, D), f32)
    for c in range(FF // D):
        here = slice(D * c, D * (c + 1))
        copies[1 + c].wait()
        if fast:
            build(c)
        pre = dense_mul(first_low, late_ref[:, D * (c + 1) : D * (c + 2)]) + dense_mul(
            inner_red, inner_up_ref[:, here]
        )
        pre_ref[:, here] = pre
        active = (0.5 * pre * (1.0 + lax.erf(pre * 0.7071067811865476))).astype(bf16)
        act_ref[:, here] = active
        outer_red = outer_red + dense_right_t(active, outer_down_ref[:, here])
        outer_out = outer_out + dense_mul(active, wide_ref[here, :])
    outer_red = outer_red.astype(bf16)
    outer_out = outer_out + dense_mul(outer_red, outer_up_ref[...])
    second, second_root = normal(first_norm + outer_out)
    position = meta_ref[0] * rows + lax.broadcasted_iota(jnp.int32, (rows, D), 0)
    valid = (position < meta_ref[1]).astype(f32)
    out_ref[...] = ((second * gain_ref[2:3, :] + gain_ref[3:4, :]) * valid).astype(bf16)
    grad_second = normal_back(valid * cot_ref[...].astype(f32) * gain_ref[2:3, :], second, second_root)
    grad_outer = grad_second.astype(bf16)
    first_up = RANK * 3
    first_down = RANK * (3 + FF // D)
    terms_ref[first_down + RANK * (FF // D) :, :] = dense_left_t(outer_red, grad_outer)
    outer_grad_red = dense_right_t(grad_outer, outer_up_ref[...]).astype(bf16)
    inner_grad_red = jnp.zeros((rows, RANK), f32)
    grad_first = grad_second
    for c in range(FF // D):
        here = slice(D * c, D * (c + 1))
        grad_active = dense_right_t(grad_outer, wide_ref[here, :]) + dense_mul(
            outer_grad_red, outer_down_ref[:, here]
        )
        pre = pre_ref[:, here]
        slope = 0.5 * (1.0 + lax.erf(pre * 0.7071067811865476)) + pre * (
            0.3989422804014327 * jnp.exp(-0.5 * pre * pre)
        )
        grad_inner = (slope * grad_active).astype(bf16)
        terms_ref[first_up + RANK * c : first_up + RANK * (c + 1), :] = dense_left_t(inner_red, grad_inner)
        terms_ref[first_down + RANK * c : first_down + RANK * (c + 1), :] = dense_left_t(
            outer_grad_red, act_ref[:, here]
        )
        inner_grad_red = inner_grad_red + dense_right_t(grad_inner, inner_up_ref[:, here])
        grad_first = grad_first + dense_right_t(grad_inner, late_ref[:, D * (c + 1) : D * (c + 2)])
    inner_grad_red = inner_grad_red.astype(bf16)
    terms_ref[2 * RANK : 3 * RANK, :] = dense_left_t(inner_grad_red, first_low)
    grad_first = grad_first + dense_mul(inner_grad_red, inner_down_ref[...])
    grad_attended = normal_back(grad_first * gain_ref[0:1, :], first, first_root)
    grad_ref[...] = grad_attended
    grad_low = grad_attended.astype(bf16)
    context_grad_red = dense_right_t(grad_low, up_ref[...]).astype(bf16)
    terms_ref[:RANK, :] = dense_left_t(context_grad_red, context)
    terms_ref[RANK : 2 * RANK, :] = dense_left_t(context_red, grad_low)
    grad_context = (
        dense_right_t(grad_low, late_ref[:, :D]) + dense_mul(context_grad_red, down_ref[...])
    ).astype(bf16)
    for g in range(4):
        hold_ref[group ^ g, :DENSE_ROWS, :] = fold_rows(grad_context[:, SHARE * g : SHARE * (g + 1)])
    for a in range(4):
        piece_refs[a][...] = hold_ref[a, :DENSE_ROWS, :]


def spread_kernel(meta_ref, *refs):
    part_refs = refs[:8]
    outs = refs[14:20]
    sum_ref, sems = refs[20:]
    quarter = plane_quarter(meta_ref[0])
    core = (meta_ref[0] >> 1) & 1
    chosen = meta_ref[3]
    for n in range(8):
        part = (core ^ (n // 4)) * 4 + (quarter ^ (n % 4))
        sum_ref[pl.ds(pl.multiple_of(part * RANK, RANK), RANK), :] = part_refs[n][:RANK, :].astype(f32)
        sum_ref[pl.ds(pl.multiple_of(LATE_ROWS + part * EARLY_PART, 8), EARLY_PART), :] = part_refs[n][RANK:, :].astype(f32)
    places = [outs[0].at[chosen, j] for j in range(3)] + [outs[1].at[chosen, j] for j in range(3)]
    places += [None, None, outs[0].at[chosen, 3], outs[1].at[chosen, 3], outs[2].at[chosen]]
    places += [outs[n].at[chosen, :, pl.ds(D * c, D)] for n in (3, 4) for c in range(FF // D)]
    places.append(outs[5].at[chosen])
    copies = [
        pltpu.make_async_copy(sum_ref.at[pl.ds(RANK * n, RANK), :], where, sems.at[n])
        for n, where in enumerate(places)
        if where is not None
    ]
    for copy in copies:
        copy.start()
    for copy in copies:
        copy.wait()


LATE_ROWS = 8 * RANK
EARLY_KINDS = 12
EARLY_PART = EARLY_KINDS * RANK // 8
ANY = pl.BlockSpec(memory_space=pl.ANY)
SMEM = pl.BlockSpec(memory_space=pltpu.SMEM)
VMEM = pl.BlockSpec(memory_space=pltpu.VMEM)


def shards(
    tokens,
    cotangent,
    w_query,
    w_key,
    w_value,
    w_output,
    w_inner,
    w_outer,
    gain_first,
    shift_first,
    gain_second,
    shift_second,
    attn_down,
    attn_up,
    inner_down,
    inner_up,
    outer_down,
    outer_up,
    lengths,
    rand_blocks,
    adapter_pick,
):
    device_total = lax.axis_size("seq") * lax.axis_size("head")
    local_rows = tokens.shape[0]
    seq_total = lengths.shape[0]
    members = device_total // seq_total
    rows_total = members * local_rows
    block_total = rows_total // BLOCK
    chunk = 4 * local_rows
    index = lax.axis_index("seq") * lax.axis_size("head") + lax.axis_index("head")
    place = index % members
    seq_number = index // members
    group = (place >> 3) & 3
    seq_length = lengths[seq_number]
    chosen = adapter_pick[seq_number]
    fast = device_total == 32 and members == 32
    together = lax.optimization_barrier

    def send(value, even, odd):
        return lax.ppermute(
            value, AXES, [(j, j ^ (odd if (j >> 1) & 1 else even)) for j in range(device_total)]
        )

    def swap(value, mask):
        return send(value, mask, mask)

    def one(value):
        return send(value, 4, 1)

    def two(value):
        return send(value, 1, 4)

    def exchange(pieces, masks=PEERS):
        return [pieces[0]] + [swap(pieces[a], masks[a]) for a in range(1, 4)]

    def gather_start(value):
        if not fast:
            masks = [slab_offset(n, place, False) for n in range(members // 4)]
            return [value] + [swap(value, mask) for mask in masks[1:]]
        return [value, one(value), two(value)]

    def gather_end(slabs):
        if not fast:
            return slabs
        slabs = slabs + [two(slabs[1])]
        return slabs + [swap(slab, 2) for slab in slabs]

    def gather_direct(value):
        return gather_start(value) + ([swap(value, 5)] if fast else [])

    def gather_hand(slabs):
        return slabs + [swap(slab, 2) for slab in slabs] if fast else slabs

    def gather_all(value):
        return lax.all_gather(value, AXES, axis=0, tiled=True)

    def share_columns(table, which=group):
        return lax.dynamic_slice_in_dim(table, which * SHARE, SHARE, table.ndim - 1)

    slab = D // device_total
    meta = jnp.stack([place, seq_length, group, chosen]).astype(jnp.int32)
    if fast:
        late_local, *slices = pl.pallas_call(
            pack_kernel,
            in_specs=[SMEM] + [VMEM] * 6,
            out_specs=[VMEM] * 5,
            out_shape=[jax.ShapeDtypeStruct((slab, D + 2 * FF), bf16)]
            + [jax.ShapeDtypeStruct((slab, 3 * WIDE), bf16)] * 4,
            name="pack",
        )(rand_blocks, w_query, w_key, w_value, w_output, w_inner, w_outer)
        late = gather_all(late_local)
        mine = exchange(slices)
        far_tokens = swap(tokens, PEERS[2])
        near_tokens = swap(jnp.concatenate([tokens, far_tokens], axis=0), PEERS[1])
        token_refs = [tokens, far_tokens, near_tokens]
        w_slabs = gather_hand(gather_direct(jnp.concatenate(mine, axis=0)))
    else:
        late = gather_all(
            jnp.concatenate([w_output, w_inner] + [w_outer[slab * c : slab * (c + 1)] for c in range(FF // D)], axis=1)
        )
        full_qkv = gather_all(jnp.concatenate([w_query, w_key, w_value], axis=1))
        rand_all = lax.all_gather(rand_blocks, "seq", axis=0, tiled=True)
        rand_flat = lax.dynamic_slice_in_dim(rand_all, seq_number * block_total, block_total, 0).reshape(-1)
        token_refs = exchange([tokens] * 4)
        w_slabs = [
            jnp.concatenate(
                [
                    jnp.pad(share_columns(full_qkv[:, D * j : D * (j + 1)]), ((0, 0), (0, WIDE - SHARE)))
                    for j in range(3)
                ],
                axis=1,
            )
        ]

    wide_rows = jax.ShapeDtypeStruct((rows_total, WIDE), bf16)
    piece_shapes = [jax.ShapeDtypeStruct((local_rows, WIDE), bf16)] * 4
    side_weight, down_stack, up_stack, query_own, pair_own, rand_table = pl.pallas_call(
        functools.partial(project_kernel, fast),
        in_specs=[SMEM] + [VMEM] * (2 + len(token_refs) + len(w_slabs)),
        out_specs=[VMEM] * 6,
        out_shape=[
            jax.ShapeDtypeStruct((D, 3 * WIDE), bf16),
            jax.ShapeDtypeStruct((WIDE // 2, D), bf16),
            jax.ShapeDtypeStruct((WIDE // 2, 3 * WIDE), bf16),
            jax.ShapeDtypeStruct((chunk, WIDE), bf16),
            jax.ShapeDtypeStruct((chunk, 2 * SHARE), bf16),
            jax.ShapeDtypeStruct((32, WIDE // 2), jnp.int32),
        ],
        scratch_shapes=[
            pltpu.VMEM((3, WIDE // 2, WIDE), bf16),
            pltpu.VMEM((chunk, D), bf16),
            pltpu.VMEM((D, 3 * WIDE), f32),
        ],
        compiler_params=pltpu.CompilerParams(vmem_limit_bytes=VMEM_LIMIT),
        name="project",
    )(meta, attn_down, attn_up, *token_refs, *w_slabs)
    if fast:
        rand_flat = rand_table
    pair_list = pl.pallas_call(
        functools.partial(collect_kernel, fast, block_total),
        in_specs=[SMEM, SMEM],
        out_specs=SMEM,
        out_shape=jax.ShapeDtypeStruct((3 * block_total + 8,), jnp.int32),
        name="collect",
    )(meta, rand_flat)
    pair_slabs = gather_start(pair_own)
    pair_list, pair_slabs[1] = together((pair_list, pair_slabs[1]))
    pair_slabs = gather_end(pair_slabs)
    key_all, value_all, *ctx, aux = pl.pallas_call(
        functools.partial(attend_kernel, fast),
        in_specs=[SMEM, SMEM] + [VMEM] * (1 + len(pair_slabs)),
        out_specs=[VMEM] * 7,
        out_shape=[wide_rows] * 2 + piece_shapes + [jax.ShapeDtypeStruct((chunk, WIDE), f32)],
        scratch_shapes=[pltpu.VMEM((rows_total // chunk, (2 if fast else 1) * STACK, chunk), f32)],
        compiler_params=pltpu.CompilerParams(vmem_limit_bytes=VMEM_LIMIT),
        name="attend",
    )(meta, rand_flat, query_own, *pair_slabs)
    *tables, ctx[1] = together((attn_down, attn_up, inner_down, inner_up, outer_down, outer_up, ctx[1]))
    ctx_pieces = exchange(ctx)

    gains = jnp.stack([gain_first, shift_first, gain_second, shift_second])
    chosen_maps = pl.pallas_call(
        select_kernel,
        in_specs=[SMEM] + [VMEM] * 6,
        out_specs=[VMEM] * 6,
        out_shape=[jax.ShapeDtypeStruct((RANK, width), bf16) for width in (D, D, D, FF, FF, D)],
        name="select",
    )(meta, *tables)
    *chosen_maps, late = together((*chosen_maps, late))
    middle_in = [tokens, cotangent, late, gains, *chosen_maps]
    wide_shape = [pltpu.VMEM((FF, D), bf16)]
    if not fast:
        middle_in.append(
            late[:, D + FF :].reshape(device_total, slab, FF // D, D).transpose(0, 2, 1, 3).reshape(FF, D)
        )
        wide_shape = []
    count = len(middle_in)

    def middle(meta_ref, *refs):
        ins, outs, scratch = refs[4 : 4 + count], refs[4 + count : 11 + count], refs[11 + count :]
        wide_ref = scratch[-1] if fast else ins[-1]
        middle_kernel(
            fast, meta_ref, refs[:4], *ins[:10], wide_ref, *outs[:2], outs[2:6], outs[6], *scratch[:5]
        )


    output, grad_attended, *grad_pieces, early_terms = pl.pallas_call(
        middle,
        in_specs=[SMEM] + [VMEM] * 6 + [ANY] + [VMEM] * (count - 3),
        out_specs=[VMEM] * 7,
        out_shape=[
            jax.ShapeDtypeStruct((local_rows, D), bf16),
            jax.ShapeDtypeStruct((local_rows, D), f32),
        ]
        + [jax.ShapeDtypeStruct((DENSE_ROWS, WIDE), bf16)] * 4
        + [jax.ShapeDtypeStruct((EARLY_KINDS * RANK, D), f32)],
        scratch_shapes=[
            pltpu.VMEM((4, local_rows, WIDE), bf16),
            pltpu.VMEM((local_rows, FF), f32),
            pltpu.VMEM((local_rows, FF), bf16),
            pltpu.VMEM(late.shape, bf16),
            pltpu.SemaphoreType.DMA((1 + 2 * (FF // D),)),
        ]
        + wide_shape,
        compiler_params=pltpu.CompilerParams(vmem_limit_bytes=VMEM_LIMIT),
        name="middle",
    )(meta, *ctx_pieces, *middle_in)
    query_send, grad_pieces[0] = together((query_own, grad_pieces[0]))
    query_slabs = gather_hand(gather_direct(query_send))
    grad_wide = pl.pallas_call(
        delta_kernel,
        in_specs=[VMEM] * 5,
        out_specs=VMEM,
        out_shape=jax.ShapeDtypeStruct((chunk, WIDE), bf16),
        name="delta",
    )(*exchange(grad_pieces), aux)
    def reduced(terms):
        paired = terms[0] + swap(terms[1], 2)
        moved = exchange([paired[a] for a in range(4)])
        part = (moved[0] + moved[1]) + (moved[2] + moved[3])
        moved = [part] + [swap(part, depth) for depth in DEPTHS[1:]]
        return (moved[0] + moved[1]) + (moved[2] + moved[3])

    grad_slabs = gather_start(grad_wide)
    out_shapes = [
        jax.ShapeDtypeStruct(shape, f32)
        for shape in (
            (ADAPTERS, 4, RANK, D),
            (ADAPTERS, 4, RANK, D),
            (ADAPTERS, RANK, D),
            (ADAPTERS, RANK, FF),
            (ADAPTERS, RANK, FF),
            (ADAPTERS, RANK, D),
        )
    ]
    zero_shapes = out_shapes if fast else []
    query_grad, *zeros = pl.pallas_call(
        functools.partial(near_kernel, fast),
        in_specs=[SMEM, SMEM] + [VMEM] * 4,
        out_specs=[VMEM] + [ANY] * len(zero_shapes),
        out_shape=[jax.ShapeDtypeStruct((chunk, WIDE), bf16)] + zero_shapes,
        scratch_shapes=[pltpu.VMEM((4, RANK, D), f32), pltpu.SemaphoreType.DMA((ADAPTERS * 12,))],
        compiler_params=pltpu.CompilerParams(vmem_limit_bytes=VMEM_LIMIT),
        cost_estimate=pl.CostEstimate(flops=12000000000, bytes_accessed=8000000, transcendentals=1000000),
        name="near",
    )(meta, rand_flat, query_own, key_all, value_all, grad_wide)
    query_grad, *grad_slabs = together((query_grad, *grad_slabs))
    grad_slabs = gather_end(grad_slabs)
    kept, given, near_terms, away_terms = pl.pallas_call(
        functools.partial(far_kernel, fast),
        in_specs=[SMEM, SMEM] + [VMEM] * (7 + len(token_refs) + 2 * len(grad_slabs)),
        out_specs=[VMEM] * 4,
        out_shape=[jax.ShapeDtypeStruct((2 * local_rows, D), bf16)] * 2
        + [jax.ShapeDtypeStruct((4, RANK + EARLY_PART, D), kind) for kind in (f32, bf16 if fast else f32)],
        scratch_shapes=[
            pltpu.VMEM((rows_total, WIDE), bf16),
            pltpu.VMEM((rows_total, WIDE), bf16),
            pltpu.VMEM((chunk, WIDE), f32),
            pltpu.VMEM((chunk, WIDE), f32),
            pltpu.VMEM((chunk, 3 * WIDE), bf16),
            pltpu.VMEM((chunk, D), bf16),
            pltpu.VMEM((8, RANK + EARLY_PART, D), f32),
        ],
        compiler_params=pltpu.CompilerParams(vmem_limit_bytes=VMEM_LIMIT),
        name="far",
    )(
        meta,
        pair_list,
        key_all,
        value_all,
        query_grad,
        side_weight,
        down_stack,
        up_stack,
        early_terms,
        *token_refs,
        *query_slabs,
        *grad_slabs,
    )
    kept = kept.astype(f32) + swap(given, PEERS[1]).astype(f32)
    passed = swap(kept[local_rows:].astype(bf16), PEERS[2])
    grad_tokens = grad_attended + (kept[:local_rows] + passed.astype(f32))

    if fast:
        paired = near_terms + swap(away_terms, 2).astype(f32)
        moved = [paired[0]] + [swap(paired[a].astype(bf16), PLANE[a]).astype(f32) for a in range(1, 4)]
        part = ((moved[0] + moved[1]) + (moved[2] + moved[3])).astype(bf16)
        moved = [piece.astype(f32) for piece in exchange([part] * 4)]
        part = ((moved[0] + moved[1]) + (moved[2] + moved[3])).astype(bf16)
        part_list = exchange([part] * 4, PLANE)
        part_list = part_list + [swap(value, 2) for value in part_list]
        sums = pl.pallas_call(
            spread_kernel,
            in_specs=[SMEM] + [VMEM] * 8 + [ANY] * 6,
            out_specs=[ANY] * 6,
            out_shape=out_shapes,
            scratch_shapes=[
                pltpu.VMEM((LATE_ROWS + EARLY_KINDS * RANK, D), f32),
                pltpu.SemaphoreType.DMA((8 + EARLY_KINDS,)),
            ],
            input_output_aliases={9 + n: n for n in range(6)},
            name="spread",
        )(meta, *part_list, *zeros)
        return (output, grad_tokens, *sums)

    terms = jnp.concatenate([near_terms, away_terms], axis=0)
    terms = jnp.concatenate([terms[:, :RANK].reshape(-1, D), terms[:, RANK:].reshape(-1, D)], axis=0)
    slots = (jnp.arange(seq_total) == seq_number).astype(f32)[:, None, None]
    every = lax.psum(slots * terms[None], AXES)

    def spread(kinds, width):
        def term(s):
            rows = jnp.concatenate([every[s, kind * RANK : (kind + width // D) * RANK] for kind in kinds], axis=0)
            value = rows.reshape(len(kinds), width // D, RANK, D).transpose(0, 2, 1, 3)
            value = value.reshape(len(kinds), RANK, width)
            return (jnp.arange(ADAPTERS) == adapter_pick[s]).astype(f32)[:, None, None, None] * value[None]

        return functools.reduce(lambda x, y: x + y, [term(s) for s in range(seq_total)])

    wide = FF // D
    sums = [
        spread((0, 1, 2, 8), D),
        spread((3, 4, 5, 9), D),
        spread((10,), D),
        spread((11,), FF),
        spread((11 + wide,), FF),
        spread((11 + 2 * wide,), D),
    ]
    return (
        output,
        grad_tokens,
        *[value.reshape(leaf.shape) for value, leaf in zip(sums, out_shapes, strict=True)],
    )


def solution(mesh):
    rows = P(AXES, None)
    placed = (rows,) * 8 + (P(),) * 11 + (P("seq", None), P())
    return jax.shard_map(
        shards,
        mesh=mesh,
        in_specs=placed,
        out_specs=(rows, rows) + (P(),) * 6,
        check_vma=False,
    )
```

```python
import functools

import jax
import jax.numpy as jnp
from jax import lax
from jax.experimental import pallas as pl
from jax.experimental.pallas import tpu as pltpu
from jax.sharding import PartitionSpec as P

D = 768
HEADS = 12
HDIM = 64
BLOCK = 64
ADAPTERS = 8
RANK = 16
FF = 3072

PEERS = (0, 8, 16, 24)
PLANE = (0, 1, 4, 5)
GROUP_HEADS = HEADS // 4
SHARE = GROUP_HEADS * HDIM
WIDE = 256
LSE_LANE = SHARE
DEL_LANE = SHARE + 9
MASK_LANE = SHARE + 18
FLOOR = -1e30
STACK = GROUP_HEADS * BLOCK
AXES = ("seq", "head")
norm_eps = 1e-12
f32 = jnp.float32
bf16 = jnp.bfloat16
VMEM_LIMIT = 60 * 1024 * 1024


def dense_mul(left_op, right_op):
    return jnp.dot(left_op, right_op, preferred_element_type=f32)


def dense_right_t(left_op, right_op):
    return lax.dot_general(left_op, right_op, (((1,), (1,)), ((), ())), preferred_element_type=f32)


def dense_left_t(left_op, right_op):
    return lax.dot_general(left_op, right_op, (((0,), (0,)), ((), ())), preferred_element_type=f32)


def lanes(rows):
    return lax.broadcasted_iota(jnp.int32, (rows, WIDE), 1)


def head_lanes(lane, head):
    return (lane >= HDIM * head) & (lane < HDIM * (head + 1))


def part_lanes(lane, first, head):
    return (lane >= first + 3 * head) & (lane < first + 3 * head + 3)


def project_rows(raw, u_ref):
    lane = lanes(raw.shape[0])
    data = lane < SHARE

    def part(j):
        piece = raw[:, WIDE * j : WIDE * (j + 1)]
        return (piece + dense_mul(piece[:, WIDE // 2 :].astype(bf16), u_ref[j])).astype(bf16).astype(f32)

    query = jnp.where(data, part(0) * 0.125, jnp.where(lane == MASK_LANE, 1.0, 0.0)).astype(bf16)
    return query, jnp.concatenate([part(1)[:, :SHARE], part(2)[:, :SHARE]], axis=1).astype(bf16)


def widen_pair(pair, position, seq_length):
    lane = lanes(pair.shape[0])
    data = lane < SHARE
    blank = jnp.zeros((pair.shape[0], WIDE - SHARE), bf16)
    key = jnp.concatenate([pair[:, :SHARE], blank], axis=1)
    value = jnp.concatenate([pair[:, SHARE:], blank], axis=1)
    mask = jnp.where(position < seq_length, 0.0, FLOOR)
    key_side = jnp.where(lane < DEL_LANE, 1.0, jnp.where(lane == MASK_LANE, mask, 0.0)).astype(bf16)
    value_side = jnp.where((lane >= DEL_LANE) & (lane < MASK_LANE), 1.0, 0.0).astype(bf16)
    return jnp.where(data, key, key_side), jnp.where(data, value, value_side)


def slab_offset(n, place, fast):
    if not fast:
        return (n & 7) | ((n >> 3) << 5)
    core = (place >> 1) & 1
    near = 4 - 3 * core if n < 4 else 1 + 3 * core
    return (0, near, 5 - near, 5)[n % 4] ^ (2 * (n // 4))


def slab_row(offset):
    return (offset & 7) | ((offset >> 5) << 3)


def plane_quarter(place):
    return (place & 1) | ((place >> 1) & 2)


def rand_at(fast, rand_ref, block, r):
    if not fast:
        return rand_ref[block * 3 + r]
    return rand_ref[(block // 4) * 2, WIDE // 4 + (block & 3) * 3 + r]


def pack_kernel(rand_ref, query_ref, key_ref, value_ref, output_ref, inner_ref, outer_ref, late_ref, *slice_refs):
    slab = query_ref.shape[0]
    group = ((lax.axis_index("seq") * lax.axis_size("head") + lax.axis_index("head")) >> 3) & 3
    late_ref[:, :D] = output_ref[...]
    late_ref[:, D : D + FF] = inner_ref[...]
    outer = outer_ref[...].astype(f32)
    for c in range(FF // D):
        late_ref[:, D + FF + D * c : D + FF + D * (c + 1)] = outer[slab * c : slab * (c + 1)].astype(bf16)
    spare = (slab, WIDE - SHARE)
    lane = lax.broadcasted_iota(jnp.int32, spare, 1)
    marks = jnp.zeros(spare, f32)
    for n in range(12):
        marks = jnp.where(lane == n, rand_ref[n // 3, n % 3].astype(f32), marks)
    marks = jnp.where(lax.broadcasted_iota(jnp.int32, spare, 0) == 0, marks, 0.0)
    sources = [ref[...].astype(f32) for ref in (query_ref, key_ref, value_ref)]
    for p in range(4):
        pieces = []
        for source in sources:
            mine = source[:, :SHARE]
            for g in range(1, 4):
                mine = jnp.where((group ^ p) == g, source[:, SHARE * g : SHARE * (g + 1)], mine)
            pieces += [mine, marks]
        slice_refs[p][...] = jnp.concatenate(pieces, axis=1).astype(bf16)


def put_tokens(fast, token_refs, tok_ref):
    rows = 2 * BLOCK
    if fast:
        own, far, near = token_refs
        parts = [own[...], near[:rows, :], far[...], near[rows:, :]]
    else:
        parts = [ref[...] for ref in token_refs]
    for a in range(4):
        tok_ref[rows * a : rows * (a + 1), :] = parts[a]


def project_kernel(fast, meta_ref, down_ref, up_ref, *refs):
    count = 3 if fast else 4
    tok_refs, refs = refs[:count], refs[count:]
    w_refs, (w_ref, down_stack_ref, up_stack_ref, q_ref, pair_ref, rand_ref, u_ref, tok_ref, wide_ref) = refs[:-9], refs[-9:]
    place = meta_ref[0]
    group = meta_ref[2]
    chosen = meta_ref[3]
    half = WIDE // 2
    lead = WIDE // 4
    rand_ref[...] = jnp.zeros_like(rand_ref)
    if fast:
        slab = D // 32
        for n, piece in enumerate(w_refs):
            rows = piece[...].astype(f32)
            for a in range(4):
                device = place ^ slab_offset(n, place, fast) ^ PEERS[a]
                wide_ref[pl.ds(pl.multiple_of(device * slab, 8), slab), :] = rows[slab * a : slab * (a + 1)]
                rand_ref[pl.ds(device, 1), :] = rows[slab * a : slab * a + 1, half:WIDE].astype(jnp.int32)
    else:
        wide_ref[...] = w_refs[0][...].astype(f32)
    own = lax.broadcasted_iota(jnp.int32, (D, half), 1) < lead
    above = jnp.zeros((lead, D), f32)
    below = jnp.zeros((half - lead - RANK, D), f32)
    side = jnp.zeros((RANK, WIDE - SHARE), f32)
    downs = []
    ups = []
    for j in range(3):
        low = slice(WIDE * j, WIDE * j + half)
        high = slice(WIDE * j + half, WIDE * (j + 1))
        turned = jnp.concatenate([above, down_ref[chosen, j].astype(f32), below], axis=0).T
        w_ref[:, low] = wide_ref[:, low].astype(bf16)
        w_ref[:, high] = jnp.where(own, wide_ref[:, high], turned).astype(bf16)
        up = up_ref[chosen, j].astype(f32)
        mine = jnp.zeros((RANK, SHARE), f32)
        for g in range(4):
            mine = mine + jnp.where(group == g, up[:, SHARE * g : SHARE * (g + 1)], 0.0)
        mine = jnp.concatenate([mine, side], axis=1)
        u_ref[j] = jnp.concatenate([above[:, :WIDE], mine, below[:, :WIDE]], axis=0).astype(bf16)
        downs.append(down_ref[chosen, j].astype(f32))
        ups.append(jnp.concatenate([mine if n == j else jnp.zeros_like(mine) for n in range(3)], axis=1))
    rest = jnp.zeros((half - 3 * RANK, D), f32)
    down_stack_ref[...] = jnp.concatenate(downs + [rest], axis=0).astype(bf16)
    up_stack_ref[...] = jnp.concatenate(ups + [rest], axis=0).astype(bf16)
    put_tokens(fast, tok_refs, tok_ref)
    q_ref[...], pair_ref[...] = project_rows(dense_mul(tok_ref[...], w_ref[...]), u_ref)


def block_rows(ref, block, count=1):
    return ref[pl.ds(pl.multiple_of(block * BLOCK, BLOCK), count * BLOCK), :]


def merge_heads(stacked):
    lane = lanes(BLOCK)
    total = jnp.zeros((BLOCK, WIDE), f32)
    for head in range(GROUP_HEADS):
        total = jnp.where(head_lanes(lane, head), stacked[BLOCK * head : BLOCK * (head + 1)], total)
    return total


def key_set(ref, picks, block, block_total, fill):
    own = block_rows(ref, block)
    left = block_rows(ref, jnp.maximum(block - 1, 0))
    right = block_rows(ref, jnp.minimum(block + 1, block_total - 1))
    if fill:
        blank = jnp.where(lanes(BLOCK) == MASK_LANE, FLOOR, 0.0).astype(bf16)
        left = jnp.where(block - 1 >= 2, left, blank)
        right = jnp.where(block + 1 < block_total, right, blank)
    rand = [block_rows(ref, pick) for pick in picks]
    return jnp.concatenate([own, left, right, block_rows(ref, 0, 2)] + rand, axis=0)


def own_block(place, t):
    return 2 * (place ^ PEERS[t // 2]) + t % 2


def attend_kernel(fast, meta_ref, rand_ref, q_ref, *refs):
    slab_refs, (k_ref, v_ref, *ctx_refs, aux_ref, s_ref) = refs[:-8], refs[-8:]
    place = meta_ref[0]
    piece = 2 * BLOCK
    for n, slab_ref in enumerate(slab_refs):
        for a in range(4):
            device = place ^ slab_offset(n, place, fast) ^ PEERS[a]
            here = pl.ds(pl.multiple_of(device * piece, piece), piece)
            position = device * piece + lax.broadcasted_iota(jnp.int32, (piece, WIDE), 0)
            k_ref[here, :], v_ref[here, :] = widen_pair(
                slab_ref[piece * a : piece * (a + 1), :], position, meta_ref[1]
            )
    total_rows = k_ref.shape[0]
    block_total = total_rows // BLOCK
    chunks = total_rows // (8 * BLOCK)

    def queries(t):
        rows = q_ref[pl.ds(t * BLOCK, BLOCK), :]
        lane = lanes(BLOCK)
        blank = jnp.zeros_like(rows)
        return jnp.concatenate(
            [
                jnp.where(head_lanes(lane, head) | (lane == MASK_LANE), rows, blank)
                for head in range(GROUP_HEADS)
            ],
            axis=0,
        )

    def finish(t, low, exact, top, total):
        lane = lanes(BLOCK)
        rows = pl.ds(t * BLOCK, BLOCK)
        ctx_refs[t // 2][pl.ds((t % 2) * BLOCK, BLOCK), :] = merge_heads(low).astype(bf16)
        aux = merge_heads(exact)
        lse = top + jnp.log(total)
        for head in range(GROUP_HEADS):
            aux = jnp.where(lane == LSE_LANE + head, lse[BLOCK * head : BLOCK * (head + 1)], aux)
        aux_ref[rows, :] = aux

    def split(probs):
        low = probs.astype(bf16)
        return low, (probs - low.astype(f32)).astype(bf16)

    def sparse(t):
        block = own_block(place, t)
        picks = [rand_at(fast, rand_ref, block, r) for r in range(3)]
        scores = dense_right_t(queries(t), key_set(k_ref, picks, block, block_total, True))
        top = jnp.max(scores, axis=1, keepdims=True)
        weights = jnp.exp(scores - top)
        total = jnp.sum(weights, axis=1, keepdims=True)
        low, rest = split(weights * (1.0 / total))
        values = key_set(v_ref, picks, block, block_total, False)
        context = dense_mul(low, values)
        return context, context + dense_mul(rest, values), top, total

    for a in range(4):

        @pl.when((place ^ PEERS[a]) != 0)
        def _(a=a):
            results = [sparse(2 * a), sparse(2 * a + 1)]
            finish(2 * a, *results[0])
            finish(2 * a + 1, *results[1])

    at_once = s_ref.shape[1] // STACK

    def full(a, first):
        stack = jnp.concatenate([queries(2 * a + first + n) for n in range(at_once)], axis=0)
        height = at_once * STACK

        def score(c, state):
            top, total, tops = state
            part = dense_right_t(stack, block_rows(k_ref, c * 8, 8))
            here = jnp.max(part, axis=1, keepdims=True)
            weights = jnp.exp(part - here)
            s_ref[c] = weights
            later = jnp.maximum(top, here)
            total = total * jnp.exp(top - later) + jnp.sum(weights, axis=1, keepdims=True) * jnp.exp(here - later)
            return later, total, jnp.where(turn == c, here, tops)

        turn = lax.broadcasted_iota(jnp.int32, (height, 128), 1)
        top, total, tops = lax.fori_loop(
            0,
            chunks,
            score,
            (jnp.full((height, 1), FLOOR, f32), jnp.zeros((height, 1), f32), jnp.full((height, 128), FLOOR, f32)),
        )
        scales = jnp.exp(tops - top) * (1.0 / total)

        def mix(c, state):
            scale = jnp.sum(jnp.where(turn == c, scales, 0.0), axis=1, keepdims=True)
            low, rest = split(s_ref[c] * scale)
            values = block_rows(v_ref, c * 8, 8)
            return (state[0] + dense_mul(low, values), state[1] + dense_mul(rest, values))

        zero = jnp.zeros((height, WIDE), f32)
        context, rest = lax.fori_loop(0, chunks, mix, (zero, zero), unroll=4)
        for n in range(at_once):
            here = slice(STACK * n, STACK * (n + 1))
            finish(2 * a + first + n, context[here], (context + rest)[here], top[here], total[here])

    for a in range(4):

        @pl.when((place ^ PEERS[a]) == 0)
        def _(a=a):
            for first in range(0, 2, at_once):
                full(a, first)


DENSE_ROWS = 96


def fold_rows(rows):
    last = rows[DENSE_ROWS:]
    beside = jnp.concatenate([last[:, HDIM * h : HDIM * (h + 1)] for h in range(GROUP_HEADS)], axis=0)
    return jnp.concatenate([rows[:DENSE_ROWS], beside], axis=1)


def unfold_rows(folded):
    beside = folded[:, SHARE:]
    count = DENSE_ROWS // GROUP_HEADS
    last = jnp.concatenate([beside[count * h : count * (h + 1)] for h in range(GROUP_HEADS)], axis=1)
    rows = jnp.concatenate([folded[:, :SHARE], last], axis=0)
    return jnp.concatenate([rows, jnp.zeros((rows.shape[0], WIDE - SHARE), rows.dtype)], axis=1)


def split_parts(value):
    high = value.astype(bf16).astype(f32)
    middle = (value - high).astype(bf16).astype(f32)
    return (high, middle, value - high - middle)


def delta_kernel(*refs):
    grad_refs, aux_ref, out_ref = refs[:4], refs[4], refs[5]
    rows = 2 * BLOCK
    lane = lanes(rows)
    for a in range(4):
        here = pl.ds(a * rows, rows)
        grad = unfold_rows(grad_refs[a][...]).astype(f32)
        aux = aux_ref[here, :]
        result = jnp.where(lane < SHARE, grad, 0.0)
        product = grad * aux
        for head in range(GROUP_HEADS):
            delta = jnp.sum(jnp.where(head_lanes(lane, head), product, 0.0), axis=1, keepdims=True)
            lse = jnp.sum(jnp.where(lane == LSE_LANE + head, aux, 0.0), axis=1, keepdims=True)
            for p, value in enumerate(split_parts(lse)):
                result = jnp.where(lane == LSE_LANE + 3 * head + p, -value, result)
            for p, value in enumerate(split_parts(delta)):
                result = jnp.where(lane == DEL_LANE + 3 * head + p, -value, result)
        out_ref[here, :] = result.astype(bf16)


def query_stacks(rows, grads):
    lane = lanes(BLOCK)
    blank = jnp.zeros_like(rows)
    queries = []
    outers = []
    for head in range(GROUP_HEADS):
        here = head_lanes(lane, head)
        queries.append(
            jnp.where(
                here | (lane == MASK_LANE), rows, jnp.where(part_lanes(lane, LSE_LANE, head), grads, blank)
            )
        )
        outers.append(jnp.where(here | part_lanes(lane, DEL_LANE, head), grads, blank))
    return jnp.concatenate(queries, axis=0), jnp.concatenate(outers, axis=0)


def near_kernel(fast, meta_ref, rand_ref, q_ref, k_ref, v_ref, g_ref, dq_ref, *refs):
    zero_outs, (blank_ref, sems) = refs[:-2], refs[-2:]
    place = meta_ref[0]
    block_total = k_ref.shape[0] // BLOCK
    copies = []
    if zero_outs:
        blank_ref[...] = jnp.zeros_like(blank_ref)
        for n, where in enumerate(zero_outs):
            shape = where.shape
            source = blank_ref if len(shape) == 4 else blank_ref.at[0 : shape[2] // D]
            for adapter in range(ADAPTERS):
                if len(shape) == 4:
                    copies.append((blank_ref, where.at[adapter], n))
                else:
                    for c in range(shape[2] // D):
                        copies.append((blank_ref.at[c], where.at[adapter, :, pl.ds(D * c, D)], n))
        copies = [pltpu.make_async_copy(source, where, sems.at[n]) for n, (source, where, _) in enumerate(copies)]
        for copy in copies:
            copy.start()

    def query_side(stack, outer, keys, values):
        probs = jnp.exp(dense_right_t(stack, keys))
        scored = (probs * dense_right_t(outer, values)).astype(bf16)
        return dense_mul(scored, keys)

    def place_of(a, k):
        return pl.ds(pl.multiple_of((2 * a + k) * BLOCK, BLOCK), BLOCK)

    def put_query(a, k, stacked):
        dq_ref[place_of(a, k), :] = (merge_heads(stacked) * 0.125).astype(bf16)

    def stacks(a, k):
        here = place_of(a, k)
        return query_stacks(q_ref[here, :], g_ref[here, :])

    def sparse(a, k):
        block = 2 * (place ^ (8 * a)) + k
        picks = [rand_at(fast, rand_ref, block, r) for r in range(3)]
        return query_side(
            *stacks(a, k),
            key_set(k_ref, picks, block, block_total, True),
            key_set(v_ref, picks, block, block_total, False),
        )

    def piece(a, carry):
        @pl.when((place ^ (8 * a)) != 0)
        def _():
            results = [sparse(a, 0), sparse(a, 1)]
            put_query(a, 0, results[0])
            put_query(a, 1, results[1])

        @pl.when((place ^ (8 * a)) == 0)
        def _():
            pairs = [stacks(a, 0), stacks(a, 1)]
            stack = jnp.concatenate([pair[0] for pair in pairs], axis=0)
            outer = jnp.concatenate([pair[1] for pair in pairs], axis=0)

            def add(c, total):
                return total + query_side(stack, outer, block_rows(k_ref, c * 16, 16), block_rows(v_ref, c * 16, 16))

            total = lax.fori_loop(0, block_total // 16, add, jnp.zeros((2 * STACK, WIDE), f32), unroll=2)
            put_query(a, 0, total[:STACK])
            put_query(a, 1, total[STACK:])

        return carry

    lax.fori_loop(0, 4, piece, 0)
    for copy in copies:
        copy.wait()


def collect_kernel(fast, block_total, meta_ref, rand_ref, pair_ref):
    place = meta_ref[0]

    def collect(block, count):
        for r in range(3):
            target = rand_at(fast, rand_ref, block, r)
            mine = (((target // 2) ^ place) & ~24) == 0

            @pl.when(mine)
            def _(target=target, count=count):
                pair_ref[count + 1] = target * 65536 + block

            count = count + mine.astype(jnp.int32)
        return count

    pair_ref[0] = lax.fori_loop(2, block_total, collect, jnp.int32(0))


def far_kernel(fast, meta_ref, pair_ref, k_ref, v_ref, dq_ref, w_ref, down_ref, up_ref, early_ref, *refs):
    count = 3 if fast else 4
    tok_refs, refs = refs[:count], refs[count:]
    slab_refs, refs = refs[:-11], refs[-11:]
    part_refs, near_ref, away_ref, refs = refs[:2], refs[2], refs[3], refs[4:]
    q_ref, g_ref, dk_ref, dv_ref, grad_ref, tok_ref, terms_ref = refs
    place = meta_ref[0]
    group = meta_ref[2]
    block_total = k_ref.shape[0] // BLOCK
    count = len(slab_refs) // 2
    rows = 2 * BLOCK
    for n in range(count):
        here = pl.ds(pl.multiple_of(slab_row(slab_offset(n, place, fast)) * 4 * rows, rows), 4 * rows)
        q_ref[here, :] = slab_refs[n][...]
        g_ref[here, :] = slab_refs[count + n][...]

    def stacks(blocks):
        pairs = []
        for block in blocks:
            other = (block // 2) ^ place
            where = slab_row(other) * 8 + ((other >> 3) & 3) * 2 + (block & 1)
            pairs.append(query_stacks(block_rows(q_ref, where), block_rows(g_ref, where)))
        return (
            jnp.concatenate([pair[0] for pair in pairs], axis=0),
            jnp.concatenate([pair[1] for pair in pairs], axis=0),
        )

    def key_side(keys, values, blocks, allowed):
        stack, outer = stacks(blocks)
        probs = jnp.exp(dense_right_t(keys, stack))
        if allowed is not None:
            probs = jnp.where(allowed, probs, 0.0)
        scored = (probs * dense_right_t(values, outer)).astype(bf16)
        return dense_mul(scored, stack), dense_mul(probs.astype(bf16), outer)

    def put(here, grads):
        dk_ref[here, :] += grads[0]
        dv_ref[here, :] += grads[1]

    key_local = lax.broadcasted_iota(jnp.int32, (rows, 6 * STACK), 0) // BLOCK
    turn = lax.broadcasted_iota(jnp.int32, (rows, 6 * STACK), 1) // STACK
    for a in range(4):
        first = 2 * (place ^ PEERS[a])
        here = slice(rows * a, rows * (a + 1))
        blocks = [0, 1, jnp.maximum(first - 1, 0), first, first + 1, jnp.minimum(first + 2, block_total - 1)]
        key_block = first + key_local
        block = first - 3 + turn
        near = (key_block - block <= 1) & (block - key_block <= 1) & (block >= 2) & (block < block_total)
        allowed = ((turn < 2) | near) & (key_block >= 2)
        keys = block_rows(k_ref, first, 2)
        values = block_rows(v_ref, first, 2)
        dk_ref[here, :], dv_ref[here, :] = key_side(keys, values, blocks, allowed)

    pair_total = pair_ref[0]

    def random_pairs(step, carry):
        grads = []
        for k in range(4):
            number = 4 * step + k
            live = number < pair_total
            code = pair_ref[jnp.minimum(number, pair_total - 1) + 1]
            target = code // 65536
            block = code - target * 65536
            start = ((((target // 2) ^ place) >> 3) & 3) * rows + (target & 1) * BLOCK
            grads.append(
                (
                    pl.ds(pl.multiple_of(start, BLOCK), BLOCK),
                    key_side(block_rows(k_ref, target), block_rows(v_ref, target), (block,), live),
                )
            )
        for here, parts in grads:
            put(here, parts)
        return carry

    lax.fori_loop(0, (pair_total + 3) // 4, random_pairs, 0)

    @pl.when((place & ~24) == 0)
    def _():
        here = pl.ds(pl.multiple_of(group * rows, rows), rows)
        keys = block_rows(k_ref, 0, 2)
        values = block_rows(v_ref, 0, 2)

        def every(step, carry):
            put(here, key_side(keys, values, [8 * step + k for k in range(8)], None))
            return carry

        lax.fori_loop(0, block_total // 8, every, 0, unroll=2)

    data = lanes(rows) < SHARE
    for a in range(4):
        here = slice(rows * a, rows * (a + 1))
        grad_ref[here, :WIDE] = dq_ref[here, :]
        grad_ref[here, WIDE : 2 * WIDE] = jnp.where(data, dk_ref[here, :], 0.0).astype(bf16)
        grad_ref[here, 2 * WIDE :] = jnp.where(data, dv_ref[here, :], 0.0).astype(bf16)
    put_tokens(fast, tok_refs, tok_ref)
    tokens = tok_ref[...]
    grad = grad_ref[...]
    reduced = dense_right_t(tokens, down_ref[...]).astype(bf16)
    grad_reduced = dense_right_t(grad, up_ref[...]).astype(bf16)
    down_terms = dense_left_t(grad_reduced, tokens)
    up_terms = dense_left_t(reduced, grad)
    terms = [down_terms[RANK * j : RANK * (j + 1)] for j in range(3)]
    ups = []
    for j in range(3):
        up = up_terms[RANK * j : RANK * (j + 1), WIDE * j : WIDE * j + SHARE]
        ups.append(jnp.concatenate([jnp.where(group == g, up, 0.0) for g in range(4)], axis=1))
    terms += ups + [jnp.zeros((RANK, D), f32)] * 2
    core = (place >> 1) & 1
    quarter = plane_quarter(place)
    for part, value in enumerate(terms):
        early = early_ref[EARLY_PART * part : EARLY_PART * (part + 1), :]
        where = (((part // 4) ^ core) * 4 + ((part % 4) ^ quarter)) if fast else part
        terms_ref[where, :RANK] = value
        terms_ref[where, RANK:] = early
    near_ref[...] = terms_ref[:4]
    away_ref[...] = terms_ref[4:].astype(away_ref.dtype)
    for n, a in enumerate((0, 2, 1, 3)):
        here = slice(rows * a, rows * (a + 1))
        part = (dense_right_t(grad[here], w_ref[...]) + dense_mul(grad_reduced[here], down_ref[...])).astype(bf16)
        part_refs[n // 2][rows * (n % 2) : rows * (n % 2 + 1), :] = part


def normal(hidden):
    center = hidden - jnp.mean(hidden, axis=-1, keepdims=True)
    root = lax.rsqrt(jnp.mean(center * center, axis=-1, keepdims=True) + norm_eps)
    return center * root, root


def normal_back(grad, normed, root):
    mean = jnp.mean(grad, axis=-1, keepdims=True)
    return root * (grad - mean - normed * jnp.mean(grad * normed, axis=-1, keepdims=True))


def select_kernel(meta_ref, *refs):
    chosen = meta_ref[3]
    tables, (down_ref, up_ref, *rest) = refs[:6], refs[6:]
    down_ref[...] = tables[0][chosen, 3]
    up_ref[...] = tables[1][chosen, 3]
    for table, ref in zip(tables[2:], rest, strict=True):
        ref[...] = table[chosen]


def middle_kernel(
    fast,
    meta_ref,
    ctx_refs,
    tok_ref,
    cot_ref,
    late_hbm,
    gain_ref,
    down_ref,
    up_ref,
    inner_down_ref,
    inner_up_ref,
    outer_down_ref,
    outer_up_ref,
    wide_ref,
    out_ref,
    grad_ref,
    piece_refs,
    terms_ref,
    hold_ref,
    pre_ref,
    act_ref,
    late_ref,
    sems,
):
    group = meta_ref[2]
    rows = tok_ref.shape[0]
    share = D // (FF // D)
    places = [(slice(None), slice(D * c, D * (c + 1))) for c in range(1 + FF // D)]
    if fast:
        places += [(slice(share * c, share * (c + 1)), slice(D + FF, D + 2 * FF)) for c in range(FF // D)]
    copies = [
        pltpu.make_async_copy(late_hbm.at[place], late_ref.at[place], sems.at[n]) for n, place in enumerate(places)
    ]
    order = [0] + [n for c in range(FF // D) for n in (1 + c, 1 + FF // D + c) if n < len(copies)]
    for n in order:
        copies[n].start()

    def build(c):
        copies[1 + FF // D + c].wait()
        slab = 24
        for pair in range(share // (2 * slab)):
            first = share * c + 2 * slab * pair
            block = late_ref[first : first + 2 * slab, D + FF :].astype(f32)
            cut = [
                block[slab * side : slab * (side + 1), D * n : D * (n + 1)]
                for side in range(2)
                for n in range(FF // D)
            ]
            wide_ref[4 * first : 4 * first + 8 * slab, :] = jnp.concatenate(cut, axis=0).astype(bf16)

    for a in range(4):
        hold_ref[a] = ctx_refs[a][...]
    context = jnp.concatenate([hold_ref[group ^ g][:, :SHARE] for g in range(4)], axis=1)
    context_red = dense_right_t(context, down_ref[...]).astype(bf16)
    copies[0].wait()
    attended = dense_mul(context, late_ref[:, :D]) + dense_mul(context_red, up_ref[...])
    first, first_root = normal(tok_ref[...].astype(f32) + attended)
    first_norm = first * gain_ref[0:1, :] + gain_ref[1:2, :]
    first_low = first_norm.astype(bf16)
    inner_red = dense_right_t(first_low, inner_down_ref[...]).astype(bf16)
    outer_red = jnp.zeros((rows, RANK), f32)
    outer_out = jnp.zeros((rows, D), f32)
    for c in range(FF // D):
        here = slice(D * c, D * (c + 1))
        copies[1 + c].wait()
        if fast:
            build(c)
        pre = dense_mul(first_low, late_ref[:, D * (c + 1) : D * (c + 2)]) + dense_mul(
            inner_red, inner_up_ref[:, here]
        )
        pre_ref[:, here] = pre
        active = (0.5 * pre * (1.0 + lax.erf(pre * 0.7071067811865476))).astype(bf16)
        act_ref[:, here] = active
        outer_red = outer_red + dense_right_t(active, outer_down_ref[:, here])
        outer_out = outer_out + dense_mul(active, wide_ref[here, :])
    outer_red = outer_red.astype(bf16)
    outer_out = outer_out + dense_mul(outer_red, outer_up_ref[...])
    second, second_root = normal(first_norm + outer_out)
    position = meta_ref[0] * rows + lax.broadcasted_iota(jnp.int32, (rows, D), 0)
    valid = (position < meta_ref[1]).astype(f32)
    out_ref[...] = ((second * gain_ref[2:3, :] + gain_ref[3:4, :]) * valid).astype(bf16)
    grad_second = normal_back(valid * cot_ref[...].astype(f32) * gain_ref[2:3, :], second, second_root)
    grad_outer = grad_second.astype(bf16)
    first_up = RANK * 3
    first_down = RANK * (3 + FF // D)
    terms_ref[first_down + RANK * (FF // D) :, :] = dense_left_t(outer_red, grad_outer)
    outer_grad_red = dense_right_t(grad_outer, outer_up_ref[...]).astype(bf16)
    inner_grad_red = jnp.zeros((rows, RANK), f32)
    grad_first = grad_second
    for c in range(FF // D):
        here = slice(D * c, D * (c + 1))
        grad_active = dense_right_t(grad_outer, wide_ref[here, :]) + dense_mul(
            outer_grad_red, outer_down_ref[:, here]
        )
        pre = pre_ref[:, here]
        slope = 0.5 * (1.0 + lax.erf(pre * 0.7071067811865476)) + pre * (
            0.3989422804014327 * jnp.exp(-0.5 * pre * pre)
        )
        grad_inner = (slope * grad_active).astype(bf16)
        terms_ref[first_up + RANK * c : first_up + RANK * (c + 1), :] = dense_left_t(inner_red, grad_inner)
        terms_ref[first_down + RANK * c : first_down + RANK * (c + 1), :] = dense_left_t(
            outer_grad_red, act_ref[:, here]
        )
        inner_grad_red = inner_grad_red + dense_right_t(grad_inner, inner_up_ref[:, here])
        grad_first = grad_first + dense_right_t(grad_inner, late_ref[:, D * (c + 1) : D * (c + 2)])
    inner_grad_red = inner_grad_red.astype(bf16)
    terms_ref[2 * RANK : 3 * RANK, :] = dense_left_t(inner_grad_red, first_low)
    grad_first = grad_first + dense_mul(inner_grad_red, inner_down_ref[...])
    grad_attended = normal_back(grad_first * gain_ref[0:1, :], first, first_root)
    grad_ref[...] = grad_attended
    grad_low = grad_attended.astype(bf16)
    context_grad_red = dense_right_t(grad_low, up_ref[...]).astype(bf16)
    terms_ref[:RANK, :] = dense_left_t(context_grad_red, context)
    terms_ref[RANK : 2 * RANK, :] = dense_left_t(context_red, grad_low)
    grad_context = (
        dense_right_t(grad_low, late_ref[:, :D]) + dense_mul(context_grad_red, down_ref[...])
    ).astype(bf16)
    for g in range(4):
        hold_ref[group ^ g, :DENSE_ROWS, :] = fold_rows(grad_context[:, SHARE * g : SHARE * (g + 1)])
    for a in range(4):
        piece_refs[a][...] = hold_ref[a, :DENSE_ROWS, :]


def spread_kernel(meta_ref, *refs):
    part_refs = refs[:8]
    outs = refs[14:20]
    sum_ref, sems = refs[20:]
    quarter = plane_quarter(meta_ref[0])
    core = (meta_ref[0] >> 1) & 1
    chosen = meta_ref[3]
    for n in range(8):
        part = (core ^ (n // 4)) * 4 + (quarter ^ (n % 4))
        sum_ref[pl.ds(pl.multiple_of(part * RANK, RANK), RANK), :] = part_refs[n][:RANK, :].astype(f32)
        sum_ref[pl.ds(pl.multiple_of(LATE_ROWS + part * EARLY_PART, 8), EARLY_PART), :] = part_refs[n][RANK:, :].astype(f32)
    places = [outs[0].at[chosen, j] for j in range(3)] + [outs[1].at[chosen, j] for j in range(3)]
    places += [None, None, outs[0].at[chosen, 3], outs[1].at[chosen, 3], outs[2].at[chosen]]
    places += [outs[n].at[chosen, :, pl.ds(D * c, D)] for n in (3, 4) for c in range(FF // D)]
    places.append(outs[5].at[chosen])
    copies = [
        pltpu.make_async_copy(sum_ref.at[pl.ds(RANK * n, RANK), :], where, sems.at[n])
        for n, where in enumerate(places)
        if where is not None
    ]
    for copy in copies:
        copy.start()
    for copy in copies:
        copy.wait()


LATE_ROWS = 8 * RANK
EARLY_KINDS = 12
EARLY_PART = EARLY_KINDS * RANK // 8
ANY = pl.BlockSpec(memory_space=pl.ANY)
SMEM = pl.BlockSpec(memory_space=pltpu.SMEM)
VMEM = pl.BlockSpec(memory_space=pltpu.VMEM)


def shards(
    tokens,
    cotangent,
    w_query,
    w_key,
    w_value,
    w_output,
    w_inner,
    w_outer,
    gain_first,
    shift_first,
    gain_second,
    shift_second,
    attn_down,
    attn_up,
    inner_down,
    inner_up,
    outer_down,
    outer_up,
    lengths,
    rand_blocks,
    adapter_pick,
):
    device_total = lax.axis_size("seq") * lax.axis_size("head")
    local_rows = tokens.shape[0]
    seq_total = lengths.shape[0]
    members = device_total // seq_total
    rows_total = members * local_rows
    block_total = rows_total // BLOCK
    chunk = 4 * local_rows
    index = lax.axis_index("seq") * lax.axis_size("head") + lax.axis_index("head")
    place = index % members
    seq_number = index // members
    group = (place >> 3) & 3
    seq_length = lengths[seq_number]
    chosen = adapter_pick[seq_number]
    fast = device_total == 32 and members == 32
    together = lax.optimization_barrier

    def send(value, even, odd):
        return lax.ppermute(
            value, AXES, [(j, j ^ (odd if (j >> 1) & 1 else even)) for j in range(device_total)]
        )

    def swap(value, mask):
        return send(value, mask, mask)

    def one(value):
        return send(value, 4, 1)

    def two(value):
        return send(value, 1, 4)

    def exchange(pieces, masks=PEERS):
        return [pieces[0]] + [swap(pieces[a], masks[a]) for a in range(1, 4)]

    def gather_start(value):
        if not fast:
            masks = [slab_offset(n, place, False) for n in range(members // 4)]
            return [value] + [swap(value, mask) for mask in masks[1:]]
        return [value, one(value), two(value)]

    def gather_end(slabs):
        if not fast:
            return slabs
        slabs = slabs + [two(slabs[1])]
        return slabs + [swap(slab, 2) for slab in slabs]

    def gather_direct(value):
        return gather_start(value) + ([swap(value, 5)] if fast else [])

    def gather_hand(slabs):
        return slabs + [swap(slab, 2) for slab in slabs] if fast else slabs

    def gather_all(value):
        return lax.all_gather(value, AXES, axis=0, tiled=True)

    def share_columns(table, which=group):
        return lax.dynamic_slice_in_dim(table, which * SHARE, SHARE, table.ndim - 1)

    slab = D // device_total
    meta = jnp.stack([place, seq_length, group, chosen]).astype(jnp.int32)
    if fast:
        late_local, *slices = pl.pallas_call(
            pack_kernel,
            in_specs=[SMEM] + [VMEM] * 6,
            out_specs=[VMEM] * 5,
            out_shape=[jax.ShapeDtypeStruct((slab, D + 2 * FF), bf16)]
            + [jax.ShapeDtypeStruct((slab, 3 * WIDE), bf16)] * 4,
            name="pack",
        )(rand_blocks, w_query, w_key, w_value, w_output, w_inner, w_outer)
        late = gather_all(late_local)
        mine = exchange(slices)
        far_tokens = swap(tokens, PEERS[2])
        near_tokens = swap(jnp.concatenate([tokens, far_tokens], axis=0), PEERS[1])
        token_refs = [tokens, far_tokens, near_tokens]
        w_slabs = gather_hand(gather_direct(jnp.concatenate(mine, axis=0)))
    else:
        late = gather_all(
            jnp.concatenate([w_output, w_inner] + [w_outer[slab * c : slab * (c + 1)] for c in range(FF // D)], axis=1)
        )
        full_qkv = gather_all(jnp.concatenate([w_query, w_key, w_value], axis=1))
        rand_all = lax.all_gather(rand_blocks, "seq", axis=0, tiled=True)
        rand_flat = lax.dynamic_slice_in_dim(rand_all, seq_number * block_total, block_total, 0).reshape(-1)
        token_refs = exchange([tokens] * 4)
        w_slabs = [
            jnp.concatenate(
                [
                    jnp.pad(share_columns(full_qkv[:, D * j : D * (j + 1)]), ((0, 0), (0, WIDE - SHARE)))
                    for j in range(3)
                ],
                axis=1,
            )
        ]

    wide_rows = jax.ShapeDtypeStruct((rows_total, WIDE), bf16)
    piece_shapes = [jax.ShapeDtypeStruct((local_rows, WIDE), bf16)] * 4
    side_weight, down_stack, up_stack, query_own, pair_own, rand_table = pl.pallas_call(
        functools.partial(project_kernel, fast),
        in_specs=[SMEM] + [VMEM] * (2 + len(token_refs) + len(w_slabs)),
        out_specs=[VMEM] * 6,
        out_shape=[
            jax.ShapeDtypeStruct((D, 3 * WIDE), bf16),
            jax.ShapeDtypeStruct((WIDE // 2, D), bf16),
            jax.ShapeDtypeStruct((WIDE // 2, 3 * WIDE), bf16),
            jax.ShapeDtypeStruct((chunk, WIDE), bf16),
            jax.ShapeDtypeStruct((chunk, 2 * SHARE), bf16),
            jax.ShapeDtypeStruct((32, WIDE // 2), jnp.int32),
        ],
        scratch_shapes=[
            pltpu.VMEM((3, WIDE // 2, WIDE), bf16),
            pltpu.VMEM((chunk, D), bf16),
            pltpu.VMEM((D, 3 * WIDE), f32),
        ],
        compiler_params=pltpu.CompilerParams(vmem_limit_bytes=VMEM_LIMIT),
        name="project",
    )(meta, attn_down, attn_up, *token_refs, *w_slabs)
    if fast:
        rand_flat = rand_table
    pair_list = pl.pallas_call(
        functools.partial(collect_kernel, fast, block_total),
        in_specs=[SMEM, SMEM],
        out_specs=SMEM,
        out_shape=jax.ShapeDtypeStruct((3 * block_total + 8,), jnp.int32),
        name="collect",
    )(meta, rand_flat)
    pair_slabs = gather_start(pair_own)
    pair_list, pair_slabs[1] = together((pair_list, pair_slabs[1]))
    pair_slabs = gather_end(pair_slabs)
    key_all, value_all, *ctx, aux = pl.pallas_call(
        functools.partial(attend_kernel, fast),
        in_specs=[SMEM, SMEM] + [VMEM] * (1 + len(pair_slabs)),
        out_specs=[VMEM] * 7,
        out_shape=[wide_rows] * 2 + piece_shapes + [jax.ShapeDtypeStruct((chunk, WIDE), f32)],
        scratch_shapes=[pltpu.VMEM((rows_total // chunk, (2 if fast else 1) * STACK, chunk), f32)],
        compiler_params=pltpu.CompilerParams(vmem_limit_bytes=VMEM_LIMIT),
        name="attend",
    )(meta, rand_flat, query_own, *pair_slabs)
    *tables, ctx[1] = together((attn_down, attn_up, inner_down, inner_up, outer_down, outer_up, ctx[1]))
    ctx_pieces = exchange(ctx)

    gains = jnp.stack([gain_first, shift_first, gain_second, shift_second])
    chosen_maps = pl.pallas_call(
        select_kernel,
        in_specs=[SMEM] + [VMEM] * 6,
        out_specs=[VMEM] * 6,
        out_shape=[jax.ShapeDtypeStruct((RANK, width), bf16) for width in (D, D, D, FF, FF, D)],
        name="select",
    )(meta, *tables)
    *chosen_maps, late = together((*chosen_maps, late))
    middle_in = [tokens, cotangent, late, gains, *chosen_maps]
    wide_shape = [pltpu.VMEM((FF, D), bf16)]
    if not fast:
        middle_in.append(
            late[:, D + FF :].reshape(device_total, slab, FF // D, D).transpose(0, 2, 1, 3).reshape(FF, D)
        )
        wide_shape = []
    count = len(middle_in)

    def middle(meta_ref, *refs):
        ins, outs, scratch = refs[4 : 4 + count], refs[4 + count : 11 + count], refs[11 + count :]
        wide_ref = scratch[-1] if fast else ins[-1]
        middle_kernel(
            fast, meta_ref, refs[:4], *ins[:10], wide_ref, *outs[:2], outs[2:6], outs[6], *scratch[:5]
        )


    output, grad_attended, *grad_pieces, early_terms = pl.pallas_call(
        middle,
        in_specs=[SMEM] + [VMEM] * 6 + [ANY] + [VMEM] * (count - 3),
        out_specs=[VMEM] * 7,
        out_shape=[
            jax.ShapeDtypeStruct((local_rows, D), bf16),
            jax.ShapeDtypeStruct((local_rows, D), f32),
        ]
        + [jax.ShapeDtypeStruct((DENSE_ROWS, WIDE), bf16)] * 4
        + [jax.ShapeDtypeStruct((EARLY_KINDS * RANK, D), f32)],
        scratch_shapes=[
            pltpu.VMEM((4, local_rows, WIDE), bf16),
            pltpu.VMEM((local_rows, FF), f32),
            pltpu.VMEM((local_rows, FF), bf16),
            pltpu.VMEM(late.shape, bf16),
            pltpu.SemaphoreType.DMA((1 + 2 * (FF // D),)),
        ]
        + wide_shape,
        compiler_params=pltpu.CompilerParams(vmem_limit_bytes=VMEM_LIMIT),
        name="middle",
    )(meta, *ctx_pieces, *middle_in)
    query_send, grad_pieces[0] = together((query_own, grad_pieces[0]))
    query_slabs = gather_hand(gather_direct(query_send))
    grad_wide = pl.pallas_call(
        delta_kernel,
        in_specs=[VMEM] * 5,
        out_specs=VMEM,
        out_shape=jax.ShapeDtypeStruct((chunk, WIDE), bf16),
        name="delta",
    )(*exchange(grad_pieces), aux)
    def reduced(terms):
        paired = terms[0] + swap(terms[1], 2)
        moved = exchange([paired[a] for a in range(4)])
        part = (moved[0] + moved[1]) + (moved[2] + moved[3])
        moved = [part] + [swap(part, depth) for depth in DEPTHS[1:]]
        return (moved[0] + moved[1]) + (moved[2] + moved[3])

    grad_slabs = gather_start(grad_wide)
    out_shapes = [
        jax.ShapeDtypeStruct(shape, f32)
        for shape in (
            (ADAPTERS, 4, RANK, D),
            (ADAPTERS, 4, RANK, D),
            (ADAPTERS, RANK, D),
            (ADAPTERS, RANK, FF),
            (ADAPTERS, RANK, FF),
            (ADAPTERS, RANK, D),
        )
    ]
    zero_shapes = out_shapes if fast else []
    query_grad, *zeros = pl.pallas_call(
        functools.partial(near_kernel, fast),
        in_specs=[SMEM, SMEM] + [VMEM] * 4,
        out_specs=[VMEM] + [ANY] * len(zero_shapes),
        out_shape=[jax.ShapeDtypeStruct((chunk, WIDE), bf16)] + zero_shapes,
        scratch_shapes=[pltpu.VMEM((4, RANK, D), f32), pltpu.SemaphoreType.DMA((ADAPTERS * 12,))],
        compiler_params=pltpu.CompilerParams(vmem_limit_bytes=VMEM_LIMIT),
        cost_estimate=pl.CostEstimate(flops=12000000000, bytes_accessed=8000000, transcendentals=1000000),
        name="near",
    )(meta, rand_flat, query_own, key_all, value_all, grad_wide)
    query_grad, *grad_slabs = together((query_grad, *grad_slabs))
    grad_slabs = gather_end(grad_slabs)
    kept, given, near_terms, away_terms = pl.pallas_call(
        functools.partial(far_kernel, fast),
        in_specs=[SMEM, SMEM] + [VMEM] * (7 + len(token_refs) + 2 * len(grad_slabs)),
        out_specs=[VMEM] * 4,
        out_shape=[jax.ShapeDtypeStruct((2 * local_rows, D), bf16)] * 2
        + [jax.ShapeDtypeStruct((4, RANK + EARLY_PART, D), kind) for kind in (f32, bf16 if fast else f32)],
        scratch_shapes=[
            pltpu.VMEM((rows_total, WIDE), bf16),
            pltpu.VMEM((rows_total, WIDE), bf16),
            pltpu.VMEM((chunk, WIDE), f32),
            pltpu.VMEM((chunk, WIDE), f32),
            pltpu.VMEM((chunk, 3 * WIDE), bf16),
            pltpu.VMEM((chunk, D), bf16),
            pltpu.VMEM((8, RANK + EARLY_PART, D), f32),
        ],
        compiler_params=pltpu.CompilerParams(vmem_limit_bytes=VMEM_LIMIT),
        name="far",
    )(
        meta,
        pair_list,
        key_all,
        value_all,
        query_grad,
        side_weight,
        down_stack,
        up_stack,
        early_terms,
        *token_refs,
        *query_slabs,
        *grad_slabs,
    )
    kept = kept.astype(f32) + swap(given, PEERS[1]).astype(f32)
    passed = swap(kept[local_rows:].astype(bf16), PEERS[2])
    grad_tokens = grad_attended + (kept[:local_rows] + passed.astype(f32))

    if fast:
        paired = near_terms + swap(away_terms, 2).astype(f32)
        moved = [paired[0]] + [swap(paired[a].astype(bf16), PLANE[a]).astype(f32) for a in range(1, 4)]
        part = ((moved[0] + moved[1]) + (moved[2] + moved[3])).astype(bf16)
        moved = [piece.astype(f32) for piece in exchange([part] * 4)]
        part = ((moved[0] + moved[1]) + (moved[2] + moved[3])).astype(bf16)
        part_list = exchange([part] * 4, PLANE)
        part_list = part_list + [swap(value, 2) for value in part_list]
        sums = pl.pallas_call(
            spread_kernel,
            in_specs=[SMEM] + [VMEM] * 8 + [ANY] * 6,
            out_specs=[ANY] * 6,
            out_shape=out_shapes,
            scratch_shapes=[
                pltpu.VMEM((LATE_ROWS + EARLY_KINDS * RANK, D), f32),
                pltpu.SemaphoreType.DMA((8 + EARLY_KINDS,)),
            ],
            input_output_aliases={9 + n: n for n in range(6)},
            name="spread",
        )(meta, *part_list, *zeros)
        return (output, grad_tokens, *sums)

    terms = jnp.concatenate([near_terms, away_terms], axis=0)
    terms = jnp.concatenate([terms[:, :RANK].reshape(-1, D), terms[:, RANK:].reshape(-1, D)], axis=0)
    slots = (jnp.arange(seq_total) == seq_number).astype(f32)[:, None, None]
    every = lax.psum(slots * terms[None], AXES)

    def spread(kinds, width):
        def term(s):
            rows = jnp.concatenate([every[s, kind * RANK : (kind + width // D) * RANK] for kind in kinds], axis=0)
            value = rows.reshape(len(kinds), width // D, RANK, D).transpose(0, 2, 1, 3)
            value = value.reshape(len(kinds), RANK, width)
            return (jnp.arange(ADAPTERS) == adapter_pick[s]).astype(f32)[:, None, None, None] * value[None]

        return functools.reduce(lambda x, y: x + y, [term(s) for s in range(seq_total)])

    wide = FF // D
    sums = [
        spread((0, 1, 2, 8), D),
        spread((3, 4, 5, 9), D),
        spread((10,), D),
        spread((11,), FF),
        spread((11 + wide,), FF),
        spread((11 + 2 * wide,), D),
    ]
    return (
        output,
        grad_tokens,
        *[value.reshape(leaf.shape) for value, leaf in zip(sums, out_shapes, strict=True)],
    )


def solution(mesh):
    rows = P(AXES, None)
    placed = (rows,) * 8 + (P(),) * 11 + (P("seq", None), P())
    return jax.shard_map(
        shards,
        mesh=mesh,
        in_specs=placed,
        out_specs=(rows, rows) + (P(),) * 6,
        check_vma=False,
    )
```
